32 devices in a mesh: groups: 1, gx: 32 (over z, y, x, core).
Axes of the slice: x: 2, y: 2, z: 4, core: 2. Of those that a mesh axis runs over, the one named last changes fastest.
Arguments:
- features: bfloat16 [32, 32, 32768], P(None, ('groups', 'gx')), may hold values from -6 to 6
- block_scale: float32 [32, 32], P(None, ('groups', 'gx')), may hold values from 0.25 to 4
- spec_weight: bfloat16 [2, 32, 32, 8192], P(None, None, None, 'gx'), may hold values from -12 to 12
- bypass_weight: bfloat16 [32, 32], replicated, may hold values from -1 to 1
- mlp_in: bfloat16 [128, 32], replicated, may hold values from -1 to 1
- mlp_out: bfloat16 [32, 128], replicated, may hold values from -0.5 to 0.5
- decode_weight: bfloat16 [2, 32], replicated, may hold values from -1 to 1
- zone_ids: int32 [32, 32768], P(('groups', 'gx')), may hold values from 0 to 7
- face_open: int32 [3, 32, 32768], P(None, ('groups', 'gx')), may hold values 0 or 1
- perm_table: float32 [8], replicated, may hold values from 0.05 to 20
Outputs:
- fields: float32 [2, 32, 32768], P(None, ('groups', 'gx'))
- residual: float32 [32, 32768], P(('groups', 'gx'))
The draws below stay inside these ranges and needn't reach their ends.
All inputs are finite; a program needn't handle non-finite values. No bound on the sum of `face_open` on one device may be relied on, other than what follows from the above.
Results may differ from the reference program's by a relative error of at most 0.011.
Values sent between devices are 32-bit elements; how exact they have to be, the bound alone decides.
No kernel may reach another device: no remote copies, remote signals or barrier semaphores. Data moves between devices by JAX's collectives and lax.ppermute only.
A program may use at most 64 MiB of HBM per device.

```python
import math
import jax
import jax.numpy as jnp
from jax import lax

W = 32
HID = 128
NY = 512
NZ = 64
KX = 32
KY = 32
KZ = 8
ZONES = 8
NX = 32
NYZ = 32768
MODES = 8192


def with_ends(values, key, smallest, high):
    index_at = [jax.random.randint(jax.random.fold_in(key, axis), (), 0, length) for axis, length in enumerate(values.shape)]
    widest = values.shape.index(max(values.shape))
    neighbour = index_at[:widest] + [(index_at[widest] + 1) % values.shape[widest]] + index_at[widest + 1:]
    return values.at[tuple(index_at)].set(smallest).at[tuple(neighbour)].set(high)


def steps_of(rng, dims, split, smallest, largest):
    gain, own = 1.0, jax.random.fold_in(rng, 6)
    for axis_at, shards_of in split:
        heights = jnp.exp(jax.random.uniform(jax.random.fold_in(own, axis_at), (shards_of,), jnp.float32, smallest / len(split), largest / len(split)))
        gain = gain * jnp.repeat(heights, dims[axis_at] // shards_of).reshape([-1 if axis == axis_at else 1 for axis in range(len(dims))])
    return gain


def normal_values(key, shape, scale, limit, cuts=(), kind=jnp.bfloat16):
    level = steps_of(key, shape, cuts, -0.22, 0.18) if cuts else 1.0
    array = jax.random.normal(key, shape, jnp.float32) * scale * level
    return jnp.minimum(jnp.maximum(array, -limit), limit).astype(kind)


def setup_inputs(seed: int = 0, part: int = 0) -> dict:
    streams_of = jax.random.split(jax.random.key(seed), 11)
    own_keys = jax.random.split(jax.random.fold_in(streams_of[10], part), 11)
    features = normal_values(own_keys[0], (W, NX, NYZ), 1.0, 6.0, ((1, 32),))
    block_scale = jnp.clip(jnp.exp(math.log(4.0) - 2.7725887 * jax.random.uniform(own_keys[1], (W, NX), jnp.float32) ** steps_of(own_keys[1], (W, NX), ((1, 32),), -0.2, 0.2)), 0.25, 4.0)
    spec_weight = normal_values(streams_of[2], (2, W, W, MODES), 2.0, 12.0, ((3, 32),))
    bypass_weight = normal_values(streams_of[3], (W, W), W ** -0.5, 1.0)
    mlp_in = normal_values(streams_of[4], (HID, W), W ** -0.5, 1.0)
    mlp_out = normal_values(streams_of[5], (W, HID), HID ** -0.5, 0.5)
    decode_weight = normal_values(streams_of[6], (2, W), W ** -0.5, 1.0)
    zone_ids = with_ends(jax.random.randint(own_keys[7], (NX, NYZ), 0, ZONES), jax.random.fold_in(own_keys[7], 1), 0, ZONES - 1).astype(jnp.int32)
    face_open = with_ends((jax.random.randint(own_keys[8], (3, NX, NYZ), 0, 5) < 4).astype(jnp.int32), jax.random.fold_in(own_keys[8], 1), 0, 1)
    perm_table = jnp.clip(jnp.exp(jax.random.uniform(streams_of[9], (ZONES,), jnp.float32, math.log(0.05), math.log(20.0))), 0.05, 20.0)
    return dict(features=features, block_scale=block_scale, spec_weight=spec_weight, bypass_weight=bypass_weight, mlp_in=mlp_in, mlp_out=mlp_out, decode_weight=decode_weight, zone_ids=zone_ids, face_open=face_open, perm_table=perm_table)


def mode_index(count, length):
    half = count // 2
    return jnp.concatenate([jnp.arange(half), jnp.arange(length - half, length)]).astype(jnp.int32)


def lookup(zone_ids, perm_table):
    total = jnp.zeros(zone_ids.shape, jnp.float32)
    for zone in range(ZONES):
        total = total + jnp.where(zone_ids == zone, perm_table[zone], 0.0)
    return total


def face_flux(pressure, mobility, perm, opened, next_pressure, next_mobility, next_perm):
    harmonic = 2.0 * perm * next_perm / (perm + next_perm)
    return opened * harmonic * 0.5 * (mobility + next_mobility) * (pressure - next_pressure)


def ahead(field, axis):
    count = field.shape[axis]
    upper = lax.slice_in_dim(field, 1, count, axis=axis)
    return jnp.concatenate([upper, jnp.zeros_like(lax.slice_in_dim(field, 0, 1, axis=axis))], axis=axis)


def behind(field, axis):
    count = field.shape[axis]
    lower = lax.slice_in_dim(field, 0, count - 1, axis=axis)
    return jnp.concatenate([jnp.zeros_like(lax.slice_in_dim(field, 0, 1, axis=axis)), lower], axis=axis)


def reference(features, block_scale, spec_weight, bypass_weight, mlp_in, mlp_out, decode_weight, zone_ids, face_open, perm_table):
    highest = lax.Precision.HIGHEST
    values = (features.astype(jnp.float32) * block_scale[:, :, None]).astype(jnp.bfloat16)
    grid = values.astype(jnp.float32).reshape(W, NX, NY, NZ)
    index_x = mode_index(KX, NX)
    index_y = mode_index(KY, NY)

    def forward_channel(channel):
        spectrum = jnp.fft.rfftn(channel, axes=(0, 1, 2))
        block = jnp.transpose(spectrum[index_x][:, index_y][:, :, :KZ], (1, 2, 0))
        return jnp.real(block).reshape(-1), jnp.imag(block).reshape(-1)

    modes_real, modes_imag = lax.map(forward_channel, grid)
    mix = spec_weight.astype(jnp.float32)
    out_real = jnp.einsum('im,iom->om', modes_real, mix[0], precision=highest) - jnp.einsum('im,iom->om', modes_imag, mix[1], precision=highest)
    out_imag = jnp.einsum('im,iom->om', modes_real, mix[1], precision=highest) + jnp.einsum('im,iom->om', modes_imag, mix[0], precision=highest)

    def inverse_channel(pair):
        block = jnp.transpose((pair[0] + 1j * pair[1]).reshape(KY, KZ, KX), (2, 0, 1))
        full = jnp.zeros((NX, NY, NZ // 2 + 1), block.dtype)
        full = full.at[index_x[:, None], index_y[None, :], :KZ].set(block)
        return jnp.fft.irfftn(full, s=(NX, NY, NZ), axes=(0, 1, 2)).astype(jnp.float32)

    spectral = lax.map(inverse_channel, (out_real, out_imag)).reshape(W, NX, NY * NZ)

    def plane(pair):
        spec_row, value_row = pair
        pre = spec_row + jnp.dot(bypass_weight, value_row, preferred_element_type=jnp.float32)
        lifted = jax.nn.gelu(pre).astype(jnp.bfloat16)
        hidden = jax.nn.gelu(jnp.dot(mlp_in, lifted, preferred_element_type=jnp.float32)).astype(jnp.bfloat16)
        mixed_out = jnp.dot(mlp_out, hidden, preferred_element_type=jnp.float32).astype(jnp.bfloat16)
        return jnp.dot(decode_weight, mixed_out, preferred_element_type=jnp.float32)

    decoded = lax.map(plane, (jnp.transpose(spectral, (1, 0, 2)), jnp.transpose(values, (1, 0, 2))))
    pressure = decoded[:, 0]
    saturation = jax.nn.sigmoid(decoded[:, 1])
    fields = jnp.stack([pressure, saturation])
    mobility = saturation * saturation / (saturation * saturation + 0.5 * (1.0 - saturation) * (1.0 - saturation))
    perm = lookup(zone_ids, perm_table)
    shape3 = (NX, NY, NZ)
    pressure3 = pressure.reshape(shape3)
    mobility3 = mobility.reshape(shape3)
    perm3 = perm.reshape(shape3)
    opened = face_open.astype(jnp.float32).reshape(3, NX, NY, NZ)
    residual = jnp.zeros(shape3, jnp.float32)
    for axis in range(3):
        flux = face_flux(pressure3, mobility3, perm3, opened[axis], ahead(pressure3, axis), ahead(mobility3, axis), ahead(perm3, axis))
        residual = residual + (flux - behind(flux, axis))
    return fields, residual.reshape(NX, NY * NZ)
```

```python
import functools
import math

import jax
import jax.numpy as jnp
import ml_dtypes
import numpy as np
from jax import lax
from jax.experimental import pallas as pl
from jax.experimental.pallas import tpu as pltpu
from jax.sharding import PartitionSpec as P

NY = 512
NZ = 64
KX = 32
KY = 32
KZ = 8
ZONES = 8
LANES = 128
SUB = 8
PAIRS = LANES // NZ
ROWS = NY // PAIRS
TILES = 4
HALF = KZ * 2 * TILES
GELU_A = math.sqrt(2.0 / math.pi)
GELU_B = GELU_A * 0.044715
F32 = jnp.float32
BF16 = jnp.bfloat16


def signed(count):
    steps = np.arange(count)
    return np.where(steps < count // 2, steps, steps - count)


def angles(freqs, positions, length):
    return 2.0 * np.pi * ((freqs[:, None] * positions[None, :]) % length) / length


def halves(table, axis):
    high = np.asarray(table, np.float64).astype(ml_dtypes.bfloat16)
    low = (table - high.astype(np.float64)).astype(ml_dtypes.bfloat16)
    return np.concatenate([high, low], axis=axis)


def spread(small):
    return np.kron(small, np.eye(SUB))


def z_forward_table():
    angle = angles(np.arange(KZ), np.arange(NZ), NZ)
    table = np.zeros((TILES, PAIRS, NZ, 2, PAIRS, KZ, 2, TILES))
    for t in range(TILES):
        for p in range(PAIRS):
            table[t, p, :, 0, p, :, 0, t] = np.cos(angle).T
            table[t, p, :, 0, p, :, 1, t] = -np.sin(angle).T
            table[t, p, :, 1, p, :, 0, t] = -np.sin(angle).T
            table[t, p, :, 1, p, :, 1, t] = -np.cos(angle).T
    return halves(table.reshape(TILES * LANES, 2 * PAIRS * HALF), 0)


def y_forward_table(rows):
    angle = angles(signed(KY), np.arange(rows) * PAIRS, NY)
    return halves(np.concatenate([spread(np.cos(angle)), spread(np.sin(angle))], axis=0), 1)


def turn_tables(rows):
    parity = np.repeat(angles(signed(KY), np.arange(PAIRS), NY), HALF, axis=1)
    step = np.repeat(angles(signed(KY), np.array([rows * PAIRS]), NY), LANES, axis=1)
    tables = [np.cos(parity), np.sin(parity), np.cos(step), np.sin(step)]
    return np.repeat(np.stack(tables), SUB, axis=1).astype(np.float32)


def x_forward_table(planes):
    angle = angles(signed(KX), np.arange(planes), planes)

    def one(small):
        wide = np.zeros((planes, SUB, SUB, KX))
        for s in range(SUB):
            wide[:, s, s, :] = small.T
        return wide.reshape(planes * SUB, SUB * KX)

    return np.concatenate([one(np.cos(angle)), one(np.sin(angle))], axis=0).astype(np.float32)


def x_back_table(planes):
    return np.ascontiguousarray(x_forward_table(planes).T.reshape(SUB, KX, 2, planes, SUB)
                                .transpose(3, 4, 2, 0, 1).reshape(planes * SUB, 2 * SUB * KX))


def y_back_table(rows):
    angle = angles(signed(KY), np.arange(rows) * PAIRS, NY)
    return halves(np.concatenate([spread(np.cos(angle).T), spread(np.sin(angle).T)], axis=1), 1)


def z_back_table(total):
    angle = angles(np.arange(KZ), np.arange(NZ), NZ)
    weight = np.where(np.arange(KZ) == 0, 1.0, 2.0)[:, None] / total
    table = np.zeros((PAIRS, KZ, 2, TILES, TILES, PAIRS, NZ))
    for t in range(TILES):
        for p in range(PAIRS):
            table[p, :, 0, t, t, p, :] = weight * np.cos(angle)
            table[p, :, 1, t, t, p, :] = -weight * np.sin(angle)
    return halves(table.reshape(PAIRS * HALF, TILES * LANES), 0)


def dot(a, b, dims=((1,), (0,)), precision=None):
    return lax.dot_general(a, b, (dims, ((), ())), precision=precision, preferred_element_type=F32)


def split(x):
    high = x.astype(BF16)
    return high, (x - high.astype(F32)).astype(BF16)


def column(row):
    n = row.shape[1]
    square = lax.broadcasted_iota(jnp.int32, (n, n), 0) == lax.broadcasted_iota(jnp.int32, (n, n), 1)
    return jnp.sum(jnp.where(square, row, 0.0), axis=1, keepdims=True)


def forward_kernel(
    features, scale, zone, opened, perm_table, table_z, table_y, turns, lines, rock, total
):
    step = pl.program_id(0)
    rows = features.shape[1] // LANES

    @pl.when(step == 0)
    def _():
        total[...] = jnp.zeros_like(total)
        zones = zone[...]
        perm = jnp.zeros(zones.shape, F32)
        for k in range(ZONES):
            perm = jnp.where(zones == k, perm_table[k], perm)
        rock[0] = perm
        rock[1] = perm * opened[0].astype(F32)

    values = features[...].astype(F32) * column(scale[...])
    pieces = [
        jnp.concatenate(
            [values[SUB * t : SUB * (t + 1), LANES * j : LANES * (j + 1)] for t in range(TILES)],
            axis=1,
        )
        for j in range(rows)
    ]
    cells = jnp.concatenate(pieces, axis=0).astype(BF16)
    high, low = split(dot(jnp.concatenate([cells, cells], axis=1), table_z[...]))
    table = table_y[...]
    inner = table.shape[1] // 2
    sums = dot(
        jnp.concatenate([table[:, :inner], table], axis=1),
        jnp.concatenate([low, high, high], axis=0),
    )
    n = KY * SUB
    first = sums[:n, :LANES] + sums[n:, LANES:]
    second = sums[:n, LANES:] - sums[n:, :LANES]
    total[0], total[1] = (
        first + turns[2] * total[0] + turns[3] * total[1],
        second + turns[2] * total[1] - turns[3] * total[0],
    )

    @pl.when(step == pl.num_programs(0) - 1)
    def _():
        first, second = total[0], total[1]
        straight = turns[0] * first + turns[1] * second
        turned = turns[0] * second - turns[1] * first
        straight = straight + pltpu.roll(straight, HALF, 1)
        turned = turned + pltpu.roll(turned, HALF, 1)
        lane = lax.broadcasted_iota(jnp.int32, straight.shape, 1)
        lines[...] = jnp.where(lane < HALF, straight, turned)


def swap_blocks(pieces):
    lane = lax.broadcasted_iota(jnp.int32, pieces[0].shape, 1) // KX
    out = []
    for e in range(4):
        got = None
        for b in range(4):
            moved = pieces[b] if b == e else pltpu.roll(pieces[b], (KX * (b - e)) % LANES, 1)
            got = moved if got is None else jnp.where(lane == b, moved, got)
        out.append(got)
    return out


def mix_kernel(
    lines, weight, table_x, table_back, rock, upper, lower, back, links, modes, mixed
):
    links[0] = joined(rock[1], upper[...])
    links[1] = joined(lower[...], rock[0])
    highest = lax.Precision.HIGHEST
    half = lines.shape[1] // 2
    count = half // (2 * TILES)
    groups = count // 4
    flipped = lines[...].T
    pair = jnp.concatenate([flipped[:half], flipped[half:]], axis=1)
    spectrum = dot(pair, table_x[...], precision=highest)
    for c in range(SUB // 4):
        for a in range(groups):
            got = swap_blocks(
                [
                    spectrum[SUB * (4 * a + b) : SUB * (4 * a + b + 1), LANES * c : LANES * (c + 1)]
                    for b in range(4)
                ]
            )
            for e in range(4):
                modes[4 * c + e, :, LANES * a : LANES * (a + 1)] = got[e]
    width = weight.shape[1]
    real = jnp.zeros((width, count * KX), F32)
    imag = jnp.zeros((width, count * KX), F32)
    for i in range(width):
        t, v = i // SUB, i % SUB
        in_real = modes[v, t : t + 1, :]
        in_imag = modes[v, TILES + t : TILES + t + 1, :]
        w_real = weight[0, i].astype(F32)
        w_imag = weight[1, i].astype(F32)
        real += in_real * w_real - in_imag * w_imag
        imag += in_real * w_imag + in_imag * w_real
    for a in range(groups):
        at = slice(LANES * a, LANES * (a + 1))
        mixed[0, a, :width] = real[:, at]
        mixed[0, a, width:] = imag[:, at]
        mixed[1, a, :width] = -imag[:, at]
        mixed[1, a, width:] = real[:, at]
    rows = []
    for k in range(2):
        seen = [
            [mixed[k, a, pl.ds(v, 2 * TILES, stride=SUB), :] for v in range(SUB)]
            for a in range(groups)
        ]
        parts = [[None] * (SUB // 4) for _ in range(count)]
        for c in range(SUB // 4):
            for a in range(groups):
                got = swap_blocks(seen[a][4 * c : 4 * c + 4])
                for b in range(4):
                    parts[4 * a + b][c] = got[b]
        rows.append(jnp.concatenate([jnp.concatenate(p, axis=1) for p in parts], axis=0))
    straight, turned = rows
    sides = jnp.concatenate(
        [
            jnp.concatenate([straight, turned], axis=1),
            jnp.concatenate([turned, -straight], axis=1),
        ],
        axis=0,
    )
    back[...] = dot(table_back[...], sides, ((1,), (1,)), precision=highest)


def gelu_twice(x):
    return x + x * jnp.tanh(x * (GELU_A + GELU_B * (x * x)))


def point_kernel(
    lines,
    features,
    scale,
    bypass,
    mlp_in_t,
    mlp_out,
    decode,
    table_y,
    table_z,
    turns,
    fields,
    state,
    sides,
    smooth,
    latent,
    chunk,
):
    @pl.when(pl.program_id(0) == 0)
    def _():
        held = lines[...]
        other = pltpu.roll(held, HALF, 1)
        lane = lax.broadcasted_iota(jnp.int32, held.shape, 1)
        low = lane < HALF
        n = held.shape[0]
        sides[:n] = jnp.where(low, held, turns[0] * other + turns[1] * held)
        sides[n:] = jnp.where(low, other, turns[0] * held - turns[1] * other)

    rows = features.shape[1] // LANES
    width = features.shape[0]
    high, low = split(sides[...])
    both = dot(
        table_y[...],
        jnp.concatenate(
            [
                jnp.concatenate([high, low], axis=1),
                jnp.concatenate([high, jnp.zeros_like(low)], axis=1),
            ],
            axis=0,
        ),
    )
    high, low = split(both[:, :LANES] + both[:, LANES:])
    table = table_z[...]
    smooth[...] = dot(
        jnp.concatenate([low, high, high], axis=1),
        jnp.concatenate([table[:LANES], table], axis=0),
    )
    n = lines.shape[0]
    straight, turned = sides[:n], sides[n:]
    sides[:n] = turns[2] * straight + turns[3] * turned
    sides[n:] = turns[2] * turned - turns[3] * straight
    factor = column(scale[...])
    for u in range(rows // chunk):
        span = slice(u * chunk * LANES, (u + 1) * chunk * LANES)
        values = (features[:, span].astype(F32) * factor).astype(BF16)
        spectral = jnp.concatenate(
            [
                jnp.concatenate(
                    [
                        smooth[SUB * j : SUB * (j + 1), LANES * t : LANES * (t + 1)]
                        for t in range(TILES)
                    ],
                    axis=0,
                )
                for j in range(u * chunk, (u + 1) * chunk)
            ],
            axis=1,
        )
        pre = spectral + dot(bypass[...], values)
        lifted = (0.5 * gelu_twice(pre)).astype(BF16)
        hidden = (0.5 * gelu_twice(dot(mlp_in_t[...], lifted, ((0,), (0,))))).astype(BF16)
        latent[:, span] = dot(mlp_out[...], hidden).astype(BF16)
    wide = jnp.concatenate([decode[...].astype(F32)] * SUB, axis=1)
    block = lax.broadcasted_iota(jnp.int32, (SUB, SUB * width), 1) // width
    own = block == lax.broadcasted_iota(jnp.int32, (SUB, SUB * width), 0)
    heads = jnp.concatenate(
        [jnp.where(own, wide[0:1], 0.0), jnp.where(own, wide[1:2], 0.0)], axis=0
    ).astype(BF16)
    stacked = jnp.concatenate(
        [
            jnp.concatenate(
                [
                    latent[:, (SUB * a + g) * LANES : (SUB * a + g + 1) * LANES]
                    for a in range(rows // SUB)
                ],
                axis=1,
            )
            for g in range(SUB)
        ],
        axis=0,
    )
    decoded = dot(heads, stacked)
    for a in range(rows // SUB):
        pressure = decoded[:SUB, LANES * a : LANES * (a + 1)]
        saturation = jax.nn.sigmoid(decoded[SUB:, LANES * a : LANES * (a + 1)])
        square = saturation * saturation
        rest = 1.0 - saturation
        at = slice(SUB * a, SUB * (a + 1))
        fields[0, at] = pressure
        fields[1, at] = saturation
        state[0, at] = pressure
        state[1, at] = square / (square + 0.5 * rest * rest)


def joined(first, second):
    both = first + second
    return jnp.where(both > 0.0, first * second / jnp.where(both > 0.0, both, 1.0), 0.0)


def ahead_y(field):
    rolled = pltpu.roll(field, NZ, 1)
    lane = lax.broadcasted_iota(jnp.int32, field.shape, 1)
    row = lax.broadcasted_iota(jnp.int32, field.shape, 0)
    below = pltpu.roll(rolled, field.shape[0] - 1, 0)
    below = jnp.where(row == field.shape[0] - 1, 0.0, below)
    return jnp.where(lane < LANES - NZ, rolled, below)


def behind_y(field):
    rolled = pltpu.roll(field, NZ, 1)
    lane = lax.broadcasted_iota(jnp.int32, field.shape, 1)
    row = lax.broadcasted_iota(jnp.int32, field.shape, 0)
    above = pltpu.roll(rolled, 1, 0)
    above = jnp.where(row == 0, 0.0, above)
    return jnp.where(lane >= NZ, rolled, above)


def ahead_z(field):
    lane = lax.broadcasted_iota(jnp.int32, field.shape, 1)
    return jnp.where(lane % NZ == NZ - 1, 0.0, pltpu.roll(field, LANES - 1, 1))


def behind_z(field):
    lane = lax.broadcasted_iota(jnp.int32, field.shape, 1)
    return jnp.where(lane % NZ == 0, 0.0, pltpu.roll(field, 1, 1))


def inner_kernel(state, rock, opened, partial):
    pressure, mobility, perm = state[0], state[1], rock[0]
    residual = jnp.zeros(pressure.shape, F32)
    for axis, ahead, behind in ((1, ahead_y, behind_y), (2, ahead_z, behind_z)):
        link = opened[axis].astype(F32) * joined(perm, ahead(perm))
        flux = link * (mobility + ahead(mobility)) * (pressure - ahead(pressure))
        residual = residual + (flux - behind(flux))
    partial[...] = residual


def outer_kernel(partial, links, state, after, before, residual):
    pressure, mobility = state[0], state[1]
    upper = links[0] * (mobility + after[1]) * (pressure - after[0])
    lower = links[1] * (before[1] + mobility) * (before[0] - pressure)
    residual[...] = partial[...] + upper - lower


def near(x):
    return pltpu.with_memory_space_constraint(x, pltpu.HBM)


def whole():
    return pl.BlockSpec(memory_space=pltpu.VMEM)


def params():
    return pltpu.CompilerParams(vmem_limit_bytes=40 * 1024 * 1024)


def body(
    features,
    block_scale,
    spec_weight,
    bypass_weight,
    mlp_in,
    mlp_out,
    decode_weight,
    zone_ids,
    face_open,
    perm_table,
):
    width, rows, cells = features.shape
    devices = lax.axis_size("gx")
    planes = rows * devices
    assert rows == 1 and cells == ROWS * LANES and width == TILES * SUB
    plane = features.reshape(width, cells)
    scale = block_scale.reshape(1, width)
    zone = zone_ids.reshape(ROWS, LANES)
    opened = face_open.reshape(3, ROWS, LANES)
    shares = devices // KY
    held = KZ // shares

    steps = 4
    span = cells // steps
    part = span // LANES
    turns = jnp.asarray(turn_tables(part))
    lines, rock = pl.pallas_call(
        forward_kernel,
        grid=(steps,),
        in_specs=[
            pl.BlockSpec((width, span), lambda i: (0, steps - 1 - i)),
            pl.BlockSpec((1, width), lambda i: (0, 0)),
            pl.BlockSpec((ROWS, LANES), lambda i: (0, 0)),
            pl.BlockSpec((1, ROWS, LANES), lambda i: (0, 0, 0)),
            pl.BlockSpec(memory_space=pltpu.SMEM),
            pl.BlockSpec((2 * TILES * LANES, 2 * LANES), lambda i: (0, 0)),
            pl.BlockSpec((2 * KY * SUB, 2 * part * SUB), lambda i: (0, 0)),
            pl.BlockSpec((4, KY * SUB, LANES), lambda i: (0, 0, 0)),
        ],
        out_specs=[
            pl.BlockSpec((KY * SUB, LANES), lambda i: (0, 0)),
            pl.BlockSpec((2, ROWS, LANES), lambda i: (0, 0, 0)),
        ],
        out_shape=[
            jax.ShapeDtypeStruct((KY * SUB, LANES), F32),
            jax.ShapeDtypeStruct((2, ROWS, LANES), F32),
        ],
        scratch_shapes=[pltpu.VMEM((2, KY * SUB, LANES), F32)],
        compiler_params=params(),
        name="forward_yz",
    )(
        near(plane),
        near(scale),
        near(zone),
        near(opened),
        perm_table,
        near(jnp.asarray(z_forward_table())),
        near(jnp.asarray(y_forward_table(part))),
        near(turns),
    )
    up = [(i, i + 1) for i in range(devices - 1)]
    down = [(i + 1, i) for i in range(devices - 1)]
    upper = lax.ppermute(rock[0], "gx", down)
    lower = lax.ppermute(rock[1], "gx", up)

    blocks = lines.reshape(KY, SUB, 2, shares, held * 2 * TILES)
    blocks = blocks.transpose(0, 3, 1, 2, 4).reshape(devices, SUB, 2 * held * 2 * TILES)
    blocks = lax.all_to_all(blocks, "gx", 0, 0, tiled=True)
    lines = blocks.reshape(planes * SUB, 2 * held * 2 * TILES)

    modes = spec_weight.shape[3]
    back, links = pl.pallas_call(
        mix_kernel,
        in_specs=[whole()] * 7,
        out_specs=[whole()] * 2,
        out_shape=[
            jax.ShapeDtypeStruct((planes * SUB, 2 * held * 2 * TILES), F32),
            jax.ShapeDtypeStruct((2, ROWS, LANES), F32),
        ],
        scratch_shapes=[
            pltpu.VMEM((SUB, 2 * TILES, modes), F32),
            pltpu.VMEM((2, modes // LANES, 2 * width, LANES), F32),
        ],
        compiler_params=params(),
        name="mix_modes",
    )(
        lines,
        spec_weight,
        jnp.asarray(x_forward_table(planes)),
        jnp.asarray(x_back_table(planes)),
        rock,
        upper,
        lower,
    )

    blocks = back.reshape(devices, SUB, 2 * held * 2 * TILES)
    blocks = lax.all_to_all(blocks, "gx", 0, 0, tiled=True)
    blocks = blocks.reshape(KY, shares, SUB, 2, held * 2 * TILES).transpose(0, 2, 3, 1, 4)
    lines = blocks.reshape(KY * SUB, 2 * HALF)

    fixed = lambda i: (0, 0)
    fields, state = pl.pallas_call(
        functools.partial(point_kernel, chunk=64),
        grid=(steps,),
        in_specs=[
            pl.BlockSpec((KY * SUB, LANES), fixed),
            pl.BlockSpec((width, span), lambda i: (0, i)),
            pl.BlockSpec((1, width), fixed),
            pl.BlockSpec(bypass_weight.shape, fixed),
            pl.BlockSpec(mlp_in.shape[::-1], fixed),
            pl.BlockSpec(mlp_out.shape, fixed),
            pl.BlockSpec(decode_weight.shape, fixed),
            pl.BlockSpec((part * SUB, 4 * KY * SUB), fixed),
            pl.BlockSpec((2 * LANES, TILES * LANES), fixed),
            pl.BlockSpec((4, KY * SUB, LANES), lambda i: (0, 0, 0)),
        ],
        out_specs=[
            pl.BlockSpec((2, part, LANES), lambda i: (0, i, 0)),
            pl.BlockSpec((2, part, LANES), lambda i: (0, i, 0)),
        ],
        out_shape=[jax.ShapeDtypeStruct((2, ROWS, LANES), F32)] * 2,
        scratch_shapes=[
            pltpu.VMEM((2 * KY * SUB, LANES), F32),
            pltpu.VMEM((part * SUB, TILES * LANES), F32),
            pltpu.VMEM((width, span), BF16),
        ],
        compiler_params=params(),
        name="point_network",
    )(
        lines,
        plane,
        scale,
        bypass_weight,
        mlp_in.T,
        mlp_out,
        decode_weight,
        jnp.asarray(y_back_table(part)),
        jnp.asarray(z_back_table(planes * NY * NZ)),
        turns,
    )
    after = lax.ppermute(state, "gx", down)
    before = lax.ppermute(state, "gx", up)
    partial = pl.pallas_call(
        inner_kernel,
        in_specs=[whole()] * 3,
        out_specs=whole(),
        out_shape=jax.ShapeDtypeStruct((ROWS, LANES), F32),
        compiler_params=params(),
        name="faces_in_plane",
    )(state, rock, opened)
    residual = pl.pallas_call(
        outer_kernel,
        in_specs=[whole()] * 5,
        out_specs=whole(),
        out_shape=jax.ShapeDtypeStruct((ROWS, LANES), F32),
        compiler_params=params(),
        name="faces_between_planes",
    )(partial, links, state, after, before)
    return (fields.reshape(2, 1, cells), residual.reshape(1, cells))


def solution(mesh):
    in_specs = (
        P(None, ("groups", "gx"), None),
        P(None, ("groups", "gx")),
        P(None, None, None, "gx"),
        P(),
        P(),
        P(),
        P(),
        P(("groups", "gx"), None),
        P(None, ("groups", "gx"), None),
        P(),
    )
    out_specs = (P(None, ("groups", "gx"), None), P(("groups", "gx"), None))
    return jax.shard_map(body, mesh=mesh, in_specs=in_specs, out_specs=out_specs, check_vma=False)
```

```python
import math

import jax
import jax.numpy as jnp
import ml_dtypes
import numpy as np
from jax import lax
from jax.experimental import pallas as pl
from jax.experimental.pallas import tpu as pltpu
from jax.sharding import PartitionSpec as P

NY = 512
NZ = 64
KX = 32
KY = 32
KZ = 8
ZONES = 8
LANES = 128
SUB = 8
PAIRS = LANES // NZ
ROWS = NY // PAIRS
TILES = 4
TWO = 2
HALF = KZ * 2 * TILES
FOLD = KY // 2
GELU_A = math.sqrt(2.0 / math.pi)
GELU_B = GELU_A * 0.044715
F32 = jnp.float32
BF16 = jnp.bfloat16


def signed(count):
    steps = np.arange(count)
    return np.where(steps < count // 2, steps, steps - count)


def angles(freqs, positions, length):
    return 2.0 * np.pi * ((freqs[:, None] * positions[None, :]) % length) / length


def halves(table, axis):
    high = np.asarray(table, np.float64).astype(ml_dtypes.bfloat16)
    low = (table - high.astype(np.float64)).astype(ml_dtypes.bfloat16)
    return np.concatenate([high, low], axis=axis)


def spread(small):
    return np.kron(small, np.eye(SUB))


def z_forward_table():
    angle = angles(np.arange(KZ), np.arange(NZ), NZ)
    table = np.zeros((TWO, PAIRS, NZ, 2, KZ, PAIRS, 2, TWO))
    for t in range(TWO):
        for p in range(PAIRS):
            table[t, p, :, 0, :, p, 0, t] = np.cos(angle).T
            table[t, p, :, 0, :, p, 1, t] = -np.sin(angle).T
            table[t, p, :, 1, :, p, 0, t] = -np.sin(angle).T
            table[t, p, :, 1, :, p, 1, t] = -np.cos(angle).T
    return halves(table.reshape(TWO * LANES, LANES), 1)


def y_forward_table(rows):
    angle = angles(np.arange(FOLD + 1), np.arange(rows) * PAIRS, NY)
    return halves(np.concatenate([spread(np.cos(angle)), spread(np.sin(angle[1:]))], axis=0), 1)


def turn_forward_table(rows):
    freqs = np.arange(FOLD + 1)
    parity = angles(freqs, np.arange(PAIRS), NY)
    parity = np.tile(np.repeat(parity, 2 * TWO, axis=1), (1, 2 * KZ))
    step = np.repeat(angles(freqs, np.array([rows * PAIRS]), NY), LANES, axis=1)
    return np.stack([np.cos(parity), np.sin(parity), np.cos(step), np.sin(step)]).astype(np.float32)


def turn_back_table(rows):
    parity = np.repeat(angles(signed(KY), np.array([1]), NY), LANES, axis=1)
    step = np.repeat(angles(np.arange(1, FOLD + 1), np.array([rows * PAIRS]), NY), LANES, axis=1)
    both = np.concatenate([parity, step], axis=0)
    return np.stack([np.cos(both), np.sin(both)]).astype(np.float32)


def x_forward_table(planes):
    angle = angles(signed(KX), np.arange(planes), planes)

    def one(small):
        wide = np.zeros((planes, SUB, SUB, KX))
        for s in range(SUB):
            wide[:, s, s, :] = small.T
        return wide.reshape(planes * SUB, SUB * KX)

    return np.concatenate([one(np.cos(angle)), one(np.sin(angle))], axis=0).astype(np.float32)


def x_back_table(planes):
    table = x_forward_table(planes).reshape(2, planes * SUB, SUB * KX)
    return np.concatenate([table[0], table[1]], axis=1)


def y_back_table(rows):
    angle = angles(np.arange(1, FOLD + 1), np.arange(rows) * PAIRS, NY)
    return halves(np.concatenate([spread(np.cos(angle).T), spread(np.sin(angle).T)], axis=1), 1)


def z_back_table(total):
    angle = angles(np.arange(KZ), np.arange(NZ), NZ)
    weight = np.where(np.arange(KZ) == 0, 1.0, 2.0)[:, None] / total
    table = np.zeros((PAIRS, KZ, TILES // TWO, 2, TWO, TILES, PAIRS, NZ))
    for t in range(TILES):
        for p in range(PAIRS):
            table[p, :, t // TWO, 0, t % TWO, t, p, :] = weight * np.cos(angle)
            table[p, :, t // TWO, 1, t % TWO, t, p, :] = -weight * np.sin(angle)
    return halves(table.reshape(PAIRS * HALF, TILES * LANES), 0)


def dot(a, b, dims=((1,), (0,)), precision=None):
    return lax.dot_general(a, b, (dims, ((), ())), precision=precision, preferred_element_type=F32)


def split(x):
    high = x.astype(BF16)
    return high, (x - high.astype(F32)).astype(BF16)


def column(row):
    n = row.shape[1]
    square = lax.broadcasted_iota(jnp.int32, (n, n), 0) == lax.broadcasted_iota(jnp.int32, (n, n), 1)
    return jnp.sum(jnp.where(square, row, 0.0), axis=1, keepdims=True)


def tall(table, first, count):
    return jnp.concatenate(
        [jnp.broadcast_to(table[k : k + 1], (SUB, LANES)) for k in range(first, first + count)],
        axis=0,
    )


def twice(x):
    return jnp.concatenate([x, x], axis=1)


def forward_kernel(features, scale, table_z, table_y, turns, lines, total):
    step = pl.program_id(0)
    rows = features.shape[1] // LANES

    @pl.when(step == 0)
    def _():
        total[...] = jnp.zeros_like(total)

    values = features[...].astype(F32) * column(scale[...])

    def tile(t, j):
        return values[SUB * t : SUB * (t + 1), LANES * j : LANES * (j + 1)]

    cells = jnp.concatenate(
        [
            jnp.concatenate([tile(t, j), tile(t + 1, j)], axis=1)
            for t in range(0, TILES, TWO)
            for j in range(rows)
        ],
        axis=0,
    ).astype(BF16)
    part = dot(cells, table_z[...])
    part = part[:, :LANES] + part[:, LANES:]
    high, low = split(jnp.concatenate([part[: SUB * rows], part[SUB * rows :]], axis=1))
    table = table_y[...]
    inner = table.shape[1] // 2
    sums = dot(
        jnp.concatenate([table[:, :inner], table], axis=1),
        jnp.concatenate([low, high, high], axis=0),
    )
    n = (FOLD + 1) * SUB
    cosine = twice(tall(turns[2], 0, FOLD + 1))
    sine = twice(tall(turns[3], 0, FOLD + 1))
    first, second = total[0], total[1]
    total[0] = sums[:n] + cosine * first - sine * second
    total[1] = sine * first + cosine * second
    total[1, SUB:] += sums[n:]

    @pl.when(step == pl.num_programs(0) - 1)
    def _():
        cosine = twice(tall(turns[0], 0, FOLD + 1))
        sine = twice(tall(turns[1], 0, FOLD + 1))
        even = cosine * total[0] - sine * total[1]
        odd = sine * total[0] + cosine * total[1]
        lane = lax.broadcasted_iota(jnp.int32, (n, LANES), 1)
        own = lane // (2 * TWO) % 2 == 0

        def packed(sign):
            sides = []
            for k in range(2):
                at = slice(LANES * k, LANES * (k + 1))
                turned = pltpu.roll(odd[:, at], HALF, 1)
                whole_line = even[:, at] + jnp.where(lane < HALF, sign, -sign) * turned
                shift = LANES - 2 * TWO if k == 0 else 2 * TWO
                sides.append(whole_line + pltpu.roll(whole_line, shift, 1))
            return jnp.where(own, sides[0], sides[1])

        up, down = packed(1.0), packed(-1.0)
        lines[: FOLD * SUB] = up[: FOLD * SUB]
        for k in range(FOLD, 0, -1):
            at = (KY - k) * SUB
            lines[at : at + SUB] = down[SUB * k : SUB * (k + 1)]


def swap_blocks(pieces):
    lane = lax.broadcasted_iota(jnp.int32, pieces[0].shape, 1) // KX
    out = []
    for e in range(4):
        got = None
        for b in range(4):
            moved = pieces[b] if b == e else pltpu.roll(pieces[b], (KX * (b - e)) % LANES, 1)
            got = moved if got is None else jnp.where(lane == b, moved, got)
        out.append(got)
    return out


def mix_kernel(lines, weight, table_x, table_back, back, modes, mixed):
    highest = lax.Precision.HIGHEST
    half = lines.shape[1] // 2
    count = half // (2 * TILES)
    groups = count // 4
    flipped = lines[...].T
    pair = jnp.concatenate([flipped[:half], flipped[half:]], axis=1)
    spectrum = dot(pair, table_x[...], precision=highest)
    for c in range(SUB // 4):
        for a in range(groups):
            got = swap_blocks(
                [
                    spectrum[SUB * (4 * a + b) : SUB * (4 * a + b + 1), LANES * c : LANES * (c + 1)]
                    for b in range(4)
                ]
            )
            for e in range(4):
                modes[4 * c + e, :, LANES * a : LANES * (a + 1)] = got[e]
    width = weight.shape[1]
    real = jnp.zeros((width, count * KX), F32)
    imag = jnp.zeros((width, count * KX), F32)
    for i in range(width):
        t, v = i // SUB, i % SUB
        at = t // TWO * 2 * TWO + t % TWO
        in_real = modes[v, at : at + 1, :]
        in_imag = modes[v, at + TWO : at + TWO + 1, :]
        w_real = weight[0, i].astype(F32)
        w_imag = weight[1, i].astype(F32)
        real += in_real * w_real - in_imag * w_imag
        imag += in_real * w_imag + in_imag * w_real
    for a in range(groups):
        for t in range(TILES):
            here = slice(SUB * t, SUB * (t + 1)), slice(LANES * a, LANES * (a + 1))
            at = (t // TWO * 2 * TWO + t % TWO) * SUB
            mixed[0, a, at : at + SUB] = real[here]
            mixed[1, a, at : at + SUB] = -imag[here]
            at += TWO * SUB
            mixed[0, a, at : at + SUB] = imag[here]
            mixed[1, a, at : at + SUB] = real[here]
    rows = []
    for k in range(2):
        seen = [
            [mixed[k, a, pl.ds(v, 2 * TILES, stride=SUB), :] for v in range(SUB)]
            for a in range(groups)
        ]
        parts = [[None] * (SUB // 4) for _ in range(count)]
        for c in range(SUB // 4):
            for a in range(groups):
                got = swap_blocks(seen[a][4 * c : 4 * c + 4])
                for b in range(4):
                    parts[4 * a + b][c] = got[b]
        rows.append(jnp.concatenate([jnp.concatenate(p, axis=1) for p in parts], axis=0))
    straight, turned = rows
    sides = jnp.concatenate(
        [
            jnp.concatenate([straight, turned], axis=1),
            jnp.concatenate([turned, -straight], axis=1),
        ],
        axis=0,
    )
    back[...] = dot(table_back[...], sides, ((1,), (1,)), precision=highest)


def gelu_twice(x):
    return x + x * jnp.tanh(x * (GELU_A + GELU_B * (x * x)))


def point_kernel(
    lines,
    features,
    scale,
    bypass,
    mlp_in_t,
    mlp_out,
    decode,
    zone,
    opened,
    perm_table,
    table_y,
    table_z,
    turns,
    fields,
    near_side,
    far_side,
    sides,
    smooth,
):
    n = FOLD * SUB

    @pl.when(pl.program_id(0) == 0)
    def _():
        held = lines[...]
        other = pltpu.roll(held, HALF, 1)
        low = lax.broadcasted_iota(jnp.int32, held.shape, 1) < HALF
        cosine, sine = tall(turns[0], 0, KY), tall(turns[1], 0, KY)
        straight = jnp.where(low, held, cosine * other + sine * held)
        turned = jnp.where(low, other, cosine * held - sine * other)

        def at(x, k):
            return x[SUB * k : SUB * (k + 1)]

        for k in range(1, FOLD):
            here = slice(SUB * (k - 1), SUB * k)
            sides[0, here] = at(straight, k) + at(straight, KY - k)
            sides[1, here] = at(turned, k) - at(turned, KY - k)
        sides[0, n - SUB : n] = at(straight, FOLD)
        sides[1, n - SUB : n] = -at(turned, FOLD)
        sides[0, n:] = at(straight, 0)

    rows = features.shape[1] // LANES
    width = features.shape[0]
    even, odd = sides[0, :n], sides[1, :n]
    high, low = split(jnp.concatenate([even, odd], axis=0))
    both = jnp.concatenate([high, low], axis=1)
    both = dot(table_y[...], jnp.concatenate([both, both], axis=0))
    level = jnp.concatenate([sides[0, n:]] * rows, axis=0)
    high, low = split(both[:, :LANES] + both[:, LANES:] + level)
    table = table_z[...]
    smooth[...] = dot(
        jnp.concatenate([low, high, high], axis=1),
        jnp.concatenate([table[:LANES], table], axis=0),
    )
    cosine, sine = tall(turns[0], KY, FOLD), tall(turns[1], KY, FOLD)
    sides[0, :n] = cosine * even + sine * odd
    sides[1, :n] = cosine * odd - sine * even

    values = (features[...].astype(F32) * column(scale[...])).astype(BF16)
    spectral = jnp.concatenate(
        [
            jnp.concatenate(
                [
                    smooth[SUB * j : SUB * (j + 1), LANES * t : LANES * (t + 1)]
                    for t in range(TILES)
                ],
                axis=0,
            )
            for j in range(rows)
        ],
        axis=1,
    )
    lifted = gelu_twice(spectral + dot(bypass[...], values)).astype(BF16)
    inner = (0.5 * mlp_in_t[...].astype(F32)).astype(BF16)
    hidden = gelu_twice(dot(inner, lifted, ((0,), (0,)))).astype(BF16)

    heads = dot(decode[...], mlp_out[...])
    count = heads.shape[1]
    group = lax.broadcasted_iota(jnp.int32, (SUB, SUB * count), 1) // count
    own = group == lax.broadcasted_iota(jnp.int32, (SUB, SUB * count), 0)
    wide = jnp.concatenate([heads] * SUB, axis=1)
    wide = jnp.concatenate([jnp.where(own, wide[k : k + 1], 0.0) for k in range(2)], axis=0)
    stacked = jnp.concatenate(
        [
            jnp.concatenate(
                [
                    hidden[:, (SUB * a + g) * LANES : (SUB * a + g + 1) * LANES]
                    for a in range(rows // SUB)
                ],
                axis=1,
            )
            for g in range(SUB)
        ],
        axis=0,
    )
    decoded = dot(jnp.concatenate(split(0.5 * wide), axis=0), stacked)
    decoded = decoded[: 2 * SUB] + decoded[2 * SUB :]
    even_plane = lax.axis_index("gx") % 2 == 0
    for a in range(rows // SUB):
        pressure = decoded[:SUB, LANES * a : LANES * (a + 1)]
        saturation = jax.nn.sigmoid(decoded[SUB:, LANES * a : LANES * (a + 1)])
        square = saturation * saturation
        rest = 1.0 - saturation
        at = slice(SUB * a, SUB * (a + 1))
        fields[0, at] = pressure
        fields[1, at] = saturation
        mobility = square / (square + 0.5 * rest * rest)
        perm = lookup(zone[at], perm_table)
        gated = perm * opened[0, at].astype(F32)
        near_side[0, at] = pressure
        near_side[1, at] = mobility
        near_side[2, at] = jnp.where(even_plane, gated, perm)
        far_side[0, at] = pressure
        far_side[1, at] = mobility
        far_side[2, at] = jnp.where(even_plane, perm, gated)


def lookup(zones, perm_table):
    perm = jnp.zeros(zones.shape, F32)
    for k in range(ZONES):
        perm = jnp.where(zones == k, perm_table[k], perm)
    return perm


def joined(first, second):
    both = first + second
    return jnp.where(both > 0.0, first * second / jnp.where(both > 0.0, both, 1.0), 0.0)


def ahead_y(field):
    rolled = pltpu.roll(field, NZ, 1)
    lane = lax.broadcasted_iota(jnp.int32, field.shape, 1)
    row = lax.broadcasted_iota(jnp.int32, field.shape, 0)
    below = pltpu.roll(rolled, field.shape[0] - 1, 0)
    below = jnp.where(row == field.shape[0] - 1, 0.0, below)
    return jnp.where(lane < LANES - NZ, rolled, below)


def behind_y(field):
    rolled = pltpu.roll(field, NZ, 1)
    lane = lax.broadcasted_iota(jnp.int32, field.shape, 1)
    row = lax.broadcasted_iota(jnp.int32, field.shape, 0)
    above = pltpu.roll(rolled, 1, 0)
    above = jnp.where(row == 0, 0.0, above)
    return jnp.where(lane >= NZ, rolled, above)


def ahead_z(field):
    lane = lax.broadcasted_iota(jnp.int32, field.shape, 1)
    return jnp.where(lane % NZ == NZ - 1, 0.0, pltpu.roll(field, LANES - 1, 1))


def behind_z(field):
    lane = lax.broadcasted_iota(jnp.int32, field.shape, 1)
    return jnp.where(lane % NZ == 0, 0.0, pltpu.roll(field, 1, 1))


def inner_kernel(side, zone, opened, perm_table, partial):
    pressure, mobility = side[0], side[1]
    perm = lookup(zone[...], perm_table)
    residual = jnp.zeros(pressure.shape, F32)
    for axis, ahead, behind in ((1, ahead_y, behind_y), (2, ahead_z, behind_z)):
        link = opened[axis].astype(F32) * joined(perm, ahead(perm))
        flux = link * (mobility + ahead(mobility)) * (pressure - ahead(pressure))
        residual = residual + (flux - behind(flux))
    partial[...] = residual


def outer_kernel(partial, near_side, near_other, far_side, far_other, residual):
    total = partial[...]
    for mine, other in ((near_side, near_other), (far_side, far_other)):
        link = joined(mine[2], other[2])
        total = total + link * (mine[1] + other[1]) * (mine[0] - other[0])
    residual[...] = total


def near(x):
    return pltpu.with_memory_space_constraint(x, pltpu.HBM)


def whole():
    return pl.BlockSpec(memory_space=pltpu.VMEM)


def params():
    return pltpu.CompilerParams(vmem_limit_bytes=40 * 1024 * 1024)


def body(
    features,
    block_scale,
    spec_weight,
    bypass_weight,
    mlp_in,
    mlp_out,
    decode_weight,
    zone_ids,
    face_open,
    perm_table,
):
    width, rows, cells = features.shape
    devices = lax.axis_size("gx")
    planes = rows * devices
    assert rows == 1 and cells == ROWS * LANES and width == TILES * SUB and devices % 2 == 0
    plane = features.reshape(width, cells)
    scale = block_scale.reshape(1, width)
    zone = zone_ids.reshape(ROWS, LANES)
    opened = face_open.reshape(3, ROWS, LANES)
    shares = devices // KY
    held = KZ // shares

    fixed = lambda i: (0, 0)
    cubes = lambda i: (0, 0, 0)
    steps = 4
    span = cells // steps
    part = span // LANES
    count = 2 * FOLD + 1
    lines = pl.pallas_call(
        forward_kernel,
        grid=(steps,),
        in_specs=[
            pl.BlockSpec((width, span), lambda i: (0, steps - 1 - i)),
            pl.BlockSpec((1, width), fixed),
            pl.BlockSpec((TWO * LANES, 2 * LANES), fixed),
            pl.BlockSpec((count * SUB, 2 * part * SUB), fixed),
            pl.BlockSpec((4, FOLD + 1, LANES), cubes),
        ],
        out_specs=pl.BlockSpec((KY * SUB, LANES), fixed),
        out_shape=jax.ShapeDtypeStruct((KY * SUB, LANES), F32),
        scratch_shapes=[pltpu.VMEM((2, (FOLD + 1) * SUB, 2 * LANES), F32)],
        compiler_params=params(),
        name="forward_yz",
    )(
        near(plane),
        near(scale),
        near(jnp.asarray(z_forward_table())),
        near(jnp.asarray(y_forward_table(part))),
        near(jnp.asarray(turn_forward_table(part))),
    )

    blocks = lines.reshape(KY, SUB, 2, shares, held * 2 * TILES)
    blocks = blocks.transpose(0, 3, 1, 2, 4).reshape(devices, SUB, 2 * held * 2 * TILES)
    blocks = lax.all_to_all(blocks, "gx", 0, 0, tiled=True)
    lines = blocks.reshape(planes * SUB, 2 * held * 2 * TILES)

    modes = spec_weight.shape[3]
    back = pl.pallas_call(
        mix_kernel,
        in_specs=[whole()] * 4,
        out_specs=whole(),
        out_shape=jax.ShapeDtypeStruct((planes * SUB, 2 * held * 2 * TILES), F32),
        scratch_shapes=[
            pltpu.VMEM((SUB, 2 * TILES, modes), F32),
            pltpu.VMEM((2, modes // LANES, 2 * width, LANES), F32),
        ],
        compiler_params=params(),
        name="mix_modes",
    )(
        lines,
        spec_weight,
        jnp.asarray(x_forward_table(planes)),
        jnp.asarray(x_back_table(planes)),
    )

    blocks = back.reshape(devices, SUB, 2 * held * 2 * TILES)
    blocks = lax.all_to_all(blocks, "gx", 0, 0, tiled=True)
    blocks = blocks.reshape(KY, shares, SUB, 2, held * 2 * TILES).transpose(0, 2, 3, 1, 4)
    lines = blocks.reshape(KY * SUB, 2 * HALF)

    side = jax.ShapeDtypeStruct((3, ROWS, LANES), F32)
    fields, near_side, far_side = pl.pallas_call(
        point_kernel,
        grid=(steps,),
        in_specs=[
            pl.BlockSpec((KY * SUB, LANES), fixed),
            pl.BlockSpec((width, span), lambda i: (0, i)),
            pl.BlockSpec((1, width), fixed),
            pl.BlockSpec(bypass_weight.shape, fixed),
            pl.BlockSpec(mlp_in.shape[::-1], fixed),
            pl.BlockSpec(mlp_out.shape, fixed),
            pl.BlockSpec(decode_weight.shape, fixed),
            pl.BlockSpec((part, LANES), lambda i: (i, 0)),
            pl.BlockSpec((1, part, LANES), lambda i: (0, i, 0)),
            pl.BlockSpec(memory_space=pltpu.SMEM),
            pl.BlockSpec((part * SUB, 4 * FOLD * SUB), fixed),
            pl.BlockSpec((2 * LANES, TILES * LANES), fixed),
            pl.BlockSpec((2, KY + FOLD, LANES), cubes),
        ],
        out_specs=[
            pl.BlockSpec((2, part, LANES), lambda i: (0, i, 0)),
            pl.BlockSpec((3, part, LANES), lambda i: (0, i, 0)),
            pl.BlockSpec((3, part, LANES), lambda i: (0, i, 0)),
        ],
        out_shape=[jax.ShapeDtypeStruct((2, ROWS, LANES), F32), side, side],
        scratch_shapes=[
            pltpu.VMEM((2, (FOLD + 1) * SUB, LANES), F32),
            pltpu.VMEM((part * SUB, TILES * LANES), F32),
        ],
        compiler_params=params(),
        name="point_network",
    )(
        lines,
        plane,
        scale,
        bypass_weight,
        mlp_in.T,
        mlp_out,
        decode_weight,
        zone,
        opened,
        perm_table,
        jnp.asarray(y_back_table(part)),
        jnp.asarray(z_back_table(planes * NY * NZ)),
        jnp.asarray(turn_back_table(part)),
    )
    pairs = [(i, i + 1) for i in range(1, devices - 1, 2)]
    far_other = lax.ppermute(far_side, "gx", pairs + [(b, a) for a, b in pairs])
    pairs = [(i, i + 1) for i in range(0, devices, 2)]
    near_other = lax.ppermute(near_side, "gx", pairs + [(b, a) for a, b in pairs])
    partial = pl.pallas_call(
        inner_kernel,
        in_specs=[whole()] * 3 + [pl.BlockSpec(memory_space=pltpu.SMEM)],
        out_specs=whole(),
        out_shape=jax.ShapeDtypeStruct((ROWS, LANES), F32),
        compiler_params=params(),
        name="faces_in_plane",
    )(near_side, zone, opened, perm_table)
    residual = pl.pallas_call(
        outer_kernel,
        in_specs=[whole()] * 5,
        out_specs=whole(),
        out_shape=jax.ShapeDtypeStruct((ROWS, LANES), F32),
        compiler_params=params(),
        name="faces_between_planes",
    )(partial, near_side, near_other, far_side, far_other)
    return (fields.reshape(2, 1, cells), residual.reshape(1, cells))


def solution(mesh):
    in_specs = (
        P(None, ("groups", "gx"), None),
        P(None, ("groups", "gx")),
        P(None, None, None, "gx"),
        P(),
        P(),
        P(),
        P(),
        P(("groups", "gx"), None),
        P(None, ("groups", "gx"), None),
        P(),
    )
    out_specs = (P(None, ("groups", "gx"), None), P(("groups", "gx"), None))
    return jax.shard_map(body, mesh=mesh, in_specs=in_specs, out_specs=out_specs, check_vma=False)
```

```python
import functools
import math

import jax
import jax.numpy as jnp
import ml_dtypes
import numpy as np
from jax import lax
from jax.experimental import pallas as pl
from jax.experimental.pallas import tpu as pltpu
from jax.sharding import PartitionSpec as P

NY = 512
NZ = 64
KX = 32
KY = 32
KZ = 8
ZONES = 8
LANES = 128
SUB = 8
PAIRS = LANES // NZ
ROWS = NY // PAIRS
TILES = 4
TWO = 2
HALF = KZ * 2 * TILES
QUARTER = ROWS // 4
FOLD = KY // 2
GELU_A = math.sqrt(2.0 / math.pi)
GELU_B = GELU_A * 0.044715
F32 = jnp.float32
BF16 = jnp.bfloat16


def signed(count):
    steps = np.arange(count)
    return np.where(steps < count // 2, steps, steps - count)


def angles(freqs, positions, length):
    return 2.0 * np.pi * ((freqs[:, None] * positions[None, :]) % length) / length


def halves(table, axis):
    high = np.asarray(table, np.float64).astype(ml_dtypes.bfloat16)
    low = (table - high.astype(np.float64)).astype(ml_dtypes.bfloat16)
    return np.concatenate([high, low], axis=axis)


def spread(small):
    return np.kron(small, np.eye(SUB))


def z_forward_table():
    angle = angles(np.arange(KZ), np.arange(NZ), NZ)
    table = np.zeros((TWO, PAIRS, NZ, 2, KZ, PAIRS, 2, TWO))
    for t in range(TWO):
        for p in range(PAIRS):
            table[t, p, :, 0, :, p, 0, t] = np.cos(angle).T
            table[t, p, :, 0, :, p, 1, t] = -np.sin(angle).T
            table[t, p, :, 1, :, p, 0, t] = -np.sin(angle).T
            table[t, p, :, 1, :, p, 1, t] = -np.cos(angle).T
    return halves(table.reshape(TWO * LANES, LANES), 1)


def y_forward_table():
    angle = angles(np.arange(FOLD + 1), np.arange(QUARTER) * PAIRS, NY)
    return halves(np.concatenate([spread(np.cos(angle)), spread(np.sin(angle[1:]))], axis=0), 1)


def turn_forward_table():
    parity = angles(np.arange(FOLD + 1), np.arange(PAIRS), NY)
    parity = np.tile(np.repeat(parity, 2 * TWO, axis=1), (1, 2 * KZ))
    return np.stack([np.cos(parity), np.sin(parity)]).astype(np.float32)


def turn_back_table():
    parity = np.repeat(angles(signed(KY), np.array([1]), NY), LANES, axis=1)
    return np.stack([np.cos(parity), np.sin(parity)]).astype(np.float32)


def x_forward_table(planes):
    angle = angles(signed(KX), np.arange(planes), planes)

    def one(small):
        wide = np.zeros((planes, SUB, SUB, KX))
        for s in range(SUB):
            wide[:, s, s, :] = small.T
        return wide.reshape(planes * SUB, SUB * KX)

    return np.concatenate([one(np.cos(angle)), one(np.sin(angle))], axis=0).astype(np.float32)


def x_back_table(planes):
    table = x_forward_table(planes).reshape(2, planes * SUB, SUB * KX)
    return np.concatenate([table[0], table[1]], axis=1)


def y_back_table():
    angle = angles(np.arange(1, FOLD + 1), np.arange(QUARTER) * PAIRS, NY)
    return halves(np.concatenate([spread(np.cos(angle).T), spread(np.sin(angle).T)], axis=1), 1)


def z_back_table(total):
    angle = angles(np.arange(KZ), np.arange(NZ), NZ)
    weight = np.where(np.arange(KZ) == 0, 1.0, 2.0)[:, None] / total
    table = np.zeros((PAIRS, KZ, TILES // TWO, 2, TWO, TILES, PAIRS, NZ))
    for t in range(TILES):
        for p in range(PAIRS):
            table[p, :, t // TWO, 0, t % TWO, t, p, :] = weight * np.cos(angle)
            table[p, :, t // TWO, 1, t % TWO, t, p, :] = -weight * np.sin(angle)
    return halves(table.reshape(PAIRS * HALF, TILES * LANES), 0)


def dot(a, b, dims=((1,), (0,)), precision=None):
    return lax.dot_general(a, b, (dims, ((), ())), precision=precision, preferred_element_type=F32)


def split(x):
    high = x.astype(BF16)
    return high, (x - high.astype(F32)).astype(BF16)


def column(row):
    n = row.shape[1]
    square = lax.broadcasted_iota(jnp.int32, (n, n), 0) == lax.broadcasted_iota(jnp.int32, (n, n), 1)
    return jnp.sum(jnp.where(square, row, 0.0), axis=1, keepdims=True)


def tall(table, first, count):
    return jnp.concatenate(
        [jnp.broadcast_to(table[k : k + 1], (SUB, LANES)) for k in range(first, first + count)],
        axis=0,
    )


def twice(x):
    return jnp.concatenate([x, x], axis=1)


def quarters(real, imag, turns):
    return ((real, imag), (-imag, real), (-real, -imag), (imag, -real))[turns % 4]


def forward_kernel(features, scale, table_z, table_y, turns, lines, total):
    step = pl.program_id(0)
    rows = features.shape[1] // LANES

    @pl.when(step == 0)
    def _():
        total[...] = jnp.zeros_like(total)

    values = features[...].astype(F32) * column(scale[...])

    def tile(t, j):
        return values[SUB * t : SUB * (t + 1), LANES * j : LANES * (j + 1)]

    cells = jnp.concatenate(
        [
            jnp.concatenate([tile(t, j), tile(t + 1, j)], axis=1)
            for t in range(0, TILES, TWO)
            for j in range(rows)
        ],
        axis=0,
    ).astype(BF16)
    part = dot(cells, table_z[...])
    part = part[:, :LANES] + part[:, LANES:]
    high, low = split(jnp.concatenate([part[: SUB * rows], part[SUB * rows :]], axis=1))
    table = table_y[...]
    inner = table.shape[1] // 2
    sums = dot(
        jnp.concatenate([table[:, :inner], table], axis=1),
        jnp.concatenate([low, high, high], axis=0),
    )
    n = (FOLD + 1) * SUB
    for k in range(FOLD + 1):
        at = slice(SUB * k, SUB * (k + 1))
        real, imag = quarters(total[0, at], total[1, at], k)
        total[0, at] = real + sums[at]
        total[1, at] = imag + sums[n + SUB * (k - 1) : n + SUB * k] if k else imag

    @pl.when(step == pl.num_programs(0) - 1)
    def _():
        cosine = twice(tall(turns[0], 0, FOLD + 1))
        sine = twice(tall(turns[1], 0, FOLD + 1))
        even = cosine * total[0] - sine * total[1]
        odd = sine * total[0] + cosine * total[1]
        lane = lax.broadcasted_iota(jnp.int32, (n, LANES), 1)
        own = lane // (2 * TWO) % 2 == 0

        def packed(sign):
            sides = []
            for k in range(2):
                at = slice(LANES * k, LANES * (k + 1))
                turned = pltpu.roll(odd[:, at], HALF, 1)
                whole_line = even[:, at] + jnp.where(lane < HALF, sign, -sign) * turned
                shift = LANES - 2 * TWO if k == 0 else 2 * TWO
                sides.append(whole_line + pltpu.roll(whole_line, shift, 1))
            return jnp.where(own, sides[0], sides[1])

        up, down = packed(1.0), packed(-1.0)
        lines[: FOLD * SUB] = up[: FOLD * SUB]
        for k in range(FOLD, 0, -1):
            at = (KY - k) * SUB
            lines[at : at + SUB] = down[SUB * k : SUB * (k + 1)]


def swap_blocks(pieces):
    lane = lax.broadcasted_iota(jnp.int32, pieces[0].shape, 1) // KX
    out = []
    for e in range(4):
        got = None
        for b in range(4):
            moved = pieces[b] if b == e else pltpu.roll(pieces[b], (KX * (b - e)) % LANES, 1)
            got = moved if got is None else jnp.where(lane == b, moved, got)
        out.append(got)
    return out


def mix_kernel(lines, weight, table_x, table_back, back, modes, mixed):
    highest = lax.Precision.HIGHEST
    half = lines.shape[1] // 2
    count = half // (2 * TILES)
    groups = count // 4
    flipped = lines[...].T
    pair = jnp.concatenate([flipped[:half], flipped[half:]], axis=1)
    spectrum = dot(pair, table_x[...], precision=highest)
    for c in range(SUB // 4):
        for a in range(groups):
            got = swap_blocks(
                [
                    spectrum[SUB * (4 * a + b) : SUB * (4 * a + b + 1), LANES * c : LANES * (c + 1)]
                    for b in range(4)
                ]
            )
            for e in range(4):
                modes[4 * c + e, :, LANES * a : LANES * (a + 1)] = got[e]
    width = weight.shape[1]
    real = jnp.zeros((width, count * KX), F32)
    imag = jnp.zeros((width, count * KX), F32)
    for i in range(width):
        t, v = i // SUB, i % SUB
        at = t // TWO * 2 * TWO + t % TWO
        in_real = modes[v, at : at + 1, :]
        in_imag = modes[v, at + TWO : at + TWO + 1, :]
        w_real = weight[0, i].astype(F32)
        w_imag = weight[1, i].astype(F32)
        real += in_real * w_real - in_imag * w_imag
        imag += in_real * w_imag + in_imag * w_real
    for a in range(groups):
        for t in range(TILES):
            here = slice(SUB * t, SUB * (t + 1)), slice(LANES * a, LANES * (a + 1))
            at = (t // TWO * 2 * TWO + t % TWO) * SUB
            mixed[0, a, at : at + SUB] = real[here]
            mixed[1, a, at : at + SUB] = -imag[here]
            at += TWO * SUB
            mixed[0, a, at : at + SUB] = imag[here]
            mixed[1, a, at : at + SUB] = real[here]
    rows = []
    for k in range(2):
        seen = [
            [mixed[k, a, pl.ds(v, 2 * TILES, stride=SUB), :] for v in range(SUB)]
            for a in range(groups)
        ]
        parts = [[None] * (SUB // 4) for _ in range(count)]
        for c in range(SUB // 4):
            for a in range(groups):
                got = swap_blocks(seen[a][4 * c : 4 * c + 4])
                for b in range(4):
                    parts[4 * a + b][c] = got[b]
        rows.append(jnp.concatenate([jnp.concatenate(p, axis=1) for p in parts], axis=0))
    straight, turned = rows
    sides = jnp.concatenate(
        [
            jnp.concatenate([straight, turned], axis=1),
            jnp.concatenate([turned, -straight], axis=1),
        ],
        axis=0,
    )
    back[...] = dot(table_back[...], sides, ((1,), (1,)), precision=highest)


def gelu_twice(x):
    return x + x * jnp.tanh(x * (GELU_A + GELU_B * (x * x)))


def diagonal(block):
    height, width = block.shape
    tall_block = jnp.concatenate([block] * SUB, axis=0)
    rows = lax.broadcasted_iota(jnp.int32, (SUB * height, SUB * width), 0) // height
    columns = lax.broadcasted_iota(jnp.int32, (SUB * height, SUB * width), 1) // width
    return jnp.where(rows == columns, jnp.concatenate([tall_block] * SUB, axis=1), 0.0)


def point_kernel(
    lines,
    features,
    scale,
    bypass,
    mlp_in_t,
    mlp_out,
    decode,
    zone,
    opened,
    perm_table,
    table_y,
    table_z,
    turns,
    *refs,
    first,
):
    fields, near_side, far_side, smooth = refs[-4:]
    rows = features.shape[1] // LANES
    held = lines[...]
    other = pltpu.roll(held, HALF, 1)
    low_half = lax.broadcasted_iota(jnp.int32, held.shape, 1) < HALF
    cosine, sine = tall(turns[0], 0, KY), tall(turns[1], 0, KY)
    straight = jnp.where(low_half, held, cosine * other + sine * held)
    turned = jnp.where(low_half, other, cosine * held - sine * other)

    def at(x, k):
        return x[SUB * k : SUB * (k + 1)]

    even = [at(straight, k) + at(straight, KY - k) for k in range(1, FOLD)]
    odd = [at(turned, k) - at(turned, KY - k) for k in range(1, FOLD)]
    even.append(at(straight, FOLD))
    odd.append(-at(turned, FOLD))
    level = jnp.concatenate([at(straight, 0)] * QUARTER, axis=0)
    table = jnp.concatenate([table_z[:LANES], table_z[...]], axis=0)
    for m in range(rows // QUARTER):
        sides = [
            quarters(real, -imag, (first // QUARTER + m) * k)
            for k, (real, imag) in enumerate(zip(even, odd), 1)
        ]
        sides = [real for real, _ in sides] + [-imag for _, imag in sides]
        sides = jnp.concatenate(split(jnp.concatenate(sides, axis=0)), axis=1)
        both = dot(table_y[...], jnp.concatenate([sides, sides], axis=0))
        high, low = split(both[:, :LANES] + both[:, LANES:] + level)
        smooth[QUARTER * SUB * m : QUARTER * SUB * (m + 1)] = dot(
            jnp.concatenate([low, high, high], axis=1), table
        )

    wide_bypass = diagonal(bypass[...].astype(F32)).astype(BF16)
    wide_in = diagonal(0.5 * mlp_in_t[...].astype(F32).T).astype(BF16)
    heads = 0.5 * dot(decode[...], mlp_out[...])
    heads = jnp.concatenate([diagonal(heads[k : k + 1]) for k in range(2)], axis=0)
    wide_out = jnp.concatenate(split(heads), axis=0)

    groups = rows // SUB

    def grouped(tile):
        return jnp.concatenate(
            [
                jnp.concatenate([tile(SUB * a + g) for a in range(groups)], axis=1)
                for g in range(SUB)
            ],
            axis=0,
        )

    values = features[...].astype(F32) * column(scale[...])
    values = grouped(lambda j: values[:, LANES * j : LANES * (j + 1)]).astype(BF16)
    spectral = grouped(
        lambda j: jnp.concatenate(
            [
                smooth[SUB * j : SUB * (j + 1), LANES * t : LANES * (t + 1)]
                for t in range(TILES)
            ],
            axis=0,
        )
    )
    lifted = gelu_twice(spectral + dot(wide_bypass, values)).astype(BF16)
    hidden = gelu_twice(dot(wide_in, lifted)).astype(BF16)
    decoded = dot(wide_out, hidden)
    decoded = decoded[: 2 * SUB] + decoded[2 * SUB :]
    even_plane = lax.axis_index("gx") % 2 == 0
    for a in range(rows // SUB):
        pressure = decoded[:SUB, LANES * a : LANES * (a + 1)]
        saturation = jax.nn.sigmoid(decoded[SUB:, LANES * a : LANES * (a + 1)])
        square = saturation * saturation
        rest = 1.0 - saturation
        at = slice(SUB * a, SUB * (a + 1))
        fields[0, at] = pressure
        fields[1, at] = saturation
        mobility = square / (square + 0.5 * rest * rest)
        perm = lookup(zone[at], perm_table)
        gated = perm * opened[0, at].astype(F32)
        near_side[0, at] = pressure
        near_side[1, at] = mobility
        near_side[2, at] = jnp.where(even_plane, gated, perm)
        far_side[0, at] = pressure
        far_side[1, at] = mobility
        far_side[2, at] = jnp.where(even_plane, perm, gated)


def lookup(zones, perm_table):
    perm = jnp.zeros(zones.shape, F32)
    for k in range(ZONES):
        perm = jnp.where(zones == k, perm_table[k], perm)
    return perm


def joined(first, second):
    both = first + second
    return jnp.where(both > 0.0, first * second / jnp.where(both > 0.0, both, 1.0), 0.0)


def ahead_y(field):
    rolled = pltpu.roll(field, NZ, 1)
    lane = lax.broadcasted_iota(jnp.int32, field.shape, 1)
    row = lax.broadcasted_iota(jnp.int32, field.shape, 0)
    below = pltpu.roll(rolled, field.shape[0] - 1, 0)
    below = jnp.where(row == field.shape[0] - 1, 0.0, below)
    return jnp.where(lane < LANES - NZ, rolled, below)


def behind_y(field):
    rolled = pltpu.roll(field, NZ, 1)
    lane = lax.broadcasted_iota(jnp.int32, field.shape, 1)
    row = lax.broadcasted_iota(jnp.int32, field.shape, 0)
    above = pltpu.roll(rolled, 1, 0)
    above = jnp.where(row == 0, 0.0, above)
    return jnp.where(lane >= NZ, rolled, above)


def ahead_z(field):
    lane = lax.broadcasted_iota(jnp.int32, field.shape, 1)
    return jnp.where(lane % NZ == NZ - 1, 0.0, pltpu.roll(field, LANES - 1, 1))


def behind_z(field):
    lane = lax.broadcasted_iota(jnp.int32, field.shape, 1)
    return jnp.where(lane % NZ == 0, 0.0, pltpu.roll(field, 1, 1))


def inner_kernel(first, last, zone, opened, perm_table, partial):
    pressure, mobility = [jnp.concatenate([first[k], last[k]], axis=0) for k in range(2)]
    perm = lookup(zone[...], perm_table)
    residual = jnp.zeros(pressure.shape, F32)
    for axis, ahead, behind in ((1, ahead_y, behind_y), (2, ahead_z, behind_z)):
        link = opened[axis].astype(F32) * joined(perm, ahead(perm))
        flux = link * (mobility + ahead(mobility)) * (pressure - ahead(pressure))
        residual = residual + (flux - behind(flux))
    partial[...] = residual


def outer_kernel(partial, *refs):
    residual = refs[-1]

    def flow(mine, other):
        link = joined(mine[2], other[2])
        return link * (mine[1] + other[1]) * (mine[0] - other[0])

    cut = refs[0].shape[1]
    for at, sides in ((slice(0, cut), refs[:4]), (slice(cut, ROWS), refs[4:8])):
        residual[at] = partial[at] + flow(sides[0], sides[3]) + flow(sides[1], sides[2])


def near(x):
    return pltpu.with_memory_space_constraint(x, pltpu.HBM)


def whole():
    return pl.BlockSpec(memory_space=pltpu.VMEM)


def params():
    return pltpu.CompilerParams(vmem_limit_bytes=40 * 1024 * 1024)


def body(
    features,
    block_scale,
    spec_weight,
    bypass_weight,
    mlp_in,
    mlp_out,
    decode_weight,
    zone_ids,
    face_open,
    perm_table,
):
    width, rows, cells = features.shape
    devices = lax.axis_size("gx")
    planes = rows * devices
    assert rows == 1 and cells == ROWS * LANES and width == TILES * SUB and devices % 2 == 0
    plane = features.reshape(width, cells)
    scale = block_scale.reshape(1, width)
    zone = zone_ids.reshape(ROWS, LANES)
    opened = face_open.reshape(3, ROWS, LANES)
    shares = devices // KY
    held = KZ // shares

    fixed = lambda i: (0, 0)
    cubes = lambda i: (0, 0, 0)
    steps = ROWS // QUARTER
    part = QUARTER
    span = part * LANES
    count = 2 * FOLD + 1
    lines = pl.pallas_call(
        forward_kernel,
        grid=(steps,),
        in_specs=[
            pl.BlockSpec((width, span), lambda i: (0, steps - 1 - i)),
            pl.BlockSpec((1, width), fixed),
            pl.BlockSpec((TWO * LANES, 2 * LANES), fixed),
            pl.BlockSpec((count * SUB, 2 * part * SUB), fixed),
            pl.BlockSpec((2, FOLD + 1, LANES), cubes),
        ],
        out_specs=pl.BlockSpec((KY * SUB, LANES), fixed),
        out_shape=jax.ShapeDtypeStruct((KY * SUB, LANES), F32),
        scratch_shapes=[pltpu.VMEM((2, (FOLD + 1) * SUB, 2 * LANES), F32)],
        compiler_params=params(),
        name="forward_yz",
    )(
        near(plane),
        near(scale),
        near(jnp.asarray(z_forward_table())),
        near(jnp.asarray(y_forward_table())),
        near(jnp.asarray(turn_forward_table())),
    )

    blocks = lines.reshape(KY, SUB, 2, shares, held * 2 * TILES)
    blocks = blocks.transpose(0, 3, 1, 2, 4).reshape(devices, SUB, 2 * held * 2 * TILES)
    blocks = lax.all_to_all(blocks, "gx", 0, 0, tiled=True)
    lines = blocks.reshape(planes * SUB, 2 * held * 2 * TILES)

    modes = spec_weight.shape[3]
    back = pl.pallas_call(
        mix_kernel,
        in_specs=[whole()] * 4,
        out_specs=whole(),
        out_shape=jax.ShapeDtypeStruct((planes * SUB, 2 * held * 2 * TILES), F32),
        scratch_shapes=[
            pltpu.VMEM((SUB, 2 * TILES, modes), F32),
            pltpu.VMEM((2, modes // LANES, 2 * width, LANES), F32),
        ],
        compiler_params=params(),
        name="mix_modes",
    )(
        lines,
        spec_weight,
        jnp.asarray(x_forward_table(planes)),
        jnp.asarray(x_back_table(planes)),
    )

    blocks = back.reshape(devices, SUB, 2 * held * 2 * TILES)
    blocks = lax.all_to_all(blocks, "gx", 0, 0, tiled=True)
    blocks = blocks.reshape(KY, shares, SUB, 2, held * 2 * TILES).transpose(0, 2, 3, 1, 4)
    lines = blocks.reshape(KY * SUB, 2 * HALF)

    def network(first, count, carried):
        at = first // count
        side = jax.ShapeDtypeStruct((3, count, LANES), F32)
        return pl.pallas_call(
            functools.partial(point_kernel, first=first),
            grid=(1,),
            in_specs=[
                pl.BlockSpec((KY * SUB, LANES), fixed),
                pl.BlockSpec((width, count * LANES), lambda i: (0, at)),
                pl.BlockSpec((1, width), fixed),
                pl.BlockSpec(bypass_weight.shape, fixed),
                pl.BlockSpec(mlp_in.shape[::-1], fixed),
                pl.BlockSpec(mlp_out.shape, fixed),
                pl.BlockSpec(decode_weight.shape, fixed),
                pl.BlockSpec((count, LANES), lambda i: (at, 0)),
                pl.BlockSpec((1, count, LANES), lambda i: (0, at, 0)),
                pl.BlockSpec(memory_space=pltpu.SMEM),
                pl.BlockSpec((QUARTER * SUB, 4 * FOLD * SUB), fixed),
                pl.BlockSpec((2 * LANES, TILES * LANES), fixed),
                pl.BlockSpec((2, KY, LANES), cubes),
            ]
            + [pl.BlockSpec(memory_space=pl.ANY)] * len(carried),
            out_specs=[
                pl.BlockSpec((2, count, LANES), lambda i: (0, at, 0)),
                pl.BlockSpec((3, count, LANES), cubes),
                pl.BlockSpec((3, count, LANES), cubes),
            ],
            out_shape=[
                jax.ShapeDtypeStruct((2, ROWS, LANES), F32),
                side,
                side,
            ],
            scratch_shapes=[pltpu.VMEM((count * SUB, TILES * LANES), F32)],
            input_output_aliases={13 + k: k for k in range(len(carried))},
            compiler_params=params(),
            cost_estimate=pl.CostEstimate(
                flops=count * LANES * 400000, bytes_accessed=count * LANES * 200, transcendentals=0
            ),
            name="point_network",
        )(
            lines,
            plane,
            scale,
            bypass_weight,
            mlp_in.T,
            mlp_out,
            decode_weight,
            zone,
            opened,
            perm_table,
            jnp.asarray(y_back_table()),
            jnp.asarray(z_back_table(planes * NY * NZ)),
            jnp.asarray(turn_back_table()),
            *carried,
        )

    far = [(i, i + 1) for i in range(1, devices - 1, 2)]
    far = far + [(b, a) for a, b in far]
    near_by = [(i, i + 1) for i in range(0, devices, 2)]
    near_by = near_by + [(b, a) for a, b in near_by]
    fields, *first = network(0, ROWS - QUARTER, ())
    first_other = [lax.ppermute(first[1], "gx", far), lax.ppermute(first[0], "gx", near_by)]
    fields, *last = network(ROWS - QUARTER, QUARTER, (fields,))
    last_other = [lax.ppermute(last[1], "gx", far), lax.ppermute(last[0], "gx", near_by)]
    partial = pl.pallas_call(
        inner_kernel,
        in_specs=[whole()] * 4 + [pl.BlockSpec(memory_space=pltpu.SMEM)],
        out_specs=whole(),
        out_shape=jax.ShapeDtypeStruct((ROWS, LANES), F32),
        compiler_params=params(),
        name="faces_in_plane",
    )(first[0], last[0], zone, opened, perm_table)
    residual = pl.pallas_call(
        outer_kernel,
        in_specs=[whole()] * 9,
        out_specs=whole(),
        out_shape=jax.ShapeDtypeStruct((ROWS, LANES), F32),
        compiler_params=params(),
        name="faces_between_planes",
    )(partial, *first, *first_other, *last, *last_other)
    return (fields.reshape(2, 1, cells), residual.reshape(1, cells))


def solution(mesh):
    in_specs = (
        P(None, ("groups", "gx"), None),
        P(None, ("groups", "gx")),
        P(None, None, None, "gx"),
        P(),
        P(),
        P(),
        P(),
        P(("groups", "gx"), None),
        P(None, ("groups", "gx"), None),
        P(),
    )
    out_specs = (P(None, ("groups", "gx"), None), P(("groups", "gx"), None))
    return jax.shard_map(body, mesh=mesh, in_specs=in_specs, out_specs=out_specs, check_vma=False)
```

```python
import functools
import math

import jax
import jax.numpy as jnp
import ml_dtypes
import numpy as np
from jax import lax
from jax.experimental import pallas as pl
from jax.experimental.pallas import tpu as pltpu
from jax.sharding import PartitionSpec as P

NY = 512
NZ = 64
KX = 32
KY = 32
KZ = 8
ZONES = 8
LANES = 128
SUB = 8
PAIRS = LANES // NZ
ROWS = NY // PAIRS
TILES = 4
TWO = 2
HALF = KZ * 2 * TILES
QUARTER = ROWS // 4
FOLD = KY // 2
GELU_A = math.sqrt(2.0 / math.pi)
GELU_B = GELU_A * 0.044715
F32 = jnp.float32
BF16 = jnp.bfloat16


def signed(count):
    steps = np.arange(count)
    return np.where(steps < count // 2, steps, steps - count)


def angles(freqs, positions, length):
    return 2.0 * np.pi * ((freqs[:, None] * positions[None, :]) % length) / length


def halves(table, axis):
    high = np.asarray(table, np.float64).astype(ml_dtypes.bfloat16)
    low = (table - high.astype(np.float64)).astype(ml_dtypes.bfloat16)
    return np.concatenate([high, low], axis=axis)


def spread(small):
    return np.kron(small, np.eye(SUB))


def z_forward_table():
    angle = angles(np.arange(KZ), np.arange(NZ), NZ)
    table = np.zeros((TWO, PAIRS, NZ, 2, KZ, PAIRS, 2, TWO))
    for t in range(TWO):
        for p in range(PAIRS):
            table[t, p, :, 0, :, p, 0, t] = np.cos(angle).T
            table[t, p, :, 0, :, p, 1, t] = -np.sin(angle).T
            table[t, p, :, 1, :, p, 0, t] = -np.sin(angle).T
            table[t, p, :, 1, :, p, 1, t] = -np.cos(angle).T
    return halves(table.reshape(TWO * LANES, LANES), 1)


def y_forward_table():
    angle = angles(np.arange(FOLD + 1), np.arange(QUARTER) * PAIRS, NY)
    return halves(np.concatenate([spread(np.cos(angle)), spread(np.sin(angle[1:]))], axis=0), 1)


def turn_forward_table():
    parity = angles(np.arange(FOLD + 1), np.arange(PAIRS), NY)
    parity = np.tile(np.repeat(parity, 2 * TWO, axis=1), (1, 2 * KZ))
    return np.stack([np.cos(parity), np.sin(parity)]).astype(np.float32)


def turn_back_table():
    parity = np.repeat(angles(signed(KY), np.array([1]), NY), LANES, axis=1)
    return np.stack([np.cos(parity), np.sin(parity)]).astype(np.float32)


def x_forward_table(planes):
    angle = angles(signed(KX), np.arange(planes), planes)

    def one(small):
        wide = np.zeros((2, planes, SUB // 2, SUB, KX))
        for s in range(SUB):
            wide[s // (SUB // 2), :, s % (SUB // 2), s, :] = small.T
        return wide.reshape(planes * SUB, SUB * KX)

    return np.concatenate([one(np.cos(angle)), one(np.sin(angle))], axis=0).astype(np.float32)


def x_back_table(planes):
    table = x_forward_table(planes).reshape(2, planes * SUB, SUB * KX)
    return np.concatenate([table[0], table[1]], axis=1)


def y_back_table():
    angle = angles(np.arange(1, FOLD + 1), np.arange(QUARTER) * PAIRS, NY)
    return halves(np.concatenate([spread(np.cos(angle).T), spread(np.sin(angle).T)], axis=1), 1)


def z_back_table(total):
    angle = angles(np.arange(KZ), np.arange(NZ), NZ)
    weight = np.where(np.arange(KZ) == 0, 1.0, 2.0)[:, None] / total
    table = np.zeros((PAIRS, KZ, TILES // TWO, 2, TWO, TILES, PAIRS, NZ))
    for t in range(TILES):
        for p in range(PAIRS):
            table[p, :, t // TWO, 0, t % TWO, t, p, :] = weight * np.cos(angle)
            table[p, :, t // TWO, 1, t % TWO, t, p, :] = -weight * np.sin(angle)
    return halves(table.reshape(PAIRS * HALF, TILES * LANES), 0)


def dot(a, b, dims=((1,), (0,)), precision=None):
    return lax.dot_general(a, b, (dims, ((), ())), precision=precision, preferred_element_type=F32)


def split(x):
    high = x.astype(BF16)
    return high, (x - high.astype(F32)).astype(BF16)


def column(row):
    n = row.shape[1]
    square = lax.broadcasted_iota(jnp.int32, (n, n), 0) == lax.broadcasted_iota(jnp.int32, (n, n), 1)
    return jnp.sum(jnp.where(square, row, 0.0), axis=1, keepdims=True)


def tall(table, first, count):
    return jnp.concatenate(
        [jnp.broadcast_to(table[k : k + 1], (SUB, LANES)) for k in range(first, first + count)],
        axis=0,
    )


def twice(x):
    return jnp.concatenate([x, x], axis=1)


def quarters(real, imag, turns):
    return ((real, imag), (-imag, real), (-real, -imag), (imag, -real))[turns % 4]


def forward_kernel(
    features, scale, table_z, table_y, turns, lines, values, held, factor, own_z, own_y, own_turns, done
):
    span = QUARTER * LANES
    chunks = features.shape[1] // span
    loads = [(scale, factor), (features.at[:, :span], held.at[0]), (table_z, own_z)]
    loads += [(table_y, own_y), (turns, own_turns)]
    loads += [(features.at[:, span * m : span * (m + 1)], held.at[m]) for m in range(1, chunks)]
    loads = [pltpu.make_async_copy(*pair, done.at[k]) for k, pair in enumerate(loads)]
    for load in loads:
        load.start()

    n = (FOLD + 1) * SUB
    even, odd = [None] * (FOLD + 1), [None] * (FOLD + 1)
    for m in range(chunks):
        if m == 0:
            for load in loads[:3]:
                load.wait()
            gain = column(factor[...])
        elif m == 1:
            for load in loads[5:]:
                load.wait()
        scaled = held[m].astype(F32) * gain
        values[:, span * m : span * (m + 1)] = scaled.astype(BF16)

        def tile(t, j):
            return scaled[SUB * t : SUB * (t + 1), LANES * j : LANES * (j + 1)]

        cells = jnp.concatenate(
            [
                jnp.concatenate([tile(t, j), tile(t + 1, j)], axis=1)
                for t in range(0, TILES, TWO)
                for j in range(QUARTER)
            ],
            axis=0,
        ).astype(BF16)
        part = dot(cells, own_z[...])
        part = part[:, :LANES] + part[:, LANES:]
        high, low = split(
            jnp.concatenate([part[: SUB * QUARTER], part[SUB * QUARTER :]], axis=1)
        )
        if m == 0:
            for load in loads[3:5]:
                load.wait()
        table = own_y[...]
        inner = table.shape[1] // 2
        sums = dot(
            jnp.concatenate([table[:, :inner], table], axis=1),
            jnp.concatenate([low, high, high], axis=0),
        )
        for k in range(FOLD + 1):
            real = sums[SUB * k : SUB * (k + 1)]
            imag = sums[n + SUB * (k - 1) : n + SUB * k] if k else jnp.zeros_like(real)
            real, imag = quarters(real, imag, m * k)
            even[k] = real if even[k] is None else even[k] + real
            odd[k] = imag if odd[k] is None else odd[k] + imag

    first, second = jnp.concatenate(even, axis=0), jnp.concatenate(odd, axis=0)
    cosine = twice(tall(own_turns[0], 0, FOLD + 1))
    sine = twice(tall(own_turns[1], 0, FOLD + 1))
    even = cosine * first - sine * second
    odd = sine * first + cosine * second
    lane = lax.broadcasted_iota(jnp.int32, (n, LANES), 1)
    own = (lane & (2 * TWO)) == 0

    def packed(sign):
        sides = []
        for k in range(2):
            at = slice(LANES * k, LANES * (k + 1))
            line = even[:, at] + sign * pltpu.roll(odd[:, at], HALF, 1)
            shift = LANES - 2 * TWO if k == 0 else 2 * TWO
            sides.append(line + pltpu.roll(line, shift, 1))
        line = jnp.where(own, sides[0], sides[1])
        raised = pltpu.roll(pltpu.roll(line, HALF, 1), n - SUB // 2, 0)
        return jnp.where(lane < HALF, line, raised)

    up, down = packed(1.0), packed(-1.0)
    for k in range(FOLD):
        lines[SUB // 2 * k : SUB // 2 * (k + 1)] = up[SUB * k : SUB * k + SUB // 2]
    for k in range(FOLD, 0, -1):
        at = (KY - k) * SUB // 2
        lines[at : at + SUB // 2] = down[SUB * k : SUB * k + SUB // 2]


def swap_blocks(pieces):
    lane = lax.broadcasted_iota(jnp.int32, pieces[0].shape, 1) // KX
    out = []
    for e in range(4):
        got = None
        for b in range(4):
            moved = pieces[b] if b == e else pltpu.roll(pieces[b], (KX * (b - e)) % LANES, 1)
            got = moved if got is None else jnp.where(lane == b, moved, got)
        out.append(got)
    return out


def diagonal(block):
    width = block.shape[1]
    wide = (1, SUB * width)
    if width % LANES:
        row = lax.broadcasted_iota(jnp.int32, (width, SUB * width), 0)
        lane = lax.broadcasted_iota(jnp.int32, (width, SUB * width), 1)
        spread_out = (lax.rem(lane, width) == row).astype(F32).astype(BF16)
        block = dot(block.astype(BF16), spread_out)
    else:
        block = jnp.concatenate([block] * SUB, axis=1)
    lane = lax.broadcasted_iota(jnp.int32, wide, 1)
    return jnp.concatenate(
        [
            jnp.where((lane >= width * g) & (lane < width * (g + 1)), block, 0.0)
            for g in range(SUB)
        ],
        axis=0,
    )


def turned_by_i(x, axis):
    size = x.shape[axis]
    place = lax.broadcasted_iota(jnp.int32, x.shape, axis)
    after = pltpu.roll(x, size - TWO, axis)
    before = pltpu.roll(x, TWO, axis)
    return jnp.where((place & TWO) == 0, -after, before)


def mix_kernel(
    lines,
    weight,
    table_x,
    table_back,
    bypass,
    mlp_in_t,
    mlp_out,
    decode,
    back,
    wide_bypass,
    wide_in,
    wide_out,
    modes,
    mixed,
):
    wide_bypass[...] = diagonal(bypass[...].astype(F32)).astype(BF16)
    wide_in[...] = diagonal(0.5 * mlp_in_t[...].astype(F32).T).astype(BF16)
    heads = 0.5 * dot(decode[...], mlp_out[...])
    heads = jnp.concatenate([diagonal(heads[k : k + 1]) for k in range(2)], axis=0)
    wide_out[...] = jnp.concatenate(split(heads), axis=0)

    highest = lax.Precision.HIGHEST
    half = lines.shape[1] // 2
    count = half // (2 * TILES)
    groups = count // 4
    flipped = lines[...].T
    straight = jnp.concatenate([flipped[:half], flipped[half:]], axis=1)
    pair = jnp.concatenate([straight, -turned_by_i(straight, 0)], axis=1)
    spectrum = dot(pair, table_x[...], precision=highest)
    for c in range(SUB // 4):
        for a in range(groups):
            got = swap_blocks(
                [
                    spectrum[SUB * (4 * a + b) : SUB * (4 * a + b + 1), LANES * c : LANES * (c + 1)]
                    for b in range(4)
                ]
            )
            for e in range(4):
                modes[4 * c + e, :, LANES * a : LANES * (a + 1)] = got[e]
    width = weight.shape[1]
    real = jnp.zeros((width, count * KX), F32)
    imag = jnp.zeros((width, count * KX), F32)
    for i in range(width):
        t, v = i // SUB, i % SUB
        at = t // TWO * 2 * TWO + t % TWO
        in_real = modes[v, at : at + 1, :]
        in_imag = modes[v, at + TWO : at + TWO + 1, :]
        w_real = weight[0, i].astype(F32)
        w_imag = weight[1, i].astype(F32)
        real += in_real * w_real - in_imag * w_imag
        imag += in_real * w_imag + in_imag * w_real
    for a in range(groups):
        for t in range(TILES):
            here = slice(SUB * t, SUB * (t + 1)), slice(LANES * a, LANES * (a + 1))
            at = (t // TWO * 2 * TWO + t % TWO) * SUB
            mixed[0, a, at : at + SUB] = real[here]
            mixed[1, a, at : at + SUB] = -imag[here]
            at += TWO * SUB
            mixed[0, a, at : at + SUB] = imag[here]
            mixed[1, a, at : at + SUB] = real[here]
    rows = []
    for k in range(2):
        seen = [
            [mixed[k, a, pl.ds(v, 2 * TILES, stride=SUB), :] for v in range(SUB)]
            for a in range(groups)
        ]
        parts = [[None] * (SUB // 4) for _ in range(count)]
        for c in range(SUB // 4):
            for a in range(groups):
                got = swap_blocks(seen[a][4 * c : 4 * c + 4])
                for b in range(4):
                    parts[4 * a + b][c] = got[b]
        rows.append(jnp.concatenate([jnp.concatenate(p, axis=1) for p in parts], axis=0))
    got = dot(table_back[...], jnp.concatenate(rows, axis=1), ((1,), (1,)), precision=highest)
    count = got.shape[0] // 2
    back[...] = jnp.concatenate([got[:count], got[count:]], axis=1)


def gelu_twice(x):
    return x + x * jnp.tanh(x * (GELU_A + GELU_B * (x * x)))


def point_kernel(
    lines,
    values,
    wide_bypass,
    wide_in,
    wide_out,
    zone,
    opened,
    perm_table,
    tables,
    turns,
    near_side,
    far_side,
    filled,
    smooth,
    first,
):
    rows = near_side.shape[1]
    sent = lines[...]
    rolled = pltpu.roll(sent, HALF, 1)
    top = lax.broadcasted_iota(jnp.int32, sent.shape, 0) % SUB < SUB // 2
    of_even = jnp.where(top, sent, pltpu.roll(rolled, SUB // 2, 0))
    of_odd = jnp.where(top, pltpu.roll(sent, sent.shape[0] - SUB // 2, 0), rolled)
    held = jnp.concatenate(
        [x[SUB * k : SUB * (k + 1)] for k in range(KY // 2) for x in (of_even, of_odd)], axis=0
    )
    low_half = lax.broadcasted_iota(jnp.int32, held.shape, 1) < HALF
    held = jnp.where(low_half, held, pltpu.roll(held, HALF, 1))
    other = turned_by_i(held, 1)
    cosine, sine = tall(turns[0], 0, KY), tall(turns[1], 0, KY)
    straight = jnp.where(low_half, held, cosine * held + sine * other)
    turned = jnp.where(low_half, other, cosine * other - sine * held)

    def at(x, k):
        return x[SUB * k : SUB * (k + 1)]

    even = [at(straight, k) + at(straight, KY - k) for k in range(1, FOLD)]
    odd = [at(turned, k) - at(turned, KY - k) for k in range(1, FOLD)]
    even.append(at(straight, FOLD))
    odd.append(-at(turned, FOLD))
    level = jnp.concatenate([at(straight, 0)] * QUARTER, axis=0)
    count = QUARTER * SUB
    table = jnp.concatenate([tables[count : count + LANES], tables[count:]], axis=0)
    for m in range(rows // QUARTER):
        sides = [
            quarters(real, -imag, (first // QUARTER + m) * k)
            for k, (real, imag) in enumerate(zip(even, odd), 1)
        ]
        sides = [real for real, _ in sides] + [-imag for _, imag in sides]
        sides = jnp.concatenate(split(jnp.concatenate(sides, axis=0)), axis=1)
        both = dot(tables[:count], jnp.concatenate([sides, sides], axis=0))
        high, low = split(both[:, :LANES] + both[:, LANES:] + level)
        smooth[QUARTER * SUB * m : QUARTER * SUB * (m + 1)] = dot(
            jnp.concatenate([low, high, high], axis=1), table
        )

    groups = rows // SUB

    def grouped(tile):
        return jnp.concatenate(
            [
                jnp.concatenate([tile(SUB * a + g) for a in range(groups)], axis=1)
                for g in range(SUB)
            ],
            axis=0,
        )

    own = grouped(lambda j: values[:, LANES * (first + j) : LANES * (first + j + 1)])
    spectral = grouped(
        lambda j: jnp.concatenate(
            [
                smooth[SUB * j : SUB * (j + 1), LANES * t : LANES * (t + 1)]
                for t in range(TILES)
            ],
            axis=0,
        )
    )
    lifted = gelu_twice(spectral + dot(wide_bypass[...], own)).astype(BF16)
    hidden = gelu_twice(dot(wide_in[...], lifted)).astype(BF16)
    decoded = dot(wide_out[...], hidden)
    decoded = decoded[: 2 * SUB] + decoded[2 * SUB :]
    even_plane = lax.axis_index("gx") % 2 == 0
    for a in range(rows // SUB):
        pressure = decoded[:SUB, LANES * a : LANES * (a + 1)]
        saturation = jax.nn.sigmoid(decoded[SUB:, LANES * a : LANES * (a + 1)])
        square = saturation * saturation
        rest = 1.0 - saturation
        at = slice(SUB * a, SUB * (a + 1))
        here = slice(first + SUB * a, first + SUB * (a + 1))
        filled[at] = saturation
        mobility = square / (square + 0.5 * rest * rest)
        perm = lookup(zone[here], perm_table)
        gated = perm * opened[0, here].astype(F32)
        near_side[0, at] = pressure
        near_side[1, at] = mobility
        near_side[2, at] = jnp.where(even_plane, gated, perm)
        far_side[0, at] = pressure
        far_side[1, at] = mobility
        far_side[2, at] = jnp.where(even_plane, perm, gated)


def lookup(zones, perm_table):
    perm = jnp.zeros(zones.shape, F32)
    for k in range(ZONES):
        perm = jnp.where(zones == k, perm_table[k], perm)
    return perm


def joined(first, second):
    both = first + second
    return jnp.where(both > 0.0, first * second / jnp.where(both > 0.0, both, 1.0), 0.0)


def ahead_y(field):
    rolled = pltpu.roll(field, NZ, 1)
    lane = lax.broadcasted_iota(jnp.int32, field.shape, 1)
    row = lax.broadcasted_iota(jnp.int32, field.shape, 0)
    below = pltpu.roll(rolled, field.shape[0] - 1, 0)
    below = jnp.where(row == field.shape[0] - 1, 0.0, below)
    return jnp.where(lane < LANES - NZ, rolled, below)


def behind_y(field):
    rolled = pltpu.roll(field, NZ, 1)
    lane = lax.broadcasted_iota(jnp.int32, field.shape, 1)
    row = lax.broadcasted_iota(jnp.int32, field.shape, 0)
    above = pltpu.roll(rolled, 1, 0)
    above = jnp.where(row == 0, 0.0, above)
    return jnp.where(lane >= NZ, rolled, above)


def ahead_z(field):
    lane = lax.broadcasted_iota(jnp.int32, field.shape, 1)
    return jnp.where(lane % NZ == NZ - 1, 0.0, pltpu.roll(field, LANES - 1, 1))


def behind_z(field):
    lane = lax.broadcasted_iota(jnp.int32, field.shape, 1)
    return jnp.where(lane % NZ == 0, 0.0, pltpu.roll(field, 1, 1))


def inner_kernel(
    first, last, first_filled, last_filled, zone, opened, perm_table, fields, partial
):
    pressure, mobility = [jnp.concatenate([first[k], last[k]], axis=0) for k in range(2)]
    fields[0] = pressure
    fields[1] = jnp.concatenate([first_filled[...], last_filled[...]], axis=0)
    perm = lookup(zone[...], perm_table)
    residual = jnp.zeros(pressure.shape, F32)
    for axis, ahead, behind in ((1, ahead_y, behind_y), (2, ahead_z, behind_z)):
        link = opened[axis].astype(F32) * joined(perm, ahead(perm))
        flux = link * (mobility + ahead(mobility)) * (pressure - ahead(pressure))
        residual = residual + (flux - behind(flux))
    partial[...] = residual


def outer_kernel(partial, *refs):
    residual = refs[-1]

    def flow(mine, other):
        link = joined(mine[2], other[2])
        return link * (mine[1] + other[1]) * (mine[0] - other[0])

    cut = refs[0].shape[1]
    for at, sides in ((slice(0, cut), refs[:4]), (slice(cut, ROWS), refs[4:8])):
        residual[at] = partial[at] + flow(sides[0], sides[3]) + flow(sides[1], sides[2])


def near(x):
    return pltpu.with_memory_space_constraint(x, pltpu.HBM)


def whole():
    return pl.BlockSpec(memory_space=pltpu.VMEM)


def params():
    return pltpu.CompilerParams(vmem_limit_bytes=40 * 1024 * 1024)


def body(
    features,
    block_scale,
    spec_weight,
    bypass_weight,
    mlp_in,
    mlp_out,
    decode_weight,
    zone_ids,
    face_open,
    perm_table,
):
    width, rows, cells = features.shape
    devices = lax.axis_size("gx")
    planes = rows * devices
    assert rows == 1 and cells == ROWS * LANES and width == TILES * SUB and devices % 2 == 0
    plane = features.reshape(width, cells)
    scale = block_scale.reshape(1, width)
    zone = zone_ids.reshape(ROWS, LANES)
    opened = face_open.reshape(3, ROWS, LANES)
    shares = devices // KY
    held = KZ // shares

    span = QUARTER * LANES
    chunks = cells // span
    table_z, table_y, turns = z_forward_table(), y_forward_table(), turn_forward_table()
    lines, values = pl.pallas_call(
        forward_kernel,
        in_specs=[pl.BlockSpec(memory_space=pl.ANY)] * 5,
        out_specs=[whole()] * 2,
        out_shape=[
            jax.ShapeDtypeStruct((KY * SUB // 2, LANES), F32),
            jax.ShapeDtypeStruct((width, cells), BF16),
        ],
        scratch_shapes=[
            pltpu.VMEM((chunks, width, span), BF16),
            pltpu.VMEM((1, width), F32),
            pltpu.VMEM(table_z.shape, BF16),
            pltpu.VMEM(table_y.shape, BF16),
            pltpu.VMEM(turns.shape, F32),
            pltpu.SemaphoreType.DMA((4 + chunks,)),
        ],
        compiler_params=params(),
        name="forward_yz",
    )(*map(near, (plane, scale, jnp.asarray(table_z), jnp.asarray(table_y), jnp.asarray(turns))))

    part = SUB // 2
    share = held * 2 * TILES
    blocks = lines.reshape(KY, part, 2, shares, share)
    blocks = blocks.transpose(0, 3, 1, 2, 4).reshape(devices, part, 2 * share)
    blocks = lax.all_to_all(blocks, "gx", 0, 0, tiled=True)
    lines = blocks.reshape(planes * part, 2 * share)

    modes = spec_weight.shape[3]
    hidden = mlp_in.shape[0]
    back, *wide = pl.pallas_call(
        mix_kernel,
        in_specs=[whole()] * 8,
        out_specs=[whole()] * 4,
        out_shape=[
            jax.ShapeDtypeStruct((planes * part, 2 * share), F32),
            jax.ShapeDtypeStruct((SUB * width, SUB * width), BF16),
            jax.ShapeDtypeStruct((SUB * hidden, SUB * width), BF16),
            jax.ShapeDtypeStruct((4 * SUB, SUB * hidden), BF16),
        ],
        scratch_shapes=[
            pltpu.VMEM((SUB, 2 * TILES, modes), F32),
            pltpu.VMEM((2, modes // LANES, 2 * width, LANES), F32),
        ],
        compiler_params=params(),
        name="mix_modes",
    )(
        lines,
        spec_weight,
        jnp.asarray(x_forward_table(planes)),
        jnp.asarray(x_back_table(planes)),
        bypass_weight,
        mlp_in.T,
        mlp_out,
        decode_weight,
    )

    blocks = back.reshape(devices, part, 2 * share)
    blocks = lax.all_to_all(blocks, "gx", 0, 0, tiled=True)
    blocks = blocks.reshape(KY, shares, part, 2, share).transpose(0, 2, 3, 1, 4)
    lines = blocks.reshape(KY * part, 2 * HALF)

    tables = np.concatenate([y_back_table(), z_back_table(planes * NY * NZ)], axis=0)
    tables = jnp.asarray(tables)

    def network(first, count):
        side = jax.ShapeDtypeStruct((3, count, LANES), F32)
        smem = pl.BlockSpec(memory_space=pltpu.SMEM)
        return pl.pallas_call(
            functools.partial(point_kernel, first=first),
            in_specs=[whole()] * 7 + [smem] + [whole()] * 2,
            out_specs=[whole()] * 3,
            out_shape=[side, side, jax.ShapeDtypeStruct((count, LANES), F32)],
            scratch_shapes=[pltpu.VMEM((count * SUB, TILES * LANES), F32)],
            compiler_params=params(),
            cost_estimate=pl.CostEstimate(
                flops=count * LANES * 400000, bytes_accessed=count * LANES * 200, transcendentals=0
            ),
            name="point_network",
        )(
            lines,
            values,
            *wide,
            zone,
            opened,
            perm_table,
            tables,
            jnp.asarray(turn_back_table()),
        )

    far = [(i, i + 1) for i in range(1, devices - 1, 2)]
    far = far + [(b, a) for a, b in far]
    near_by = [(i, i + 1) for i in range(0, devices, 2)]
    near_by = near_by + [(b, a) for a, b in near_by]
    *first, first_filled = network(0, ROWS - QUARTER)
    first_other = [lax.ppermute(first[1], "gx", far), lax.ppermute(first[0], "gx", near_by)]
    *last, last_filled = network(ROWS - QUARTER, QUARTER)
    last_other = [lax.ppermute(last[1], "gx", far), lax.ppermute(last[0], "gx", near_by)]
    fields, partial = pl.pallas_call(
        inner_kernel,
        in_specs=[whole()] * 6 + [pl.BlockSpec(memory_space=pltpu.SMEM)],
        out_specs=[whole()] * 2,
        out_shape=[
            jax.ShapeDtypeStruct((2, ROWS, LANES), F32),
            jax.ShapeDtypeStruct((ROWS, LANES), F32),
        ],
        compiler_params=params(),
        name="faces_in_plane",
    )(first[0], last[0], first_filled, last_filled, zone, opened, perm_table)
    residual = pl.pallas_call(
        outer_kernel,
        in_specs=[whole()] * 9,
        out_specs=whole(),
        out_shape=jax.ShapeDtypeStruct((ROWS, LANES), F32),
        compiler_params=params(),
        name="faces_between_planes",
    )(partial, *first, *first_other, *last, *last_other)
    return (fields.reshape(2, 1, cells), residual.reshape(1, cells))


def solution(mesh):
    in_specs = (
        P(None, ("groups", "gx"), None),
        P(None, ("groups", "gx")),
        P(None, None, None, "gx"),
        P(),
        P(),
        P(),
        P(),
        P(("groups", "gx"), None),
        P(None, ("groups", "gx"), None),
        P(),
    )
    out_specs = (P(None, ("groups", "gx"), None), P(("groups", "gx"), None))
    return jax.shard_map(body, mesh=mesh, in_specs=in_specs, out_specs=out_specs, check_vma=False)
```

```python
import functools
import math

import jax
import jax.numpy as jnp
import ml_dtypes
import numpy as np
from jax import lax
from jax.experimental import pallas as pl
from jax.experimental.pallas import tpu as pltpu
from jax.sharding import PartitionSpec as P

NY = 512
NZ = 64
KX = 32
KY = 32
KZ = 8
ZONES = 8
LANES = 128
SUB = 8
PAIRS = LANES // NZ
ROWS = NY // PAIRS
TILES = 4
TWO = 2
HALF = KZ * 2 * TILES
QUARTER = ROWS // 4
FOLD = KY // 2
GELU_A = math.sqrt(2.0 / math.pi)
GELU_B = GELU_A * 0.044715
F32 = jnp.float32
BF16 = jnp.bfloat16


def signed(count):
    steps = np.arange(count)
    return np.where(steps < count // 2, steps, steps - count)


def angles(freqs, positions, length):
    return 2.0 * np.pi * ((freqs[:, None] * positions[None, :]) % length) / length


def halves(table, axis):
    high = np.asarray(table, np.float64).astype(ml_dtypes.bfloat16)
    low = (table - high.astype(np.float64)).astype(ml_dtypes.bfloat16)
    return np.concatenate([high, low], axis=axis)


def spread(small):
    return np.kron(small, np.eye(SUB))


def z_forward_table():
    angle = angles(np.arange(KZ), np.arange(NZ), NZ)
    table = np.zeros((TWO, PAIRS, NZ, 2, KZ, PAIRS, 2, TWO))
    for t in range(TWO):
        for p in range(PAIRS):
            table[t, p, :, 0, :, p, 0, t] = np.cos(angle).T
            table[t, p, :, 0, :, p, 1, t] = -np.sin(angle).T
            table[t, p, :, 1, :, p, 0, t] = -np.sin(angle).T
            table[t, p, :, 1, :, p, 1, t] = -np.cos(angle).T
    return halves(table.reshape(TWO * LANES, LANES), 1)


def y_forward_table():
    angle = angles(np.arange(FOLD + 1), np.arange(QUARTER) * PAIRS, NY)
    return halves(np.concatenate([spread(np.cos(angle)), spread(np.sin(angle[1:]))], axis=0), 1)


def turn_forward_table():
    parity = angles(np.arange(FOLD + 1), np.arange(PAIRS), NY)
    parity = np.tile(np.repeat(parity, 2 * TWO, axis=1), (1, 2 * KZ))
    return np.stack([np.cos(parity), np.sin(parity)]).astype(np.float32)


def turn_back_table():
    parity = np.repeat(angles(signed(KY), np.array([1]), NY), LANES, axis=1)
    return np.stack([np.cos(parity), np.sin(parity)]).astype(np.float32)


def x_forward_table(planes):
    angle = angles(signed(KX), np.arange(planes), planes)

    def one(small):
        wide = np.zeros((2, planes, SUB // 2, SUB, KX))
        for s in range(SUB):
            wide[s // (SUB // 2), :, s % (SUB // 2), s, :] = small.T
        return wide.reshape(planes * SUB, SUB * KX)

    return np.concatenate([one(np.cos(angle)), one(np.sin(angle))], axis=0)


def x_back_table(planes):
    table = x_forward_table(planes).reshape(2, planes * SUB, SUB * KX)
    return np.concatenate([table[0], table[1]], axis=1)


def y_back_table():
    angle = angles(np.arange(1, FOLD + 1), np.arange(QUARTER) * PAIRS, NY)
    return halves(np.concatenate([spread(np.cos(angle).T), spread(np.sin(angle).T)], axis=1), 1)


def z_back_table(total):
    angle = angles(np.arange(KZ), np.arange(NZ), NZ)
    weight = np.where(np.arange(KZ) == 0, 1.0, 2.0)[:, None] / total
    table = np.zeros((PAIRS, KZ, TILES // TWO, 2, TWO, TILES, PAIRS, NZ))
    for t in range(TILES):
        for p in range(PAIRS):
            table[p, :, t // TWO, 0, t % TWO, t, p, :] = weight * np.cos(angle)
            table[p, :, t // TWO, 1, t % TWO, t, p, :] = -weight * np.sin(angle)
    return halves(table.reshape(PAIRS * HALF, TILES * LANES), 0)


def dot(a, b, dims=((1,), (0,)), precision=None):
    return lax.dot_general(a, b, (dims, ((), ())), precision=precision, preferred_element_type=F32)


def split(x):
    high = x.astype(BF16)
    return high, (x - high.astype(F32)).astype(BF16)


def column(row):
    n = row.shape[1]
    square = lax.broadcasted_iota(jnp.int32, (n, n), 0) == lax.broadcasted_iota(jnp.int32, (n, n), 1)
    return jnp.sum(jnp.where(square, row, 0.0), axis=1, keepdims=True)


def tall(table, first, count):
    return jnp.concatenate(
        [jnp.broadcast_to(table[k : k + 1], (SUB, LANES)) for k in range(first, first + count)],
        axis=0,
    )


def twice(x):
    return jnp.concatenate([x, x], axis=1)


def quarters(real, imag, turns):
    return ((real, imag), (-imag, real), (-real, -imag), (imag, -real))[turns % 4]


def forward_kernel(
    features, scale, table_z, table_y, turns, lines, values, held, factor, own_z, own_y, own_turns, done
):
    span = QUARTER * LANES
    chunks = features.shape[1] // span
    loads = [(scale, factor), (features.at[:, :span], held.at[0]), (table_z, own_z)]
    loads += [(table_y, own_y), (turns, own_turns)]
    loads += [(features.at[:, span * m : span * (m + 1)], held.at[m]) for m in range(1, chunks)]
    loads = [pltpu.make_async_copy(*pair, done.at[k]) for k, pair in enumerate(loads)]
    for load in loads:
        load.start()

    n = (FOLD + 1) * SUB
    even, odd = [None] * (FOLD + 1), [None] * (FOLD + 1)

    def along_z(m):
        scaled = held[m].astype(F32) * gain
        values[:, span * m : span * (m + 1)] = scaled.astype(BF16)

        def tile(t, j):
            return scaled[SUB * t : SUB * (t + 1), LANES * j : LANES * (j + 1)]

        cells = jnp.concatenate(
            [
                jnp.concatenate([tile(t, j), tile(t + 1, j)], axis=1)
                for t in range(0, TILES, TWO)
                for j in range(QUARTER)
            ],
            axis=0,
        ).astype(BF16)
        part = dot(cells, own_z[...])
        part = part[:, :LANES] + part[:, LANES:]
        high, low = split(
            jnp.concatenate([part[: SUB * QUARTER], part[SUB * QUARTER :]], axis=1)
        )
        return jnp.concatenate([low, high, high], axis=0)

    def along_y(m, part):
        table = own_y[...]
        inner = table.shape[1] // 2
        sums = dot(jnp.concatenate([table[:, :inner], table], axis=1), part)
        for k in range(FOLD + 1):
            real = sums[SUB * k : SUB * (k + 1)]
            imag = sums[n + SUB * (k - 1) : n + SUB * k] if k else jnp.zeros_like(real)
            real, imag = quarters(real, imag, m * k)
            even[k] = real if even[k] is None else even[k] + real
            odd[k] = imag if odd[k] is None else odd[k] + imag

    for load in loads[:3]:
        load.wait()
    gain = column(factor[...])
    part = along_z(0)
    for load in loads[3:5]:
        load.wait()
    along_y(0, part)
    for load in loads[5:]:
        load.wait()
    parts = [along_z(m) for m in range(1, chunks)]
    for m, part in enumerate(parts, 1):
        along_y(m, part)

    first, second = jnp.concatenate(even, axis=0), jnp.concatenate(odd, axis=0)
    cosine = twice(tall(own_turns[0], 0, FOLD + 1))
    sine = twice(tall(own_turns[1], 0, FOLD + 1))
    even = cosine * first - sine * second
    odd = sine * first + cosine * second
    lane = lax.broadcasted_iota(jnp.int32, (n, LANES), 1)
    own = (lane & (2 * TWO)) == 0

    def packed(sign):
        sides = []
        for k in range(2):
            at = slice(LANES * k, LANES * (k + 1))
            line = even[:, at] + sign * pltpu.roll(odd[:, at], HALF, 1)
            shift = LANES - 2 * TWO if k == 0 else 2 * TWO
            sides.append(line + pltpu.roll(line, shift, 1))
        line = jnp.where(own, sides[0], sides[1])
        raised = pltpu.roll(pltpu.roll(line, HALF, 1), n - SUB // 2, 0)
        return jnp.where(lane < HALF, line, raised)

    up, down = packed(1.0), packed(-1.0)
    for k in range(FOLD):
        lines[SUB // 2 * k : SUB // 2 * (k + 1)] = up[SUB * k : SUB * k + SUB // 2]
    for k in range(FOLD, 0, -1):
        at = (KY - k) * SUB // 2
        lines[at : at + SUB // 2] = down[SUB * k : SUB * k + SUB // 2]


def swap_blocks(pieces):
    lane = lax.broadcasted_iota(jnp.int32, pieces[0].shape, 1) // KX
    out = []
    for e in range(4):
        got = None
        for b in range(4):
            moved = pieces[b] if b == e else pltpu.roll(pieces[b], (KX * (b - e)) % LANES, 1)
            got = moved if got is None else jnp.where(lane == b, moved, got)
        out.append(got)
    return out


def diagonal(block):
    width = block.shape[1]
    wide = (1, SUB * width)
    if width % LANES:
        row = lax.broadcasted_iota(jnp.int32, (width, SUB * width), 0)
        lane = lax.broadcasted_iota(jnp.int32, (width, SUB * width), 1)
        spread_out = (lax.rem(lane, width) == row).astype(F32).astype(BF16)
        block = dot(block, spread_out)
    else:
        block = jnp.concatenate([block.astype(F32)] * SUB, axis=1)
    lane = lax.broadcasted_iota(jnp.int32, wide, 1)
    return jnp.concatenate(
        [
            jnp.where((lane >= width * g) & (lane < width * (g + 1)), block, 0.0).astype(BF16)
            for g in range(SUB)
        ],
        axis=0,
    )


def turned_by_i(x, axis):
    size = x.shape[axis]
    place = lax.broadcasted_iota(jnp.int32, x.shape, axis)
    after = pltpu.roll(x, size - TWO, axis)
    before = pltpu.roll(x, TWO, axis)
    return jnp.where((place & TWO) == 0, -after, before)


def mix_kernel(
    lines,
    weight,
    table_x,
    table_back,
    bypass,
    mlp_in_t,
    mlp_out,
    decode,
    back,
    wide_bypass,
    wide_in,
    wide_out,
    modes,
    mixed,
):
    wide_bypass[...] = diagonal(bypass[...])
    inner = 0.5 * mlp_in_t[...].astype(F32)
    count = wide_out.shape[1]
    wide_in[:count] = diagonal(inner.T.astype(BF16))
    heads = 0.5 * dot(decode[...], mlp_out[...])
    through = dot(heads, inner, ((1,), (1,)), precision=lax.Precision.HIGHEST)
    def rows_of(x):
        rows = [part[k : k + 1] for part in split(x) for k in range(2)]
        return jnp.concatenate([diagonal(row).astype(F32) for row in rows], axis=0).astype(BF16)

    wide_out[...] = rows_of(heads)
    wide_in[count:] = rows_of(through)

    half = lines.shape[1] // 2
    count = half // (2 * TILES)
    groups = count // 4
    flipped = lines[...].T
    straight = jnp.concatenate([flipped[:half], flipped[half:]], axis=1)
    pair = jnp.concatenate([straight, -turned_by_i(straight, 0)], axis=1)
    high, low = split(pair)
    table = table_x[...]
    inner = table.shape[0] // 2
    spectrum = dot(
        jnp.concatenate([low, high, high], axis=1),
        jnp.concatenate([table[:inner], table], axis=0),
    )
    for c in range(SUB // 4):
        for a in range(groups):
            got = swap_blocks(
                [
                    spectrum[SUB * (4 * a + b) : SUB * (4 * a + b + 1), LANES * c : LANES * (c + 1)]
                    for b in range(4)
                ]
            )
            for e in range(4):
                modes[4 * c + e, :, LANES * a : LANES * (a + 1)] = got[e]
    width = weight.shape[1]
    real = jnp.zeros((width, count * KX), F32)
    imag = jnp.zeros((width, count * KX), F32)
    for i in range(width):
        t, v = i // SUB, i % SUB
        at = t // TWO * 2 * TWO + t % TWO
        in_real = modes[v, at : at + 1, :]
        in_imag = modes[v, at + TWO : at + TWO + 1, :]
        w_real = weight[0, i].astype(F32)
        w_imag = weight[1, i].astype(F32)
        real += in_real * w_real - in_imag * w_imag
        imag += in_real * w_imag + in_imag * w_real
    for a in range(groups):
        for t in range(TILES):
            here = slice(SUB * t, SUB * (t + 1)), slice(LANES * a, LANES * (a + 1))
            at = (t // TWO * 2 * TWO + t % TWO) * SUB
            mixed[0, a, at : at + SUB] = real[here]
            mixed[1, a, at : at + SUB] = -imag[here]
            at += TWO * SUB
            mixed[0, a, at : at + SUB] = imag[here]
            mixed[1, a, at : at + SUB] = real[here]
    rows = []
    for k in range(2):
        seen = [
            [mixed[k, a, pl.ds(v, 2 * TILES, stride=SUB), :] for v in range(SUB)]
            for a in range(groups)
        ]
        parts = [[None] * (SUB // 4) for _ in range(count)]
        for c in range(SUB // 4):
            for a in range(groups):
                got = swap_blocks(seen[a][4 * c : 4 * c + 4])
                for b in range(4):
                    parts[4 * a + b][c] = got[b]
        rows.append(jnp.concatenate([jnp.concatenate(p, axis=1) for p in parts], axis=0))
    high, low = split(jnp.concatenate(rows, axis=1))
    table = table_back[...]
    inner = table.shape[1] // 2
    got = dot(
        jnp.concatenate([table[:, :inner], table], axis=1),
        jnp.concatenate([low, high, high], axis=1),
        ((1,), (1,)),
    )
    count = got.shape[0] // 2
    back[...] = jnp.concatenate([got[:count], got[count:]], axis=1)


def gelu_twice(x):
    return x + x * jnp.tanh(x * (GELU_A + GELU_B * (x * x)))


def point_kernel(
    lines,
    values,
    wide_bypass,
    wide_in,
    wide_out,
    zone,
    opened,
    perm_table,
    tables,
    turns,
    near_side,
    far_side,
    filled,
    smooth,
    first,
):
    rows = near_side.shape[1]
    sent = lines[...]
    rolled = pltpu.roll(sent, HALF, 1)
    top = lax.broadcasted_iota(jnp.int32, sent.shape, 0) % SUB < SUB // 2
    of_even = jnp.where(top, sent, pltpu.roll(rolled, SUB // 2, 0))
    of_odd = jnp.where(top, pltpu.roll(sent, sent.shape[0] - SUB // 2, 0), rolled)
    held = jnp.concatenate(
        [x[SUB * k : SUB * (k + 1)] for k in range(KY // 2) for x in (of_even, of_odd)], axis=0
    )
    low_half = lax.broadcasted_iota(jnp.int32, held.shape, 1) < HALF
    held = jnp.where(low_half, held, pltpu.roll(held, HALF, 1))
    other = turned_by_i(held, 1)
    cosine, sine = tall(turns[0], 0, KY), tall(turns[1], 0, KY)
    straight = jnp.where(low_half, held, cosine * held + sine * other)
    turned = jnp.where(low_half, other, cosine * other - sine * held)

    def at(x, k):
        return x[SUB * k : SUB * (k + 1)]

    even = [at(straight, k) + at(straight, KY - k) for k in range(1, FOLD)]
    odd = [at(turned, k) - at(turned, KY - k) for k in range(1, FOLD)]
    even.append(at(straight, FOLD))
    odd.append(-at(turned, FOLD))
    level = jnp.concatenate([at(straight, 0)] * QUARTER, axis=0)
    count = QUARTER * SUB
    table = jnp.concatenate([tables[count : count + LANES], tables[count:]], axis=0)
    for m in range(rows // QUARTER):
        sides = [
            quarters(real, -imag, (first // QUARTER + m) * k)
            for k, (real, imag) in enumerate(zip(even, odd), 1)
        ]
        sides = [real for real, _ in sides] + [-imag for _, imag in sides]
        sides = jnp.concatenate(split(jnp.concatenate(sides, axis=0)), axis=1)
        both = dot(tables[:count], jnp.concatenate([sides, sides], axis=0))
        high, low = split(both[:, :LANES] + both[:, LANES:] + level)
        smooth[QUARTER * SUB * m : QUARTER * SUB * (m + 1)] = dot(
            jnp.concatenate([low, high, high], axis=1), table
        )

    groups = rows // SUB

    def grouped(tile):
        return jnp.concatenate(
            [
                jnp.concatenate([tile(SUB * a + g) for a in range(groups)], axis=1)
                for g in range(SUB)
            ],
            axis=0,
        )

    own = grouped(lambda j: values[:, LANES * (first + j) : LANES * (first + j + 1)])
    spectral = grouped(
        lambda j: jnp.concatenate(
            [
                smooth[SUB * j : SUB * (j + 1), LANES * t : LANES * (t + 1)]
                for t in range(TILES)
            ],
            axis=0,
        )
    )
    lifted = gelu_twice(spectral + dot(wide_bypass[...], own)).astype(BF16)
    inner = dot(wide_in[...], lifted)
    count = wide_out.shape[1]
    decoded = dot(wide_out[...], curved(inner[:count])) + inner[count:]
    decoded = decoded[: 2 * SUB] + decoded[2 * SUB :]
    even_plane = lax.axis_index("gx") % 2 == 0
    for a in range(rows // SUB):
        pressure = decoded[:SUB, LANES * a : LANES * (a + 1)]
        saturation = jax.nn.sigmoid(decoded[SUB:, LANES * a : LANES * (a + 1)])
        square = saturation * saturation
        rest = 1.0 - saturation
        at = slice(SUB * a, SUB * (a + 1))
        here = slice(first + SUB * a, first + SUB * (a + 1))
        filled[at] = saturation
        mobility = square / (square + 0.5 * rest * rest)
        perm = lookup(zone[here], perm_table)
        gated = perm * opened[0, here].astype(F32)
        near_side[0, at] = pressure
        near_side[1, at] = mobility
        near_side[2, at] = jnp.where(even_plane, gated, perm)
        far_side[0, at] = pressure
        far_side[1, at] = mobility
        far_side[2, at] = jnp.where(even_plane, perm, gated)


def lookup(zones, perm_table):
    perm = jnp.zeros(zones.shape, F32)
    for k in range(ZONES):
        perm = jnp.where(zones == k, perm_table[k], perm)
    return perm


def curved(x):
    x = x.astype(BF16)
    return x * jnp.tanh(x * (BF16(GELU_A) + BF16(GELU_B) * (x * x)))


def joined(first, second):
    both = first + second
    return jnp.where(both > 0.0, first * second / jnp.where(both > 0.0, both, 1.0), 0.0)


def ahead_y(field):
    rolled = pltpu.roll(field, NZ, 1)
    lane = lax.broadcasted_iota(jnp.int32, field.shape, 1)
    row = lax.broadcasted_iota(jnp.int32, field.shape, 0)
    below = pltpu.roll(rolled, field.shape[0] - 1, 0)
    below = jnp.where(row == field.shape[0] - 1, 0.0, below)
    return jnp.where(lane < LANES - NZ, rolled, below)


def behind_y(field):
    rolled = pltpu.roll(field, NZ, 1)
    lane = lax.broadcasted_iota(jnp.int32, field.shape, 1)
    row = lax.broadcasted_iota(jnp.int32, field.shape, 0)
    above = pltpu.roll(rolled, 1, 0)
    above = jnp.where(row == 0, 0.0, above)
    return jnp.where(lane >= NZ, rolled, above)


def ahead_z(field):
    lane = lax.broadcasted_iota(jnp.int32, field.shape, 1)
    return jnp.where(lane % NZ == NZ - 1, 0.0, pltpu.roll(field, LANES - 1, 1))


def behind_z(field):
    lane = lax.broadcasted_iota(jnp.int32, field.shape, 1)
    return jnp.where(lane % NZ == 0, 0.0, pltpu.roll(field, 1, 1))


def inner_kernel(
    first, last, first_filled, last_filled, zone, opened, perm_table, fields, partial
):
    pressure, mobility = [jnp.concatenate([first[k], last[k]], axis=0) for k in range(2)]
    fields[0] = pressure
    fields[1] = jnp.concatenate([first_filled[...], last_filled[...]], axis=0)
    perm = lookup(zone[...], perm_table)
    residual = jnp.zeros(pressure.shape, F32)
    for axis, ahead, behind in ((1, ahead_y, behind_y), (2, ahead_z, behind_z)):
        link = opened[axis].astype(F32) * joined(perm, ahead(perm))
        flux = link * (mobility + ahead(mobility)) * (pressure - ahead(pressure))
        residual = residual + (flux - behind(flux))
    partial[...] = residual


def outer_kernel(partial, *refs):
    residual = refs[-1]

    def flow(mine, other):
        link = joined(mine[2], other[2])
        return link * (mine[1] + other[1]) * (mine[0] - other[0])

    cut = refs[0].shape[1]
    for at, sides in ((slice(0, cut), refs[:4]), (slice(cut, ROWS), refs[4:8])):
        residual[at] = partial[at] + flow(sides[0], sides[3]) + flow(sides[1], sides[2])


def near(x):
    return pltpu.with_memory_space_constraint(x, pltpu.HBM)


def whole():
    return pl.BlockSpec(memory_space=pltpu.VMEM)


def params():
    return pltpu.CompilerParams(vmem_limit_bytes=40 * 1024 * 1024)


def body(
    features,
    block_scale,
    spec_weight,
    bypass_weight,
    mlp_in,
    mlp_out,
    decode_weight,
    zone_ids,
    face_open,
    perm_table,
):
    width, rows, cells = features.shape
    devices = lax.axis_size("gx")
    planes = rows * devices
    assert rows == 1 and cells == ROWS * LANES and width == TILES * SUB and devices % 2 == 0
    plane = features.reshape(width, cells)
    scale = block_scale.reshape(1, width)
    zone = zone_ids.reshape(ROWS, LANES)
    opened = face_open.reshape(3, ROWS, LANES)
    shares = devices // KY
    held = KZ // shares

    span = QUARTER * LANES
    chunks = cells // span
    table_z, table_y, turns = z_forward_table(), y_forward_table(), turn_forward_table()
    lines, values = pl.pallas_call(
        forward_kernel,
        in_specs=[pl.BlockSpec(memory_space=pl.ANY)] * 5,
        out_specs=[whole()] * 2,
        out_shape=[
            jax.ShapeDtypeStruct((KY * SUB // 2, LANES), F32),
            jax.ShapeDtypeStruct((width, cells), BF16),
        ],
        scratch_shapes=[
            pltpu.VMEM((chunks, width, span), BF16),
            pltpu.VMEM((1, width), F32),
            pltpu.VMEM(table_z.shape, BF16),
            pltpu.VMEM(table_y.shape, BF16),
            pltpu.VMEM(turns.shape, F32),
            pltpu.SemaphoreType.DMA((4 + chunks,)),
        ],
        compiler_params=params(),
        name="forward_yz",
    )(*map(near, (plane, scale, jnp.asarray(table_z), jnp.asarray(table_y), jnp.asarray(turns))))

    part = SUB // 2
    share = held * 2 * TILES
    blocks = lines.reshape(KY, part, 2, shares, share)
    blocks = blocks.transpose(0, 3, 1, 2, 4).reshape(devices, part, 2 * share)
    blocks = lax.all_to_all(blocks, "gx", 0, 0, tiled=True)
    lines = blocks.reshape(planes * part, 2 * share)

    modes = spec_weight.shape[3]
    hidden = mlp_in.shape[0]
    back, *wide = pl.pallas_call(
        mix_kernel,
        in_specs=[whole()] * 8,
        out_specs=[whole()] * 4,
        out_shape=[
            jax.ShapeDtypeStruct((planes * part, 2 * share), F32),
            jax.ShapeDtypeStruct((SUB * width, SUB * width), BF16),
            jax.ShapeDtypeStruct((SUB * hidden + 4 * SUB, SUB * width), BF16),
            jax.ShapeDtypeStruct((4 * SUB, SUB * hidden), BF16),
        ],
        scratch_shapes=[
            pltpu.VMEM((SUB, 2 * TILES, modes), F32),
            pltpu.VMEM((2, modes // LANES, 2 * width, LANES), F32),
        ],
        compiler_params=params(),
        name="mix_modes",
    )(
        lines,
        spec_weight,
        jnp.asarray(halves(x_forward_table(planes), 0)),
        jnp.asarray(halves(x_back_table(planes), 1)),
        bypass_weight,
        mlp_in.T,
        mlp_out,
        decode_weight,
    )

    blocks = back.reshape(devices, part, 2 * share)
    blocks = lax.all_to_all(blocks, "gx", 0, 0, tiled=True)
    blocks = blocks.reshape(KY, shares, part, 2, share).transpose(0, 2, 3, 1, 4)
    lines = blocks.reshape(KY * part, 2 * HALF)

    tables = np.concatenate([y_back_table(), z_back_table(planes * NY * NZ)], axis=0)
    tables = jnp.asarray(tables)

    def network(first, count):
        side = jax.ShapeDtypeStruct((3, count, LANES), F32)
        smem = pl.BlockSpec(memory_space=pltpu.SMEM)
        return pl.pallas_call(
            functools.partial(point_kernel, first=first),
            in_specs=[whole()] * 7 + [smem] + [whole()] * 2,
            out_specs=[whole()] * 3,
            out_shape=[side, side, jax.ShapeDtypeStruct((count, LANES), F32)],
            scratch_shapes=[pltpu.VMEM((count * SUB, TILES * LANES), F32)],
            compiler_params=params(),
            cost_estimate=pl.CostEstimate(
                flops=count * LANES * 400000, bytes_accessed=count * LANES * 200, transcendentals=0
            ),
            name="point_network",
        )(
            lines,
            values,
            *wide,
            zone,
            opened,
            perm_table,
            tables,
            jnp.asarray(turn_back_table()),
        )

    far = [(i, i + 1) for i in range(1, devices - 1, 2)]
    far = far + [(b, a) for a, b in far]
    near_by = [(i, i + 1) for i in range(0, devices, 2)]
    near_by = near_by + [(b, a) for a, b in near_by]
    *first, first_filled = network(0, ROWS - QUARTER)
    first_other = [lax.ppermute(first[1], "gx", far), lax.ppermute(first[0], "gx", near_by)]
    *last, last_filled = network(ROWS - QUARTER, QUARTER)
    last_other = [lax.ppermute(last[1], "gx", far), lax.ppermute(last[0], "gx", near_by)]
    fields, partial = pl.pallas_call(
        inner_kernel,
        in_specs=[whole()] * 6 + [pl.BlockSpec(memory_space=pltpu.SMEM)],
        out_specs=[whole()] * 2,
        out_shape=[
            jax.ShapeDtypeStruct((2, ROWS, LANES), F32),
            jax.ShapeDtypeStruct((ROWS, LANES), F32),
        ],
        compiler_params=params(),
        name="faces_in_plane",
    )(first[0], last[0], first_filled, last_filled, zone, opened, perm_table)
    residual = pl.pallas_call(
        outer_kernel,
        in_specs=[whole()] * 9,
        out_specs=whole(),
        out_shape=jax.ShapeDtypeStruct((ROWS, LANES), F32),
        compiler_params=params(),
        name="faces_between_planes",
    )(partial, *first, *first_other, *last, *last_other)
    return (fields.reshape(2, 1, cells), residual.reshape(1, cells))


def solution(mesh):
    in_specs = (
        P(None, ("groups", "gx"), None),
        P(None, ("groups", "gx")),
        P(None, None, None, "gx"),
        P(),
        P(),
        P(),
        P(),
        P(("groups", "gx"), None),
        P(None, ("groups", "gx"), None),
        P(),
    )
    out_specs = (P(None, ("groups", "gx"), None), P(("groups", "gx"), None))
    return jax.shard_map(body, mesh=mesh, in_specs=in_specs, out_specs=out_specs, check_vma=False)
```

```python
import functools
import math

import jax
import jax.numpy as jnp
import ml_dtypes
import numpy as np
from jax import lax
from jax.experimental import pallas as pl
from jax.experimental.pallas import tpu as pltpu
from jax.sharding import PartitionSpec as P

NY = 512
NZ = 64
KX = 32
KY = 32
KZ = 8
ZONES = 8
LANES = 128
SUB = 8
PAIRS = LANES // NZ
ROWS = NY // PAIRS
TILES = 4
TWO = 2
HALF = KZ * 2 * TILES
QUARTER = ROWS // 4
FOLD = KY // 2
CLASSES = (
    list(range(1, FOLD + 1, 2)),
    list(range(0, FOLD + 1, 4)),
    list(range(2, FOLD + 1, 4)),
)
GELU_A = math.sqrt(2.0 / math.pi)
GELU_B = GELU_A * 0.044715
F32 = jnp.float32
BF16 = jnp.bfloat16


def signed(count):
    steps = np.arange(count)
    return np.where(steps < count // 2, steps, steps - count)


def angles(freqs, positions, length):
    return 2.0 * np.pi * ((freqs[:, None] * positions[None, :]) % length) / length


def halves(table, axis):
    high = np.asarray(table, np.float64).astype(ml_dtypes.bfloat16)
    low = (table - high.astype(np.float64)).astype(ml_dtypes.bfloat16)
    return np.concatenate([high, low], axis=axis)


def spread(small):
    return np.kron(small, np.eye(SUB))


def z_forward_table():
    angle = angles(np.arange(KZ), np.arange(NZ), NZ)
    table = np.zeros((TWO, PAIRS, NZ, 2, KZ, PAIRS, 2, TWO))
    for t in range(TWO):
        for p in range(PAIRS):
            table[t, p, :, 0, :, p, 0, t] = np.cos(angle).T
            table[t, p, :, 0, :, p, 1, t] = -np.sin(angle).T
            table[t, p, :, 1, :, p, 0, t] = -np.sin(angle).T
            table[t, p, :, 1, :, p, 1, t] = -np.cos(angle).T
    return halves(table.reshape(TWO * LANES, LANES), 1)


def y_forward_table():
    angle = angles(np.arange(FOLD + 1), np.arange(QUARTER) * PAIRS, NY)
    parts = []
    for group in CLASSES:
        parts += [np.cos(angle[group]), np.sin(angle[[k for k in group if k]])]
    return halves(spread(np.concatenate(parts, axis=0)), 1)


def turn_forward_table():
    parity = angles(np.arange(FOLD + 1), np.arange(PAIRS), NY)
    parity = np.tile(np.repeat(parity, 2 * TWO, axis=1), (1, 2 * KZ))
    return np.stack([np.cos(parity), np.sin(parity)]).astype(np.float32)


def turn_back_table():
    parity = np.repeat(angles(signed(KY), np.array([1]), NY), LANES, axis=1)
    return np.stack([np.cos(parity), np.sin(parity)]).astype(np.float32)


def x_forward_table(planes):
    angle = angles(signed(KX), np.arange(planes), planes)

    def one(small):
        wide = np.zeros((2, planes, SUB // 2, SUB, KX))
        for s in range(SUB):
            wide[s // (SUB // 2), :, s % (SUB // 2), s, :] = small.T
        return wide.reshape(planes * SUB, SUB * KX)

    return np.concatenate([one(np.cos(angle)), one(np.sin(angle))], axis=0)


def x_back_table(planes):
    table = x_forward_table(planes).reshape(2, planes * SUB, SUB * KX)
    return np.concatenate([table[0], table[1]], axis=1)


def y_back_table():
    angle = angles(np.arange(1, FOLD + 1), np.arange(QUARTER) * PAIRS, NY)
    return halves(np.concatenate([spread(np.cos(angle).T), spread(np.sin(angle).T)], axis=1), 1)


def z_back_table(total):
    angle = angles(np.arange(KZ), np.arange(NZ), NZ)
    weight = np.where(np.arange(KZ) == 0, 1.0, 2.0)[:, None] / total
    table = np.zeros((PAIRS, KZ, TILES // TWO, 2, TWO, TILES, PAIRS, NZ))
    for t in range(TILES):
        for p in range(PAIRS):
            table[p, :, t // TWO, 0, t % TWO, t, p, :] = weight * np.cos(angle)
            table[p, :, t // TWO, 1, t % TWO, t, p, :] = -weight * np.sin(angle)
    return halves(table.reshape(PAIRS * HALF, TILES * LANES), 0)


def dot(a, b, dims=((1,), (0,)), precision=None):
    return lax.dot_general(a, b, (dims, ((), ())), precision=precision, preferred_element_type=F32)


def split(x):
    high = x.astype(BF16)
    return high, (x - high.astype(F32)).astype(BF16)


def column(row):
    n = row.shape[1]
    square = lax.broadcasted_iota(jnp.int32, (n, n), 0) == lax.broadcasted_iota(jnp.int32, (n, n), 1)
    return jnp.sum(jnp.where(square, row, 0.0), axis=1, keepdims=True)


def tall(table, first, count):
    return jnp.concatenate(
        [jnp.broadcast_to(table[k : k + 1], (SUB, LANES)) for k in range(first, first + count)],
        axis=0,
    )


def twice(x):
    return jnp.concatenate([x, x], axis=1)


def quarters(real, imag, turns):
    return ((real, imag), (-imag, real), (-real, -imag), (imag, -real))[turns % 4]


def forward_kernel(
    features, scale, table_z, table_y, turns, lines, values, held, factor, own_z, own_y, own_turns, done
):
    span = QUARTER * LANES
    chunks = features.shape[1] // span
    loads = [(scale, factor), (table_z, own_z), (table_y, own_y), (turns, own_turns)]
    loads += [(features.at[:, span * m : span * (m + 1)], held.at[m]) for m in range(chunks)]
    loads = [pltpu.make_async_copy(*pair, done.at[k]) for k, pair in enumerate(loads)]
    for load in loads:
        load.start()

    n = (FOLD + 1) * SUB
    def along_z(m):
        scaled = held[m].astype(F32) * gain
        values[:, span * m : span * (m + 1)] = scaled.astype(BF16)

        def tile(t, j):
            return scaled[SUB * t : SUB * (t + 1), LANES * j : LANES * (j + 1)]

        cells = jnp.concatenate(
            [
                jnp.concatenate([tile(t, j), tile(t + 1, j)], axis=1)
                for t in range(0, TILES, TWO)
                for j in range(QUARTER)
            ],
            axis=0,
        ).astype(BF16)
        part = dot(cells, own_z[...])
        part = part[:, :LANES] + part[:, LANES:]
        return jnp.concatenate([part[: SUB * QUARTER], part[SUB * QUARTER :]], axis=1)

    def along_y(place, group, x):
        table = own_y[SUB * place : SUB * (place + 2 * len(group) - (0 in group))]
        inner = table.shape[1] // 2
        high, low = split(x)
        sums = dot(
            jnp.concatenate([table[:, :inner], table], axis=1),
            jnp.concatenate([low, high, high], axis=0),
        )
        tiles = [sums[SUB * k : SUB * (k + 1)] for k in range(sums.shape[0] // SUB)]
        cosines, sines = tiles[: len(group)], tiles[len(group) :]
        return cosines, ([jnp.zeros_like(tiles[0])] if 0 in group else []) + sines

    for load in loads:
        load.wait()
    gain = column(factor[...])
    q = [along_z(m) for m in range(chunks)]
    sums, differences = [q[0] + q[2], q[1] + q[3]], [q[0] - q[2], q[1] - q[3]]
    even, odd = [None] * (FOLD + 1), [None] * (FOLD + 1)
    place = 0
    for group in CLASSES:
        if group[0] % 2:
            cosines, sines = along_y(place, group, jnp.concatenate(differences, axis=1))
            half = cosines[0].shape[1] // 2
            for k, c, s in zip(group, cosines, sines):
                sign = 1.0 if k % 4 == 1 else -1.0
                even[k] = c[:, :half] - sign * s[:, half:]
                odd[k] = s[:, :half] + sign * c[:, half:]
        else:
            x = sums[0] + sums[1] if group[0] % 4 == 0 else sums[0] - sums[1]
            for k, c, s in zip(group, *along_y(place, group, x)):
                even[k], odd[k] = c, s
        place += 2 * len(group) - (0 in group)

    first, second = jnp.concatenate(even, axis=0), jnp.concatenate(odd, axis=0)
    cosine = twice(tall(own_turns[0], 0, FOLD + 1))
    sine = twice(tall(own_turns[1], 0, FOLD + 1))
    even = cosine * first - sine * second
    odd = sine * first + cosine * second
    lane = lax.broadcasted_iota(jnp.int32, (n, LANES), 1)
    own = (lane & (2 * TWO)) == 0

    def packed(sign):
        sides = []
        for k in range(2):
            at = slice(LANES * k, LANES * (k + 1))
            line = even[:, at] + sign * pltpu.roll(odd[:, at], HALF, 1)
            shift = LANES - 2 * TWO if k == 0 else 2 * TWO
            sides.append(line + pltpu.roll(line, shift, 1))
        line = jnp.where(own, sides[0], sides[1])
        raised = pltpu.roll(pltpu.roll(line, HALF, 1), n - SUB // 2, 0)
        return jnp.where(lane < HALF, line, raised)

    up, down = packed(1.0), packed(-1.0)
    for k in range(FOLD):
        lines[SUB // 2 * k : SUB // 2 * (k + 1)] = up[SUB * k : SUB * k + SUB // 2]
    for k in range(FOLD, 0, -1):
        at = (KY - k) * SUB // 2
        lines[at : at + SUB // 2] = down[SUB * k : SUB * k + SUB // 2]


def swap_blocks(pieces):
    lane = lax.broadcasted_iota(jnp.int32, pieces[0].shape, 1) // KX
    out = []
    for e in range(4):
        got = None
        for b in range(4):
            moved = pieces[b] if b == e else pltpu.roll(pieces[b], (KX * (b - e)) % LANES, 1)
            got = moved if got is None else jnp.where(lane == b, moved, got)
        out.append(got)
    return out


def diagonal(block):
    width = block.shape[1]
    wide = (1, SUB * width)
    if width % LANES:
        row = lax.broadcasted_iota(jnp.int32, (width, SUB * width), 0)
        lane = lax.broadcasted_iota(jnp.int32, (width, SUB * width), 1)
        spread_out = (lax.rem(lane, width) == row).astype(F32).astype(BF16)
        block = dot(block, spread_out)
    else:
        block = jnp.concatenate([block.astype(F32)] * SUB, axis=1)
    lane = lax.broadcasted_iota(jnp.int32, wide, 1)
    return jnp.concatenate(
        [
            jnp.where((lane >= width * g) & (lane < width * (g + 1)), block, 0.0).astype(BF16)
            for g in range(SUB)
        ],
        axis=0,
    )


def turned_by_i(x, axis):
    size = x.shape[axis]
    place = lax.broadcasted_iota(jnp.int32, x.shape, axis)
    after = pltpu.roll(x, size - TWO, axis)
    before = pltpu.roll(x, TWO, axis)
    return jnp.where((place & TWO) == 0, -after, before)


def mix_kernel(
    lines,
    weight,
    table_x,
    table_back,
    bypass,
    mlp_in_t,
    mlp_out,
    decode,
    back,
    wide_bypass,
    wide_in,
    wide_out,
    modes,
    mixed,
):
    wide_bypass[...] = diagonal(bypass[...])
    inner = 0.5 * mlp_in_t[...].astype(F32)
    count = wide_out.shape[1]
    wide_in[:count] = diagonal(inner.T.astype(BF16))
    heads = 0.5 * dot(decode[...], mlp_out[...])
    through = dot(heads, inner, ((1,), (1,)), precision=lax.Precision.HIGHEST)
    def rows_of(x):
        rows = [part[k : k + 1] for part in split(x) for k in range(2)]
        return jnp.concatenate([diagonal(row).astype(F32) for row in rows], axis=0).astype(BF16)

    wide_out[...] = rows_of(heads)
    wide_in[count:] = rows_of(through)

    half = lines.shape[1] // 2
    count = half // (2 * TILES)
    groups = count // 4
    flipped = lines[...].T
    straight = jnp.concatenate([flipped[:half], flipped[half:]], axis=1)
    pair = jnp.concatenate([straight, -turned_by_i(straight, 0)], axis=1)
    high, low = split(pair)
    table = table_x[...]
    inner = table.shape[0] // 2
    spectrum = dot(
        jnp.concatenate([low, high, high], axis=1),
        jnp.concatenate([table[:inner], table], axis=0),
    )
    for c in range(SUB // 4):
        for a in range(groups):
            got = swap_blocks(
                [
                    spectrum[SUB * (4 * a + b) : SUB * (4 * a + b + 1), LANES * c : LANES * (c + 1)]
                    for b in range(4)
                ]
            )
            for e in range(4):
                modes[4 * c + e, :, LANES * a : LANES * (a + 1)] = got[e]
    width = weight.shape[1]
    real = jnp.zeros((width, count * KX), F32)
    imag = jnp.zeros((width, count * KX), F32)
    for i in range(width):
        t, v = i // SUB, i % SUB
        at = t // TWO * 2 * TWO + t % TWO
        in_real = modes[v, at : at + 1, :]
        in_imag = modes[v, at + TWO : at + TWO + 1, :]
        w_real = weight[0, i].astype(F32)
        w_imag = weight[1, i].astype(F32)
        real += in_real * w_real - in_imag * w_imag
        imag += in_real * w_imag + in_imag * w_real
    for a in range(groups):
        for t in range(TILES):
            here = slice(SUB * t, SUB * (t + 1)), slice(LANES * a, LANES * (a + 1))
            at = (t // TWO * 2 * TWO + t % TWO) * SUB
            mixed[0, a, at : at + SUB] = real[here]
            mixed[1, a, at : at + SUB] = -imag[here]
            at += TWO * SUB
            mixed[0, a, at : at + SUB] = imag[here]
            mixed[1, a, at : at + SUB] = real[here]
    rows = []
    for k in range(2):
        seen = [
            [mixed[k, a, pl.ds(v, 2 * TILES, stride=SUB), :] for v in range(SUB)]
            for a in range(groups)
        ]
        parts = [[None] * (SUB // 4) for _ in range(count)]
        for c in range(SUB // 4):
            for a in range(groups):
                got = swap_blocks(seen[a][4 * c : 4 * c + 4])
                for b in range(4):
                    parts[4 * a + b][c] = got[b]
        rows.append(jnp.concatenate([jnp.concatenate(p, axis=1) for p in parts], axis=0))
    high, low = split(jnp.concatenate(rows, axis=1))
    table = table_back[...]
    inner = table.shape[1] // 2
    got = dot(
        jnp.concatenate([table[:, :inner], table], axis=1),
        jnp.concatenate([low, high, high], axis=1),
        ((1,), (1,)),
    )
    count = got.shape[0] // 2
    back[...] = jnp.concatenate([got[:count], got[count:]], axis=1)


def gelu_twice(x):
    return x + x * jnp.tanh(x * (GELU_A + GELU_B * (x * x)))


def point_kernel(
    lines,
    values,
    wide_bypass,
    wide_in,
    wide_out,
    zone,
    opened,
    perm_table,
    tables,
    turns,
    near_side,
    far_side,
    filled,
    smooth,
    first,
):
    rows = near_side.shape[1]
    sent = lines[...]
    rolled = pltpu.roll(sent, HALF, 1)
    top = lax.broadcasted_iota(jnp.int32, sent.shape, 0) % SUB < SUB // 2
    of_even = jnp.where(top, sent, pltpu.roll(rolled, SUB // 2, 0))
    of_odd = jnp.where(top, pltpu.roll(sent, sent.shape[0] - SUB // 2, 0), rolled)
    held = jnp.concatenate(
        [x[SUB * k : SUB * (k + 1)] for k in range(KY // 2) for x in (of_even, of_odd)], axis=0
    )
    low_half = lax.broadcasted_iota(jnp.int32, held.shape, 1) < HALF
    held = jnp.where(low_half, held, pltpu.roll(held, HALF, 1))
    other = turned_by_i(held, 1)
    cosine, sine = tall(turns[0], 0, KY), tall(turns[1], 0, KY)
    straight = jnp.where(low_half, held, cosine * held + sine * other)
    turned = jnp.where(low_half, other, cosine * other - sine * held)

    def at(x, k):
        return x[SUB * k : SUB * (k + 1)]

    even = [at(straight, k) + at(straight, KY - k) for k in range(1, FOLD)]
    odd = [at(turned, k) - at(turned, KY - k) for k in range(1, FOLD)]
    even.append(at(straight, FOLD))
    odd.append(-at(turned, FOLD))
    level = jnp.concatenate([at(straight, 0)] * QUARTER, axis=0)
    count = QUARTER * SUB
    table = jnp.concatenate([tables[count : count + LANES], tables[count:]], axis=0)
    for m in range(rows // QUARTER):
        sides = [
            quarters(real, -imag, (first // QUARTER + m) * k)
            for k, (real, imag) in enumerate(zip(even, odd), 1)
        ]
        sides = [real for real, _ in sides] + [-imag for _, imag in sides]
        sides = jnp.concatenate(split(jnp.concatenate(sides, axis=0)), axis=1)
        both = dot(tables[:count], jnp.concatenate([sides, sides], axis=0))
        high, low = split(both[:, :LANES] + both[:, LANES:] + level)
        smooth[QUARTER * SUB * m : QUARTER * SUB * (m + 1)] = dot(
            jnp.concatenate([low, high, high], axis=1), table
        )

    groups = rows // SUB

    def grouped(tile):
        return jnp.concatenate(
            [
                jnp.concatenate([tile(SUB * a + g) for a in range(groups)], axis=1)
                for g in range(SUB)
            ],
            axis=0,
        )

    own = grouped(lambda j: values[:, LANES * (first + j) : LANES * (first + j + 1)])
    spectral = grouped(
        lambda j: jnp.concatenate(
            [
                smooth[SUB * j : SUB * (j + 1), LANES * t : LANES * (t + 1)]
                for t in range(TILES)
            ],
            axis=0,
        )
    )
    lifted = gelu_twice(spectral + dot(wide_bypass[...], own)).astype(BF16)
    inner = dot(wide_in[...], lifted)
    count = wide_out.shape[1]
    decoded = dot(wide_out[...], curved(inner[:count])) + inner[count:]
    decoded = decoded[: 2 * SUB] + decoded[2 * SUB :]
    even_plane = lax.axis_index("gx") % 2 == 0
    for a in range(rows // SUB):
        pressure = decoded[:SUB, LANES * a : LANES * (a + 1)]
        saturation = jax.nn.sigmoid(decoded[SUB:, LANES * a : LANES * (a + 1)])
        square = saturation * saturation
        rest = 1.0 - saturation
        at = slice(SUB * a, SUB * (a + 1))
        here = slice(first + SUB * a, first + SUB * (a + 1))
        filled[at] = saturation
        mobility = square / (square + 0.5 * rest * rest)
        perm = lookup(zone[here], perm_table)
        gated = perm * opened[0, here].astype(F32)
        near_side[0, at] = pressure
        near_side[1, at] = mobility
        near_side[2, at] = jnp.where(even_plane, gated, perm)
        far_side[0, at] = pressure
        far_side[1, at] = mobility
        far_side[2, at] = jnp.where(even_plane, perm, gated)


def lookup(zones, perm_table):
    perm = jnp.zeros(zones.shape, F32)
    for k in range(ZONES):
        perm = jnp.where(zones == k, perm_table[k], perm)
    return perm


def curved(x):
    x = x.astype(BF16)
    return x * jnp.tanh(x * (BF16(GELU_A) + BF16(GELU_B) * (x * x)))


def joined(first, second):
    both = first + second
    return jnp.where(both > 0.0, first * second / jnp.where(both > 0.0, both, 1.0), 0.0)


def ahead_y(field):
    rolled = pltpu.roll(field, NZ, 1)
    lane = lax.broadcasted_iota(jnp.int32, field.shape, 1)
    row = lax.broadcasted_iota(jnp.int32, field.shape, 0)
    below = pltpu.roll(rolled, field.shape[0] - 1, 0)
    below = jnp.where(row == field.shape[0] - 1, 0.0, below)
    return jnp.where(lane < LANES - NZ, rolled, below)


def behind_y(field):
    rolled = pltpu.roll(field, NZ, 1)
    lane = lax.broadcasted_iota(jnp.int32, field.shape, 1)
    row = lax.broadcasted_iota(jnp.int32, field.shape, 0)
    above = pltpu.roll(rolled, 1, 0)
    above = jnp.where(row == 0, 0.0, above)
    return jnp.where(lane >= NZ, rolled, above)


def ahead_z(field):
    lane = lax.broadcasted_iota(jnp.int32, field.shape, 1)
    return jnp.where(lane % NZ == NZ - 1, 0.0, pltpu.roll(field, LANES - 1, 1))


def behind_z(field):
    lane = lax.broadcasted_iota(jnp.int32, field.shape, 1)
    return jnp.where(lane % NZ == 0, 0.0, pltpu.roll(field, 1, 1))


def inner_kernel(
    first, last, first_filled, last_filled, zone, opened, perm_table, fields, partial
):
    pressure, mobility = [jnp.concatenate([first[k], last[k]], axis=0) for k in range(2)]
    fields[0] = pressure
    fields[1] = jnp.concatenate([first_filled[...], last_filled[...]], axis=0)
    perm = lookup(zone[...], perm_table)
    residual = jnp.zeros(pressure.shape, F32)
    for axis, ahead, behind in ((1, ahead_y, behind_y), (2, ahead_z, behind_z)):
        link = opened[axis].astype(F32) * joined(perm, ahead(perm))
        flux = link * (mobility + ahead(mobility)) * (pressure - ahead(pressure))
        residual = residual + (flux - behind(flux))
    partial[...] = residual


def outer_kernel(partial, *refs):
    residual = refs[-1]

    def flow(mine, other):
        link = joined(mine[2], other[2])
        return link * (mine[1] + other[1]) * (mine[0] - other[0])

    cut = refs[0].shape[1]
    for at, sides in ((slice(0, cut), refs[:4]), (slice(cut, ROWS), refs[4:8])):
        residual[at] = partial[at] + flow(sides[0], sides[3]) + flow(sides[1], sides[2])


def near(x):
    return pltpu.with_memory_space_constraint(x, pltpu.HBM)


def whole():
    return pl.BlockSpec(memory_space=pltpu.VMEM)


def params():
    return pltpu.CompilerParams(vmem_limit_bytes=40 * 1024 * 1024)


def body(
    features,
    block_scale,
    spec_weight,
    bypass_weight,
    mlp_in,
    mlp_out,
    decode_weight,
    zone_ids,
    face_open,
    perm_table,
):
    width, rows, cells = features.shape
    devices = lax.axis_size("gx")
    planes = rows * devices
    assert rows == 1 and cells == ROWS * LANES and width == TILES * SUB and devices % 2 == 0
    plane = features.reshape(width, cells)
    scale = block_scale.reshape(1, width)
    zone = zone_ids.reshape(ROWS, LANES)
    opened = face_open.reshape(3, ROWS, LANES)
    shares = devices // KY
    held = KZ // shares

    span = QUARTER * LANES
    chunks = cells // span
    table_z, table_y, turns = z_forward_table(), y_forward_table(), turn_forward_table()
    lines, values = pl.pallas_call(
        forward_kernel,
        in_specs=[pl.BlockSpec(memory_space=pl.ANY)] * 5,
        out_specs=[whole()] * 2,
        out_shape=[
            jax.ShapeDtypeStruct((KY * SUB // 2, LANES), F32),
            jax.ShapeDtypeStruct((width, cells), BF16),
        ],
        scratch_shapes=[
            pltpu.VMEM((chunks, width, span), BF16),
            pltpu.VMEM((1, width), F32),
            pltpu.VMEM(table_z.shape, BF16),
            pltpu.VMEM(table_y.shape, BF16),
            pltpu.VMEM(turns.shape, F32),
            pltpu.SemaphoreType.DMA((4 + chunks,)),
        ],
        compiler_params=params(),
        name="forward_yz",
    )(*map(near, (plane, scale, jnp.asarray(table_z), jnp.asarray(table_y), jnp.asarray(turns))))

    part = SUB // 2
    share = held * 2 * TILES
    blocks = lines.reshape(KY, part, 2, shares, share)
    blocks = blocks.transpose(0, 3, 1, 2, 4).reshape(devices, part, 2 * share)
    blocks = lax.all_to_all(blocks, "gx", 0, 0, tiled=True)
    lines = blocks.reshape(planes * part, 2 * share)

    modes = spec_weight.shape[3]
    hidden = mlp_in.shape[0]
    back, *wide = pl.pallas_call(
        mix_kernel,
        in_specs=[whole()] * 8,
        out_specs=[whole()] * 4,
        out_shape=[
            jax.ShapeDtypeStruct((planes * part, 2 * share), F32),
            jax.ShapeDtypeStruct((SUB * width, SUB * width), BF16),
            jax.ShapeDtypeStruct((SUB * hidden + 4 * SUB, SUB * width), BF16),
            jax.ShapeDtypeStruct((4 * SUB, SUB * hidden), BF16),
        ],
        scratch_shapes=[
            pltpu.VMEM((SUB, 2 * TILES, modes), F32),
            pltpu.VMEM((2, modes // LANES, 2 * width, LANES), F32),
        ],
        compiler_params=params(),
        name="mix_modes",
    )(
        lines,
        spec_weight,
        jnp.asarray(halves(x_forward_table(planes), 0)),
        jnp.asarray(halves(x_back_table(planes), 1)),
        bypass_weight,
        mlp_in.T,
        mlp_out,
        decode_weight,
    )

    blocks = back.reshape(devices, part, 2 * share)
    blocks = lax.all_to_all(blocks, "gx", 0, 0, tiled=True)
    blocks = blocks.reshape(KY, shares, part, 2, share).transpose(0, 2, 3, 1, 4)
    lines = blocks.reshape(KY * part, 2 * HALF)

    tables = np.concatenate([y_back_table(), z_back_table(planes * NY * NZ)], axis=0)
    tables = jnp.asarray(tables)

    def network(first, count):
        side = jax.ShapeDtypeStruct((3, count, LANES), F32)
        smem = pl.BlockSpec(memory_space=pltpu.SMEM)
        return pl.pallas_call(
            functools.partial(point_kernel, first=first),
            in_specs=[whole()] * 7 + [smem] + [whole()] * 2,
            out_specs=[whole()] * 3,
            out_shape=[side, side, jax.ShapeDtypeStruct((count, LANES), F32)],
            scratch_shapes=[pltpu.VMEM((count * SUB, TILES * LANES), F32)],
            compiler_params=params(),
            cost_estimate=pl.CostEstimate(
                flops=count * LANES * 400000, bytes_accessed=count * LANES * 200, transcendentals=0
            ),
            name="point_network",
        )(
            lines,
            values,
            *wide,
            zone,
            opened,
            perm_table,
            tables,
            jnp.asarray(turn_back_table()),
        )

    far = [(i, i + 1) for i in range(1, devices - 1, 2)]
    far = far + [(b, a) for a, b in far]
    near_by = [(i, i + 1) for i in range(0, devices, 2)]
    near_by = near_by + [(b, a) for a, b in near_by]
    *first, first_filled = network(0, ROWS - QUARTER)
    first_other = [lax.ppermute(first[1], "gx", far), lax.ppermute(first[0], "gx", near_by)]
    *last, last_filled = network(ROWS - QUARTER, QUARTER)
    last_other = [lax.ppermute(last[1], "gx", far), lax.ppermute(last[0], "gx", near_by)]
    fields, partial = pl.pallas_call(
        inner_kernel,
        in_specs=[whole()] * 6 + [pl.BlockSpec(memory_space=pltpu.SMEM)],
        out_specs=[whole()] * 2,
        out_shape=[
            jax.ShapeDtypeStruct((2, ROWS, LANES), F32),
            jax.ShapeDtypeStruct((ROWS, LANES), F32),
        ],
        compiler_params=params(),
        name="faces_in_plane",
    )(first[0], last[0], first_filled, last_filled, zone, opened, perm_table)
    residual = pl.pallas_call(
        outer_kernel,
        in_specs=[whole()] * 9,
        out_specs=whole(),
        out_shape=jax.ShapeDtypeStruct((ROWS, LANES), F32),
        compiler_params=params(),
        name="faces_between_planes",
    )(partial, *first, *first_other, *last, *last_other)
    return (fields.reshape(2, 1, cells), residual.reshape(1, cells))


def solution(mesh):
    in_specs = (
        P(None, ("groups", "gx"), None),
        P(None, ("groups", "gx")),
        P(None, None, None, "gx"),
        P(),
        P(),
        P(),
        P(),
        P(("groups", "gx"), None),
        P(None, ("groups", "gx"), None),
        P(),
    )
    out_specs = (P(None, ("groups", "gx"), None), P(("groups", "gx"), None))
    return jax.shard_map(body, mesh=mesh, in_specs=in_specs, out_specs=out_specs, check_vma=False)
```

```python
import functools
import math

import jax
import jax.numpy as jnp
import ml_dtypes
import numpy as np
from jax import lax
from jax.experimental import pallas as pl
from jax.experimental.pallas import tpu as pltpu
from jax.sharding import PartitionSpec as P

NY = 512
NZ = 64
KX = 32
KY = 32
KZ = 8
ZONES = 8
LANES = 128
SUB = 8
PAIRS = LANES // NZ
ROWS = NY // PAIRS
TILES = 4
TWO = 2
HALF = KZ * 2 * TILES
QUARTER = ROWS // 4
FOLD = KY // 2
CLASSES = (
    list(range(1, FOLD + 1, 2)),
    list(range(0, FOLD + 1, 4)),
    list(range(2, FOLD + 1, 4)),
)
EVENS, ODDS = list(range(2, FOLD + 1, 2)), list(range(1, FOLD + 1, 2))
GELU_A = math.sqrt(2.0 / math.pi)
GELU_B = GELU_A * 0.044715
F32 = jnp.float32
BF16 = jnp.bfloat16


def signed(count):
    steps = np.arange(count)
    return np.where(steps < count // 2, steps, steps - count)


def angles(freqs, positions, length):
    return 2.0 * np.pi * ((freqs[:, None] * positions[None, :]) % length) / length


def halves(table, axis):
    high = np.asarray(table, np.float64).astype(ml_dtypes.bfloat16)
    low = (table - high.astype(np.float64)).astype(ml_dtypes.bfloat16)
    return np.concatenate([high, low], axis=axis)


def spread(small):
    return np.kron(small, np.eye(SUB))


def z_forward_table():
    angle = angles(np.arange(KZ), np.arange(NZ), NZ)
    table = np.zeros((TWO, PAIRS, NZ, 2, KZ, PAIRS, 2, TWO))
    for t in range(TWO):
        for p in range(PAIRS):
            table[t, p, :, 0, :, p, 0, t] = np.cos(angle).T
            table[t, p, :, 0, :, p, 1, t] = -np.sin(angle).T
            table[t, p, :, 1, :, p, 0, t] = -np.sin(angle).T
            table[t, p, :, 1, :, p, 1, t] = -np.cos(angle).T
    return halves(table.reshape(TWO * LANES, LANES), 1)


def y_forward_table():
    angle = angles(np.arange(FOLD + 1), np.arange(QUARTER) * PAIRS, NY)
    parts = []
    for group in CLASSES:
        parts += [np.cos(angle[group]), np.sin(angle[[k for k in group if k]])]
    return halves(spread(np.concatenate(parts, axis=0)), 1)


def turn_forward_table():
    parity = angles(np.arange(FOLD + 1), np.arange(PAIRS), NY)
    parity = np.tile(np.repeat(parity, 2 * TWO, axis=1), (1, 2 * KZ))
    return np.stack([np.cos(parity), np.sin(parity)]).astype(np.float32)


def turn_back_table():
    parity = np.repeat(angles(signed(KY), np.array([1]), NY), LANES, axis=1)
    return np.stack([np.cos(parity), np.sin(parity)]).astype(np.float32)


def x_forward_table(planes):
    angle = angles(signed(KX), np.arange(planes), planes)

    def one(small):
        wide = np.zeros((2, planes, SUB // 2, SUB, KX))
        for s in range(SUB):
            wide[s // (SUB // 2), :, s % (SUB // 2), s, :] = small.T
        return wide.reshape(planes * SUB, SUB * KX)

    return np.concatenate([one(np.cos(angle)), one(np.sin(angle))], axis=0)


def x_back_table(planes):
    table = x_forward_table(planes).reshape(2, planes * SUB, SUB * KX)
    return np.concatenate([table[0], table[1]], axis=1)


def y_back_table():
    sides = []
    for freqs in (EVENS, ODDS):
        angle = angles(np.array(freqs), np.arange(QUARTER) * PAIRS, NY)
        sides.append(halves(spread(np.concatenate([np.cos(angle).T, np.sin(angle).T], axis=1)), 1))
    return np.concatenate(sides, axis=1)


def z_back_table(total):
    angle = angles(np.arange(KZ), np.arange(NZ), NZ)
    weight = np.where(np.arange(KZ) == 0, 1.0, 2.0)[:, None] / total
    table = np.zeros((PAIRS, KZ, TILES // TWO, 2, TWO, TWO, PAIRS, NZ))
    for t in range(TWO):
        for p in range(PAIRS):
            table[p, :, :, 0, t, t, p, :] = (weight * np.cos(angle))[:, None]
            table[p, :, :, 1, t, t, p, :] = (-weight * np.sin(angle))[:, None]
    high, low = np.split(halves(table, 0), 2)
    blocks = [high, low.copy(), low.copy(), np.zeros_like(low)]
    blocks[1][:, :, 1] = 0
    blocks[2][:, :, 0] = 0
    blocks = [block.reshape(LANES, TWO * LANES) for block in blocks]
    return np.concatenate([np.concatenate(blocks[k : k + 2], axis=1) for k in (0, 2)], axis=0)


def dot(a, b, dims=((1,), (0,)), precision=None):
    return lax.dot_general(a, b, (dims, ((), ())), precision=precision, preferred_element_type=F32)


def split(x):
    high = x.astype(BF16)
    return high, (x - high.astype(F32)).astype(BF16)


def column(row):
    n = row.shape[1]
    square = lax.broadcasted_iota(jnp.int32, (n, n), 0) == lax.broadcasted_iota(jnp.int32, (n, n), 1)
    return jnp.sum(jnp.where(square, row, 0.0), axis=1, keepdims=True)


def tall(table, first, count):
    return jnp.concatenate(
        [jnp.broadcast_to(table[k : k + 1], (SUB, LANES)) for k in range(first, first + count)],
        axis=0,
    )


def twice(x):
    return jnp.concatenate([x, x], axis=1)


def quarters(real, imag, turns):
    return ((real, imag), (-imag, real), (-real, -imag), (imag, -real))[turns % 4]


def forward_kernel(
    features, scale, table_z, table_y, turns, lines, values, held, factor, own_z, own_y, own_turns, done
):
    span = QUARTER * LANES
    chunks = features.shape[1] // span
    loads = [(scale, factor), (table_z, own_z), (table_y, own_y), (turns, own_turns)]
    loads += [(features.at[:, span * m : span * (m + 1)], held.at[m]) for m in range(chunks)]
    loads = [pltpu.make_async_copy(*pair, done.at[k]) for k, pair in enumerate(loads)]
    for load in loads:
        load.start()

    n = (FOLD + 1) * SUB
    def along_z(m):
        scaled = held[m].astype(F32) * gain
        values[:, span * m : span * (m + 1)] = scaled.astype(BF16)

        def tile(t, j):
            return scaled[SUB * t : SUB * (t + 1), LANES * j : LANES * (j + 1)]

        cells = jnp.concatenate(
            [
                jnp.concatenate([tile(t, j), tile(t + 1, j)], axis=1)
                for t in range(0, TILES, TWO)
                for j in range(QUARTER)
            ],
            axis=0,
        ).astype(BF16)
        part = dot(cells, own_z[...])
        part = part[:, :LANES] + part[:, LANES:]
        return jnp.concatenate([part[: SUB * QUARTER], part[SUB * QUARTER :]], axis=1)

    def along_y(place, group, x):
        table = own_y[SUB * place : SUB * (place + 2 * len(group) - (0 in group))]
        inner = table.shape[1] // 2
        high, low = split(x)
        sums = dot(
            jnp.concatenate([table[:, :inner], table], axis=1),
            jnp.concatenate([low, high, high], axis=0),
        )
        tiles = [sums[SUB * k : SUB * (k + 1)] for k in range(sums.shape[0] // SUB)]
        cosines, sines = tiles[: len(group)], tiles[len(group) :]
        return cosines, ([jnp.zeros_like(tiles[0])] if 0 in group else []) + sines

    for load in loads:
        load.wait()
    gain = column(factor[...])
    q = [along_z(m) for m in range(chunks)]
    sums, differences = [q[0] + q[2], q[1] + q[3]], [q[0] - q[2], q[1] - q[3]]
    even, odd = [None] * (FOLD + 1), [None] * (FOLD + 1)
    place = 0
    for group in CLASSES:
        if group[0] % 2:
            cosines, sines = along_y(place, group, jnp.concatenate(differences, axis=1))
            half = cosines[0].shape[1] // 2
            for k, c, s in zip(group, cosines, sines):
                sign = 1.0 if k % 4 == 1 else -1.0
                even[k] = c[:, :half] - sign * s[:, half:]
                odd[k] = s[:, :half] + sign * c[:, half:]
        else:
            x = sums[0] + sums[1] if group[0] % 4 == 0 else sums[0] - sums[1]
            for k, c, s in zip(group, *along_y(place, group, x)):
                even[k], odd[k] = c, s
        place += 2 * len(group) - (0 in group)

    first, second = jnp.concatenate(even, axis=0), jnp.concatenate(odd, axis=0)
    cosine = twice(tall(own_turns[0], 0, FOLD + 1))
    sine = twice(tall(own_turns[1], 0, FOLD + 1))
    even = cosine * first - sine * second
    odd = sine * first + cosine * second
    lane = lax.broadcasted_iota(jnp.int32, (n, LANES), 1)
    own = (lane & (2 * TWO)) == 0

    def packed(sign):
        sides = []
        for k in range(2):
            at = slice(LANES * k, LANES * (k + 1))
            line = even[:, at] + sign * pltpu.roll(odd[:, at], HALF, 1)
            shift = LANES - 2 * TWO if k == 0 else 2 * TWO
            sides.append(line + pltpu.roll(line, shift, 1))
        line = jnp.where(own, sides[0], sides[1])
        raised = pltpu.roll(pltpu.roll(line, HALF, 1), n - SUB // 2, 0)
        return jnp.where(lane < HALF, line, raised)

    up, down = packed(1.0), packed(-1.0)
    for k in range(FOLD):
        lines[SUB // 2 * k : SUB // 2 * (k + 1)] = up[SUB * k : SUB * k + SUB // 2]
    for k in range(FOLD, 0, -1):
        at = (KY - k) * SUB // 2
        lines[at : at + SUB // 2] = down[SUB * k : SUB * k + SUB // 2]


def swap_blocks(pieces):
    lane = lax.broadcasted_iota(jnp.int32, pieces[0].shape, 1) // KX
    out = []
    for e in range(4):
        got = None
        for b in range(4):
            moved = pieces[b] if b == e else pltpu.roll(pieces[b], (KX * (b - e)) % LANES, 1)
            got = moved if got is None else jnp.where(lane == b, moved, got)
        out.append(got)
    return out


def diagonal(block):
    width = block.shape[1]
    wide = (1, SUB * width)
    if width % LANES:
        row = lax.broadcasted_iota(jnp.int32, (width, SUB * width), 0)
        lane = lax.broadcasted_iota(jnp.int32, (width, SUB * width), 1)
        spread_out = (lax.rem(lane, width) == row).astype(F32).astype(BF16)
        block = dot(block, spread_out)
    else:
        block = jnp.concatenate([block.astype(F32)] * SUB, axis=1)
    lane = lax.broadcasted_iota(jnp.int32, wide, 1)
    return jnp.concatenate(
        [
            jnp.where((lane >= width * g) & (lane < width * (g + 1)), block, 0.0).astype(BF16)
            for g in range(SUB)
        ],
        axis=0,
    )


def turned_by_i(x, axis):
    size = x.shape[axis]
    place = lax.broadcasted_iota(jnp.int32, x.shape, axis)
    after = pltpu.roll(x, size - TWO, axis)
    before = pltpu.roll(x, TWO, axis)
    return jnp.where((place & TWO) == 0, -after, before)


def mix_kernel(
    lines,
    weight,
    table_x,
    table_back,
    bypass,
    mlp_in_t,
    mlp_out,
    decode,
    back,
    wide_bypass,
    wide_in,
    wide_out,
    modes,
    mixed,
):
    wide_bypass[...] = diagonal(bypass[...])
    inner = 0.5 * mlp_in_t[...].astype(F32)
    count = wide_out.shape[1]
    wide_in[:count] = diagonal(inner.T.astype(BF16))
    heads = 0.5 * dot(decode[...], mlp_out[...])
    through = dot(heads, inner, ((1,), (1,)), precision=lax.Precision.HIGHEST)
    def rows_of(x):
        rows = [part[k : k + 1] for part in split(x) for k in range(2)]
        return jnp.concatenate([diagonal(row).astype(F32) for row in rows], axis=0).astype(BF16)

    wide_out[...] = rows_of(heads)
    wide_in[count:] = rows_of(through)

    half = lines.shape[1] // 2
    count = half // (2 * TILES)
    groups = count // 4
    flipped = lines[...].T
    straight = jnp.concatenate([flipped[:half], flipped[half:]], axis=1)
    pair = jnp.concatenate([straight, -turned_by_i(straight, 0)], axis=1)
    high, low = split(pair)
    table = table_x[...]
    inner = table.shape[0] // 2
    spectrum = dot(
        jnp.concatenate([low, high, high], axis=1),
        jnp.concatenate([table[:inner], table], axis=0),
    )
    for c in range(SUB // 4):
        for a in range(groups):
            got = swap_blocks(
                [
                    spectrum[SUB * (4 * a + b) : SUB * (4 * a + b + 1), LANES * c : LANES * (c + 1)]
                    for b in range(4)
                ]
            )
            for e in range(4):
                modes[4 * c + e, :, LANES * a : LANES * (a + 1)] = got[e]
    width = weight.shape[1]
    real = jnp.zeros((width, count * KX), F32)
    imag = jnp.zeros((width, count * KX), F32)
    for i in range(width):
        t, v = i // SUB, i % SUB
        at = t // TWO * 2 * TWO + t % TWO
        in_real = modes[v, at : at + 1, :]
        in_imag = modes[v, at + TWO : at + TWO + 1, :]
        w_real = weight[0, i].astype(F32)
        w_imag = weight[1, i].astype(F32)
        real += in_real * w_real - in_imag * w_imag
        imag += in_real * w_imag + in_imag * w_real
    for a in range(groups):
        for t in range(TILES):
            here = slice(SUB * t, SUB * (t + 1)), slice(LANES * a, LANES * (a + 1))
            at = (t // TWO * 2 * TWO + t % TWO) * SUB
            mixed[0, a, at : at + SUB] = real[here]
            mixed[1, a, at : at + SUB] = -imag[here]
            at += TWO * SUB
            mixed[0, a, at : at + SUB] = imag[here]
            mixed[1, a, at : at + SUB] = real[here]
    rows = []
    for k in range(2):
        seen = [
            [mixed[k, a, pl.ds(v, 2 * TILES, stride=SUB), :] for v in range(SUB)]
            for a in range(groups)
        ]
        parts = [[None] * (SUB // 4) for _ in range(count)]
        for c in range(SUB // 4):
            for a in range(groups):
                got = swap_blocks(seen[a][4 * c : 4 * c + 4])
                for b in range(4):
                    parts[4 * a + b][c] = got[b]
        rows.append(jnp.concatenate([jnp.concatenate(p, axis=1) for p in parts], axis=0))
    high, low = split(jnp.concatenate(rows, axis=1))
    table = table_back[...]
    inner = table.shape[1] // 2
    got = dot(
        jnp.concatenate([table[:, :inner], table], axis=1),
        jnp.concatenate([low, high, high], axis=1),
        ((1,), (1,)),
    )
    count = got.shape[0] // 2
    back[...] = jnp.concatenate([got[:count], got[count:]], axis=1)


def gelu_twice(x):
    return x + x * jnp.tanh(x * (GELU_A + GELU_B * (x * x)))


def point_kernel(
    lines,
    values,
    wide_bypass,
    wide_in,
    wide_out,
    zone,
    opened,
    perm_table,
    tables,
    turns,
    near_side,
    far_side,
    filled,
    smooth,
    first,
):
    rows = near_side.shape[1]
    sent = lines[...]
    rolled = pltpu.roll(sent, HALF, 1)
    top = lax.broadcasted_iota(jnp.int32, sent.shape, 0) % SUB < SUB // 2
    of_even = jnp.where(top, sent, pltpu.roll(rolled, SUB // 2, 0))
    of_odd = jnp.where(top, pltpu.roll(sent, sent.shape[0] - SUB // 2, 0), rolled)
    held = jnp.concatenate(
        [x[SUB * k : SUB * (k + 1)] for k in range(KY // 2) for x in (of_even, of_odd)], axis=0
    )
    low_half = lax.broadcasted_iota(jnp.int32, held.shape, 1) < HALF
    held = jnp.where(low_half, held, pltpu.roll(held, HALF, 1))
    other = turned_by_i(held, 1)
    cosine, sine = tall(turns[0], 0, KY), tall(turns[1], 0, KY)
    straight = jnp.where(low_half, held, cosine * held + sine * other)
    turned = jnp.where(low_half, other, cosine * other - sine * held)

    def at(x, k):
        return x[SUB * k : SUB * (k + 1)]

    even = [at(straight, k) + at(straight, KY - k) for k in range(1, FOLD)]
    odd = [at(turned, k) - at(turned, KY - k) for k in range(1, FOLD)]
    even.append(at(straight, FOLD))
    odd.append(-at(turned, FOLD))
    level = jnp.concatenate([at(straight, 0)] * QUARTER, axis=0)
    count = QUARTER * SUB
    quarter = first // QUARTER

    def along_y(freqs, place, turns_of):
        sides = [quarters(even[k - 1], -odd[k - 1], turns_of * k) for k in freqs]
        sides = [real for real, _ in sides] + [-imag for _, imag in sides]
        sides = jnp.concatenate(split(jnp.concatenate(sides, axis=0)), axis=1)
        both = dot(tables[:count, place : place + 2 * LANES], jnp.concatenate([sides] * 2, axis=0))
        return both[:, :LANES] + both[:, LANES:]

    wanted = sorted({(quarter + m) % 2 for m in range(rows // QUARTER)})
    even_sums = {m: along_y(EVENS, 0, m) + level for m in wanted}
    odd_sums = {m: along_y(ODDS, 2 * LANES, m) for m in wanted}
    high_table = tables[count : count + LANES, : 2 * LANES]
    low_tables = tables[count : count + LANES, 2 * LANES :], tables[count + LANES :, : 2 * LANES]
    lane = lax.broadcasted_iota(jnp.int32, (count, LANES), 1)
    second_pair = (lane & (2 * TWO)) != 0
    for m in range(rows // QUARTER):
        side = (quarter + m) % 2
        minus = (quarter + m) // 2 % 2
        gained = even_sums[side] - odd_sums[side] if minus else even_sums[side] + odd_sums[side]
        high = gained.astype(BF16)
        rounded = high.astype(F32)
        rest = gained - rounded
        for k, shift in enumerate((2 * TWO, LANES - 2 * TWO)):
            moved = pltpu.roll(rest, shift, 1)
            own = jnp.where(second_pair, *((rounded, moved) if k else (moved, rounded)))
            smooth[count * m : count * (m + 1), 2 * LANES * k : 2 * LANES * (k + 1)] = dot(
                jnp.concatenate([own.astype(BF16), high], axis=1),
                jnp.concatenate([high_table, low_tables[k]], axis=0),
            )

    groups = rows // SUB

    def grouped(tile):
        return jnp.concatenate(
            [
                jnp.concatenate([tile(SUB * a + g) for a in range(groups)], axis=1)
                for g in range(SUB)
            ],
            axis=0,
        )

    own = grouped(lambda j: values[:, LANES * (first + j) : LANES * (first + j + 1)])
    spectral = grouped(
        lambda j: jnp.concatenate(
            [
                smooth[SUB * j : SUB * (j + 1), LANES * t : LANES * (t + 1)]
                for t in range(TILES)
            ],
            axis=0,
        )
    )
    lifted = gelu_twice(spectral + dot(wide_bypass[...], own)).astype(BF16)
    inner = dot(wide_in[...], lifted)
    count = wide_out.shape[1]
    decoded = dot(wide_out[...], curved(inner[:count])) + inner[count:]
    decoded = decoded[: 2 * SUB] + decoded[2 * SUB :]
    even_plane = lax.axis_index("gx") % 2 == 0
    for a in range(rows // SUB):
        pressure = decoded[:SUB, LANES * a : LANES * (a + 1)]
        saturation = jax.nn.sigmoid(decoded[SUB:, LANES * a : LANES * (a + 1)])
        square = saturation * saturation
        rest = 1.0 - saturation
        at = slice(SUB * a, SUB * (a + 1))
        here = slice(first + SUB * a, first + SUB * (a + 1))
        filled[at] = saturation
        mobility = square / (square + 0.5 * rest * rest)
        perm = lookup(zone[here], perm_table)
        gated = perm * opened[0, here].astype(F32)
        near_side[0, at] = pressure
        near_side[1, at] = mobility
        near_side[2, at] = jnp.where(even_plane, gated, perm)
        far_side[0, at] = pressure
        far_side[1, at] = mobility
        far_side[2, at] = jnp.where(even_plane, perm, gated)


def lookup(zones, perm_table):
    perm = jnp.zeros(zones.shape, F32)
    for k in range(ZONES):
        perm = jnp.where(zones == k, perm_table[k], perm)
    return perm


def curved(x):
    x = x.astype(BF16)
    return x * jnp.tanh(x * (BF16(GELU_A) + BF16(GELU_B) * (x * x)))


def joined(first, second):
    both = first + second
    return jnp.where(both > 0.0, first * second / jnp.where(both > 0.0, both, 1.0), 0.0)


def ahead_y(field):
    rolled = pltpu.roll(field, NZ, 1)
    lane = lax.broadcasted_iota(jnp.int32, field.shape, 1)
    row = lax.broadcasted_iota(jnp.int32, field.shape, 0)
    below = pltpu.roll(rolled, field.shape[0] - 1, 0)
    below = jnp.where(row == field.shape[0] - 1, 0.0, below)
    return jnp.where(lane < LANES - NZ, rolled, below)


def behind_y(field):
    rolled = pltpu.roll(field, NZ, 1)
    lane = lax.broadcasted_iota(jnp.int32, field.shape, 1)
    row = lax.broadcasted_iota(jnp.int32, field.shape, 0)
    above = pltpu.roll(rolled, 1, 0)
    above = jnp.where(row == 0, 0.0, above)
    return jnp.where(lane >= NZ, rolled, above)


def ahead_z(field):
    lane = lax.broadcasted_iota(jnp.int32, field.shape, 1)
    return jnp.where(lane % NZ == NZ - 1, 0.0, pltpu.roll(field, LANES - 1, 1))


def behind_z(field):
    lane = lax.broadcasted_iota(jnp.int32, field.shape, 1)
    return jnp.where(lane % NZ == 0, 0.0, pltpu.roll(field, 1, 1))


def inner_kernel(
    first, last, first_filled, last_filled, zone, opened, perm_table, fields, partial
):
    pressure, mobility = [jnp.concatenate([first[k], last[k]], axis=0) for k in range(2)]
    fields[0] = pressure
    fields[1] = jnp.concatenate([first_filled[...], last_filled[...]], axis=0)
    perm = lookup(zone[...], perm_table)
    residual = jnp.zeros(pressure.shape, F32)
    for axis, ahead, behind in ((1, ahead_y, behind_y), (2, ahead_z, behind_z)):
        link = opened[axis].astype(F32) * joined(perm, ahead(perm))
        flux = link * (mobility + ahead(mobility)) * (pressure - ahead(pressure))
        residual = residual + (flux - behind(flux))
    partial[...] = residual


def outer_kernel(partial, *refs):
    residual = refs[-1]

    def flow(mine, other):
        link = joined(mine[2], other[2])
        return link * (mine[1] + other[1]) * (mine[0] - other[0])

    cut = refs[0].shape[1]
    for at, sides in ((slice(0, cut), refs[:4]), (slice(cut, ROWS), refs[4:8])):
        residual[at] = partial[at] + flow(sides[0], sides[3]) + flow(sides[1], sides[2])


def near(x):
    return pltpu.with_memory_space_constraint(x, pltpu.HBM)


def whole():
    return pl.BlockSpec(memory_space=pltpu.VMEM)


def params():
    return pltpu.CompilerParams(vmem_limit_bytes=40 * 1024 * 1024)


def body(
    features,
    block_scale,
    spec_weight,
    bypass_weight,
    mlp_in,
    mlp_out,
    decode_weight,
    zone_ids,
    face_open,
    perm_table,
):
    width, rows, cells = features.shape
    devices = lax.axis_size("gx")
    planes = rows * devices
    assert rows == 1 and cells == ROWS * LANES and width == TILES * SUB and devices % 2 == 0
    plane = features.reshape(width, cells)
    scale = block_scale.reshape(1, width)
    zone = zone_ids.reshape(ROWS, LANES)
    opened = face_open.reshape(3, ROWS, LANES)
    shares = devices // KY
    held = KZ // shares

    span = QUARTER * LANES
    chunks = cells // span
    table_z, table_y, turns = z_forward_table(), y_forward_table(), turn_forward_table()
    lines, values = pl.pallas_call(
        forward_kernel,
        in_specs=[pl.BlockSpec(memory_space=pl.ANY)] * 5,
        out_specs=[whole()] * 2,
        out_shape=[
            jax.ShapeDtypeStruct((KY * SUB // 2, LANES), F32),
            jax.ShapeDtypeStruct((width, cells), BF16),
        ],
        scratch_shapes=[
            pltpu.VMEM((chunks, width, span), BF16),
            pltpu.VMEM((1, width), F32),
            pltpu.VMEM(table_z.shape, BF16),
            pltpu.VMEM(table_y.shape, BF16),
            pltpu.VMEM(turns.shape, F32),
            pltpu.SemaphoreType.DMA((4 + chunks,)),
        ],
        compiler_params=params(),
        name="forward_yz",
    )(*map(near, (plane, scale, jnp.asarray(table_z), jnp.asarray(table_y), jnp.asarray(turns))))

    part = SUB // 2
    share = held * 2 * TILES
    blocks = lines.reshape(KY, part, 2, shares, share)
    blocks = blocks.transpose(0, 3, 1, 2, 4).reshape(devices, part, 2 * share)
    blocks = lax.all_to_all(blocks, "gx", 0, 0, tiled=True)
    lines = blocks.reshape(planes * part, 2 * share)

    modes = spec_weight.shape[3]
    hidden = mlp_in.shape[0]
    back, *wide = pl.pallas_call(
        mix_kernel,
        in_specs=[whole()] * 8,
        out_specs=[whole()] * 4,
        out_shape=[
            jax.ShapeDtypeStruct((planes * part, 2 * share), F32),
            jax.ShapeDtypeStruct((SUB * width, SUB * width), BF16),
            jax.ShapeDtypeStruct((SUB * hidden + 4 * SUB, SUB * width), BF16),
            jax.ShapeDtypeStruct((4 * SUB, SUB * hidden), BF16),
        ],
        scratch_shapes=[
            pltpu.VMEM((SUB, 2 * TILES, modes), F32),
            pltpu.VMEM((2, modes // LANES, 2 * width, LANES), F32),
        ],
        compiler_params=params(),
        name="mix_modes",
    )(
        lines,
        spec_weight,
        jnp.asarray(halves(x_forward_table(planes), 0)),
        jnp.asarray(halves(x_back_table(planes), 1)),
        bypass_weight,
        mlp_in.T,
        mlp_out,
        decode_weight,
    )

    blocks = back.reshape(devices, part, 2 * share)
    blocks = lax.all_to_all(blocks, "gx", 0, 0, tiled=True)
    blocks = blocks.reshape(KY, shares, part, 2, share).transpose(0, 2, 3, 1, 4)
    lines = blocks.reshape(KY * part, 2 * HALF)

    tables = np.concatenate([y_back_table(), z_back_table(planes * NY * NZ)], axis=0)
    tables = jnp.asarray(tables)

    def network(first, count):
        side = jax.ShapeDtypeStruct((3, count, LANES), F32)
        smem = pl.BlockSpec(memory_space=pltpu.SMEM)
        return pl.pallas_call(
            functools.partial(point_kernel, first=first),
            in_specs=[whole()] * 7 + [smem] + [whole()] * 2,
            out_specs=[whole()] * 3,
            out_shape=[side, side, jax.ShapeDtypeStruct((count, LANES), F32)],
            scratch_shapes=[pltpu.VMEM((count * SUB, TILES * LANES), F32)],
            compiler_params=params(),
            cost_estimate=pl.CostEstimate(
                flops=count * LANES * 400000, bytes_accessed=count * LANES * 200, transcendentals=0
            ),
            name="point_network",
        )(
            lines,
            values,
            *wide,
            zone,
            opened,
            perm_table,
            tables,
            jnp.asarray(turn_back_table()),
        )

    far = [(i, i + 1) for i in range(1, devices - 1, 2)]
    far = far + [(b, a) for a, b in far]
    near_by = [(i, i + 1) for i in range(0, devices, 2)]
    near_by = near_by + [(b, a) for a, b in near_by]
    *first, first_filled = network(0, ROWS - QUARTER)
    first_other = [lax.ppermute(first[1], "gx", far), lax.ppermute(first[0], "gx", near_by)]
    *last, last_filled = network(ROWS - QUARTER, QUARTER)
    last_other = [lax.ppermute(last[1], "gx", far), lax.ppermute(last[0], "gx", near_by)]
    fields, partial = pl.pallas_call(
        inner_kernel,
        in_specs=[whole()] * 6 + [pl.BlockSpec(memory_space=pltpu.SMEM)],
        out_specs=[whole()] * 2,
        out_shape=[
            jax.ShapeDtypeStruct((2, ROWS, LANES), F32),
            jax.ShapeDtypeStruct((ROWS, LANES), F32),
        ],
        compiler_params=params(),
        name="faces_in_plane",
    )(first[0], last[0], first_filled, last_filled, zone, opened, perm_table)
    residual = pl.pallas_call(
        outer_kernel,
        in_specs=[whole()] * 9,
        out_specs=whole(),
        out_shape=jax.ShapeDtypeStruct((ROWS, LANES), F32),
        compiler_params=params(),
        name="faces_between_planes",
    )(partial, *first, *first_other, *last, *last_other)
    return (fields.reshape(2, 1, cells), residual.reshape(1, cells))


def solution(mesh):
    in_specs = (
        P(None, ("groups", "gx"), None),
        P(None, ("groups", "gx")),
        P(None, None, None, "gx"),
        P(),
        P(),
        P(),
        P(),
        P(("groups", "gx"), None),
        P(None, ("groups", "gx"), None),
        P(),
    )
    out_specs = (P(None, ("groups", "gx"), None), P(("groups", "gx"), None))
    return jax.shard_map(body, mesh=mesh, in_specs=in_specs, out_specs=out_specs, check_vma=False)
```

```python
import functools
import math

import jax
import jax.numpy as jnp
import ml_dtypes
import numpy as np
from jax import lax
from jax.experimental import pallas as pl
from jax.experimental.pallas import tpu as pltpu
from jax.sharding import PartitionSpec as P

NY = 512
NZ = 64
KX = 32
KY = 32
KZ = 8
ZONES = 8
LANES = 128
SUB = 8
PAIRS = LANES // NZ
ROWS = NY // PAIRS
TILES = 4
TWO = 2
HALF = KZ * 2 * TILES
QUARTER = ROWS // 4
FOLD = KY // 2
CLASSES = (
    list(range(1, FOLD + 1, 2)),
    list(range(0, FOLD + 1, 4)),
    list(range(2, FOLD + 1, 4)),
)
EVENS, ODDS = list(range(2, FOLD + 1, 2)), list(range(1, FOLD + 1, 2))
GELU_A = math.sqrt(2.0 / math.pi)
GELU_B = GELU_A * 0.044715
F32 = jnp.float32
BF16 = jnp.bfloat16


def signed(count):
    steps = np.arange(count)
    return np.where(steps < count // 2, steps, steps - count)


def angles(freqs, positions, length):
    return 2.0 * np.pi * ((freqs[:, None] * positions[None, :]) % length) / length


def halves(table, axis):
    high = np.asarray(table, np.float64).astype(ml_dtypes.bfloat16)
    low = (table - high.astype(np.float64)).astype(ml_dtypes.bfloat16)
    return np.concatenate([high, low], axis=axis)


def spread(small):
    return np.kron(small, np.eye(SUB))


def z_forward_table():
    angle = angles(np.arange(KZ), np.arange(NZ), NZ)
    table = np.zeros((TWO, PAIRS, NZ, 2, KZ, PAIRS, 2, TWO))
    for t in range(TWO):
        for p in range(PAIRS):
            table[t, p, :, 0, :, p, 0, t] = np.cos(angle).T
            table[t, p, :, 0, :, p, 1, t] = -np.sin(angle).T
            table[t, p, :, 1, :, p, 0, t] = -np.sin(angle).T
            table[t, p, :, 1, :, p, 1, t] = -np.cos(angle).T
    return halves(table.reshape(TWO * LANES, LANES), 1)


def y_forward_table():
    angle = angles(np.arange(FOLD + 1), np.arange(QUARTER) * PAIRS, NY)
    parts = []
    for group in CLASSES:
        parts += [np.cos(angle[group]), np.sin(angle[[k for k in group if k]])]
    return halves(spread(np.concatenate(parts, axis=0)), 1)


def turn_forward_table():
    parity = angles(np.arange(FOLD + 1), np.arange(PAIRS), NY)
    parity = np.tile(np.repeat(parity, 2 * TWO, axis=1), (1, 2 * KZ))
    return np.stack([np.cos(parity), np.sin(parity)]).astype(np.float32)


def turn_back_table():
    parity = np.repeat(angles(signed(KY), np.array([1]), NY), LANES, axis=1)
    return np.stack([np.cos(parity), np.sin(parity)]).astype(np.float32)


def x_forward_table(planes):
    angle = angles(signed(KX), np.arange(planes), planes)

    def one(small):
        wide = np.zeros((2, planes, SUB // 2, SUB, KX))
        for s in range(SUB):
            wide[s // (SUB // 2), :, s % (SUB // 2), s, :] = small.T
        return wide.reshape(planes * SUB, SUB * KX)

    return np.concatenate([one(np.cos(angle)), one(np.sin(angle))], axis=0)


def x_back_table(planes):
    table = x_forward_table(planes).reshape(2, planes * SUB, SUB * KX)
    return np.concatenate([table[0], table[1]], axis=1)


def y_back_table():
    sides = []
    for freqs in (EVENS, ODDS):
        angle = angles(np.array(freqs), np.arange(QUARTER) * PAIRS, NY)
        sides.append(halves(spread(np.concatenate([np.cos(angle).T, np.sin(angle).T], axis=1)), 1))
    return np.concatenate(sides, axis=1)


def z_back_table(total):
    angle = angles(np.arange(KZ), np.arange(NZ), NZ)
    weight = np.where(np.arange(KZ) == 0, 1.0, 2.0)[:, None] / total
    table = np.zeros((PAIRS, KZ, TILES // TWO, 2, TWO, TWO, PAIRS, NZ))
    for t in range(TWO):
        for p in range(PAIRS):
            table[p, :, :, 0, t, t, p, :] = (weight * np.cos(angle))[:, None]
            table[p, :, :, 1, t, t, p, :] = (-weight * np.sin(angle))[:, None]
    high, low = np.split(halves(table, 0), 2)
    blocks = [high, low.copy(), low.copy(), np.zeros_like(low)]
    blocks[1][:, :, 1] = 0
    blocks[2][:, :, 0] = 0
    blocks = [block.reshape(LANES, TWO * LANES) for block in blocks]
    return np.concatenate([np.concatenate(blocks[k : k + 2], axis=1) for k in (0, 2)], axis=0)


def dot(a, b, dims=((1,), (0,)), precision=None):
    return lax.dot_general(a, b, (dims, ((), ())), precision=precision, preferred_element_type=F32)


def split(x):
    high = x.astype(BF16)
    return high, (x - high.astype(F32)).astype(BF16)


def column(row):
    n = row.shape[1]
    square = lax.broadcasted_iota(jnp.int32, (n, n), 0) == lax.broadcasted_iota(jnp.int32, (n, n), 1)
    return jnp.sum(jnp.where(square, row, 0.0), axis=1, keepdims=True)


def tall(table, first, count):
    return jnp.concatenate(
        [jnp.broadcast_to(table[k : k + 1], (SUB, LANES)) for k in range(first, first + count)],
        axis=0,
    )


def twice(x):
    return jnp.concatenate([x, x], axis=1)


def quarters(real, imag, turns):
    return ((real, imag), (-imag, real), (-real, -imag), (imag, -real))[turns % 4]


def forward_kernel(
    features, scale, table_z, table_y, turns, lines, values, held, factor, own_z, own_y, own_turns, done
):
    span = QUARTER * LANES
    chunks = features.shape[1] // span
    loads = [(scale, factor), (table_z, own_z), (table_y, own_y), (turns, own_turns)]
    loads += [(features.at[:, span * m : span * (m + 1)], held.at[m]) for m in range(chunks)]
    loads = [pltpu.make_async_copy(*pair, done.at[k]) for k, pair in enumerate(loads)]
    for load in loads:
        load.start()

    n = (FOLD + 1) * SUB
    def along_z(m):
        scaled = held[m].astype(F32) * gain
        values[:, span * m : span * (m + 1)] = scaled.astype(BF16)

        def tile(t, j):
            return scaled[SUB * t : SUB * (t + 1), LANES * j : LANES * (j + 1)]

        cells = jnp.concatenate(
            [
                jnp.concatenate([tile(t, j), tile(t + 1, j)], axis=1)
                for t in range(0, TILES, TWO)
                for j in range(QUARTER)
            ],
            axis=0,
        ).astype(BF16)
        part = dot(cells, own_z[...])
        part = part[:, :LANES] + part[:, LANES:]
        return jnp.concatenate([part[: SUB * QUARTER], part[SUB * QUARTER :]], axis=1)

    def along_y(place, group, x):
        table = own_y[SUB * place : SUB * (place + 2 * len(group) - (0 in group))]
        inner = table.shape[1] // 2
        high, low = split(x)
        sums = dot(
            jnp.concatenate([table[:, :inner], table], axis=1),
            jnp.concatenate([low, high, high], axis=0),
        )
        tiles = [sums[SUB * k : SUB * (k + 1)] for k in range(sums.shape[0] // SUB)]
        cosines, sines = tiles[: len(group)], tiles[len(group) :]
        return cosines, ([jnp.zeros_like(tiles[0])] if 0 in group else []) + sines

    for load in loads:
        load.wait()
    gain = column(factor[...])
    q = [along_z(m) for m in range(chunks)]
    sums, differences = [q[0] + q[2], q[1] + q[3]], [q[0] - q[2], q[1] - q[3]]
    even, odd = [None] * (FOLD + 1), [None] * (FOLD + 1)
    place = 0
    for group in CLASSES:
        if group[0] % 2:
            cosines, sines = along_y(place, group, jnp.concatenate(differences, axis=1))
            half = cosines[0].shape[1] // 2
            for k, c, s in zip(group, cosines, sines):
                sign = 1.0 if k % 4 == 1 else -1.0
                even[k] = c[:, :half] - sign * s[:, half:]
                odd[k] = s[:, :half] + sign * c[:, half:]
        else:
            x = sums[0] + sums[1] if group[0] % 4 == 0 else sums[0] - sums[1]
            for k, c, s in zip(group, *along_y(place, group, x)):
                even[k], odd[k] = c, s
        place += 2 * len(group) - (0 in group)

    first, second = jnp.concatenate(even, axis=0), jnp.concatenate(odd, axis=0)
    cosine = twice(tall(own_turns[0], 0, FOLD + 1))
    sine = twice(tall(own_turns[1], 0, FOLD + 1))
    even = cosine * first - sine * second
    odd = sine * first + cosine * second
    lane = lax.broadcasted_iota(jnp.int32, (n, LANES), 1)
    own = (lane & (2 * TWO)) == 0

    def packed(sign):
        sides = []
        for k in range(2):
            at = slice(LANES * k, LANES * (k + 1))
            line = even[:, at] + sign * pltpu.roll(odd[:, at], HALF, 1)
            shift = LANES - 2 * TWO if k == 0 else 2 * TWO
            sides.append(line + pltpu.roll(line, shift, 1))
        line = jnp.where(own, sides[0], sides[1])
        raised = pltpu.roll(pltpu.roll(line, HALF, 1), n - SUB // 2, 0)
        return jnp.where(lane < HALF, line, raised)

    up, down = packed(1.0), packed(-1.0)
    for k in range(FOLD):
        lines[SUB // 2 * k : SUB // 2 * (k + 1)] = up[SUB * k : SUB * k + SUB // 2]
    for k in range(FOLD, 0, -1):
        at = (KY - k) * SUB // 2
        lines[at : at + SUB // 2] = down[SUB * k : SUB * k + SUB // 2]


def swap_blocks(pieces):
    lane = lax.broadcasted_iota(jnp.int32, pieces[0].shape, 1) // KX
    out = []
    for e in range(4):
        got = None
        for b in range(4):
            moved = pieces[b] if b == e else pltpu.roll(pieces[b], (KX * (b - e)) % LANES, 1)
            got = moved if got is None else jnp.where(lane == b, moved, got)
        out.append(got)
    return out


def diagonal(block):
    width = block.shape[1]
    wide = (1, SUB * width)
    if width % LANES:
        row = lax.broadcasted_iota(jnp.int32, (width, SUB * width), 0)
        lane = lax.broadcasted_iota(jnp.int32, (width, SUB * width), 1)
        spread_out = (lax.rem(lane, width) == row).astype(F32).astype(BF16)
        block = dot(block, spread_out)
    else:
        block = jnp.concatenate([block.astype(F32)] * SUB, axis=1)
    lane = lax.broadcasted_iota(jnp.int32, wide, 1)
    return jnp.concatenate(
        [
            jnp.where((lane >= width * g) & (lane < width * (g + 1)), block, 0.0).astype(BF16)
            for g in range(SUB)
        ],
        axis=0,
    )


def turned_by_i(x, axis):
    size = x.shape[axis]
    place = lax.broadcasted_iota(jnp.int32, x.shape, axis)
    after = pltpu.roll(x, size - TWO, axis)
    before = pltpu.roll(x, TWO, axis)
    return jnp.where((place & TWO) == 0, -after, before)


def mix_kernel(
    lines,
    weight,
    table_x,
    table_back,
    bypass,
    mlp_in_t,
    mlp_out,
    decode,
    back,
    wide_bypass,
    wide_in,
    wide_out,
    modes,
    mixed,
):
    wide_bypass[...] = diagonal(bypass[...])
    wide_in[...] = diagonal((0.5 * mlp_in_t[...].astype(F32)).T.astype(BF16))
    heads = split(0.5 * dot(decode[...], mlp_out[...]))
    rows = [diagonal(part[k : k + 1]).astype(F32) for part in heads for k in range(2)]
    wide_out[...] = jnp.concatenate(rows, axis=0).astype(BF16)

    half = lines.shape[1] // 2
    count = half // (2 * TILES)
    groups = count // 4
    flipped = lines[...].T
    straight = jnp.concatenate([flipped[:half], flipped[half:]], axis=1)
    pair = jnp.concatenate([straight, -turned_by_i(straight, 0)], axis=1)
    high, low = split(pair)
    table = table_x[...]
    inner = table.shape[0] // 2
    spectrum = dot(
        jnp.concatenate([low, high, high], axis=1),
        jnp.concatenate([table[:inner], table], axis=0),
    )
    for c in range(SUB // 4):
        for a in range(groups):
            got = swap_blocks(
                [
                    spectrum[SUB * (4 * a + b) : SUB * (4 * a + b + 1), LANES * c : LANES * (c + 1)]
                    for b in range(4)
                ]
            )
            for e in range(4):
                modes[4 * c + e, :, LANES * a : LANES * (a + 1)] = got[e]
    width = weight.shape[1]
    real = jnp.zeros((width, count * KX), F32)
    imag = jnp.zeros((width, count * KX), F32)
    for i in range(width):
        t, v = i // SUB, i % SUB
        at = t // TWO * 2 * TWO + t % TWO
        in_real = modes[v, at : at + 1, :]
        in_imag = modes[v, at + TWO : at + TWO + 1, :]
        w_real = weight[0, i].astype(F32)
        w_imag = weight[1, i].astype(F32)
        real += in_real * w_real - in_imag * w_imag
        imag += in_real * w_imag + in_imag * w_real
    for a in range(groups):
        for t in range(TILES):
            here = slice(SUB * t, SUB * (t + 1)), slice(LANES * a, LANES * (a + 1))
            at = (t // TWO * 2 * TWO + t % TWO) * SUB
            mixed[0, a, at : at + SUB] = real[here]
            mixed[1, a, at : at + SUB] = -imag[here]
            at += TWO * SUB
            mixed[0, a, at : at + SUB] = imag[here]
            mixed[1, a, at : at + SUB] = real[here]
    rows = []
    for k in range(2):
        seen = [
            [mixed[k, a, pl.ds(v, 2 * TILES, stride=SUB), :] for v in range(SUB)]
            for a in range(groups)
        ]
        parts = [[None] * (SUB // 4) for _ in range(count)]
        for c in range(SUB // 4):
            for a in range(groups):
                got = swap_blocks(seen[a][4 * c : 4 * c + 4])
                for b in range(4):
                    parts[4 * a + b][c] = got[b]
        rows.append(jnp.concatenate([jnp.concatenate(p, axis=1) for p in parts], axis=0))
    high, low = split(jnp.concatenate(rows, axis=1))
    table = table_back[...]
    inner = table.shape[1] // 2
    got = dot(
        jnp.concatenate([table[:, :inner], table], axis=1),
        jnp.concatenate([low, high, high], axis=1),
        ((1,), (1,)),
    )
    count = got.shape[0] // 2
    back[...] = jnp.concatenate([got[:count], got[count:]], axis=1)


def gelu_twice(x):
    return x + x * jnp.tanh(x * (GELU_A + GELU_B * (x * x)))


def point_kernel(
    lines,
    values,
    wide_bypass,
    wide_in,
    wide_out,
    zone,
    opened,
    perm_table,
    tables,
    turns,
    near_side,
    far_side,
    filled,
    smooth,
    first,
):
    rows = near_side.shape[1]
    sent = lines[...]
    rolled = pltpu.roll(sent, HALF, 1)
    top = lax.broadcasted_iota(jnp.int32, sent.shape, 0) % SUB < SUB // 2
    of_even = jnp.where(top, sent, pltpu.roll(rolled, SUB // 2, 0))
    of_odd = jnp.where(top, pltpu.roll(sent, sent.shape[0] - SUB // 2, 0), rolled)
    held = jnp.concatenate(
        [x[SUB * k : SUB * (k + 1)] for k in range(KY // 2) for x in (of_even, of_odd)], axis=0
    )
    low_half = lax.broadcasted_iota(jnp.int32, held.shape, 1) < HALF
    held = jnp.where(low_half, held, pltpu.roll(held, HALF, 1))
    other = turned_by_i(held, 1)
    cosine, sine = tall(turns[0], 0, KY), tall(turns[1], 0, KY)
    straight = jnp.where(low_half, held, cosine * held + sine * other)
    turned = jnp.where(low_half, other, cosine * other - sine * held)

    def at(x, k):
        return x[SUB * k : SUB * (k + 1)]

    even = [at(straight, k) + at(straight, KY - k) for k in range(1, FOLD)]
    odd = [at(turned, k) - at(turned, KY - k) for k in range(1, FOLD)]
    even.append(at(straight, FOLD))
    odd.append(-at(turned, FOLD))
    level = jnp.concatenate([at(straight, 0)] * QUARTER, axis=0)
    count = QUARTER * SUB
    quarter = first // QUARTER

    def along_y(freqs, place, turns_of):
        sides = [quarters(even[k - 1], -odd[k - 1], turns_of * k) for k in freqs]
        sides = [real for real, _ in sides] + [-imag for _, imag in sides]
        sides = jnp.concatenate(split(jnp.concatenate(sides, axis=0)), axis=1)
        both = dot(tables[:count, place : place + 2 * LANES], jnp.concatenate([sides] * 2, axis=0))
        return both[:, :LANES] + both[:, LANES:]

    wanted = sorted({(quarter + m) % 2 for m in range(rows // QUARTER)})
    even_sums = {m: along_y(EVENS, 0, m) + level for m in wanted}
    odd_sums = {m: along_y(ODDS, 2 * LANES, m) for m in wanted}
    high_table = tables[count : count + LANES, : 2 * LANES]
    low_tables = tables[count : count + LANES, 2 * LANES :], tables[count + LANES :, : 2 * LANES]
    lane = lax.broadcasted_iota(jnp.int32, (count, LANES), 1)
    second_pair = (lane & (2 * TWO)) != 0
    for m in range(rows // QUARTER):
        side = (quarter + m) % 2
        minus = (quarter + m) // 2 % 2
        gained = even_sums[side] - odd_sums[side] if minus else even_sums[side] + odd_sums[side]
        high = gained.astype(BF16)
        rounded = high.astype(F32)
        rest = gained - rounded
        for k, shift in enumerate((2 * TWO, LANES - 2 * TWO)):
            moved = pltpu.roll(rest, shift, 1)
            own = jnp.where(second_pair, *((rounded, moved) if k else (moved, rounded)))
            smooth[count * m : count * (m + 1), 2 * LANES * k : 2 * LANES * (k + 1)] = dot(
                jnp.concatenate([own.astype(BF16), high], axis=1),
                jnp.concatenate([high_table, low_tables[k]], axis=0),
            )

    groups = rows // SUB

    def grouped(tile):
        return jnp.concatenate(
            [
                jnp.concatenate([tile(SUB * a + g) for a in range(groups)], axis=1)
                for g in range(SUB)
            ],
            axis=0,
        )

    own = grouped(lambda j: values[:, LANES * (first + j) : LANES * (first + j + 1)])
    spectral = grouped(
        lambda j: jnp.concatenate(
            [
                smooth[SUB * j : SUB * (j + 1), LANES * t : LANES * (t + 1)]
                for t in range(TILES)
            ],
            axis=0,
        )
    )
    lifted = gelu_twice(spectral + dot(wide_bypass[...], own)).astype(BF16)
    hidden = gelu_twice(dot(wide_in[...], lifted)).astype(BF16)
    decoded = dot(wide_out[...], hidden)
    decoded = decoded[: 2 * SUB] + decoded[2 * SUB :]
    even_plane = lax.axis_index("gx") % 2 == 0
    for a in range(rows // SUB):
        pressure = decoded[:SUB, LANES * a : LANES * (a + 1)]
        saturation = jax.nn.sigmoid(decoded[SUB:, LANES * a : LANES * (a + 1)])
        square = saturation * saturation
        rest = 1.0 - saturation
        at = slice(SUB * a, SUB * (a + 1))
        here = slice(first + SUB * a, first + SUB * (a + 1))
        filled[at] = saturation
        mobility = square / (square + 0.5 * rest * rest)
        perm = lookup(zone[here], perm_table)
        gated = perm * opened[0, here].astype(F32)
        near_side[0, at] = pressure
        near_side[1, at] = mobility
        near_side[2, at] = jnp.where(even_plane, gated, perm)
        far_side[0, at] = pressure
        far_side[1, at] = mobility
        far_side[2, at] = jnp.where(even_plane, perm, gated)


def lookup(zones, perm_table):
    perm = jnp.zeros(zones.shape, F32)
    for k in range(ZONES):
        perm = jnp.where(zones == k, perm_table[k], perm)
    return perm


def joined(first, second):
    both = first + second
    return jnp.where(both > 0.0, first * second / jnp.where(both > 0.0, both, 1.0), 0.0)


def ahead_y(field):
    rolled = pltpu.roll(field, NZ, 1)
    lane = lax.broadcasted_iota(jnp.int32, field.shape, 1)
    row = lax.broadcasted_iota(jnp.int32, field.shape, 0)
    below = pltpu.roll(rolled, field.shape[0] - 1, 0)
    below = jnp.where(row == field.shape[0] - 1, 0.0, below)
    return jnp.where(lane < LANES - NZ, rolled, below)


def behind_y(field):
    rolled = pltpu.roll(field, NZ, 1)
    lane = lax.broadcasted_iota(jnp.int32, field.shape, 1)
    row = lax.broadcasted_iota(jnp.int32, field.shape, 0)
    above = pltpu.roll(rolled, 1, 0)
    above = jnp.where(row == 0, 0.0, above)
    return jnp.where(lane >= NZ, rolled, above)


def ahead_z(field):
    lane = lax.broadcasted_iota(jnp.int32, field.shape, 1)
    return jnp.where(lane % NZ == NZ - 1, 0.0, pltpu.roll(field, LANES - 1, 1))


def behind_z(field):
    lane = lax.broadcasted_iota(jnp.int32, field.shape, 1)
    return jnp.where(lane % NZ == 0, 0.0, pltpu.roll(field, 1, 1))


def inner_kernel(
    first, last, first_filled, last_filled, zone, opened, perm_table, fields, partial
):
    pressure, mobility = [jnp.concatenate([first[k], last[k]], axis=0) for k in range(2)]
    fields[0] = pressure
    fields[1] = jnp.concatenate([first_filled[...], last_filled[...]], axis=0)
    perm = lookup(zone[...], perm_table)
    residual = jnp.zeros(pressure.shape, F32)
    for axis, ahead, behind in ((1, ahead_y, behind_y), (2, ahead_z, behind_z)):
        link = opened[axis].astype(F32) * joined(perm, ahead(perm))
        flux = link * (mobility + ahead(mobility)) * (pressure - ahead(pressure))
        residual = residual + (flux - behind(flux))
    partial[...] = residual


def outer_kernel(partial, *refs):
    residual = refs[-1]

    def flow(mine, other):
        link = joined(mine[2], other[2])
        return link * (mine[1] + other[1]) * (mine[0] - other[0])

    cut = refs[0].shape[1]
    for at, sides in ((slice(0, cut), refs[:4]), (slice(cut, ROWS), refs[4:8])):
        residual[at] = partial[at] + flow(sides[0], sides[3]) + flow(sides[1], sides[2])


def near(x):
    return pltpu.with_memory_space_constraint(x, pltpu.HBM)


def whole():
    return pl.BlockSpec(memory_space=pltpu.VMEM)


def params():
    return pltpu.CompilerParams(vmem_limit_bytes=40 * 1024 * 1024)


def body(
    features,
    block_scale,
    spec_weight,
    bypass_weight,
    mlp_in,
    mlp_out,
    decode_weight,
    zone_ids,
    face_open,
    perm_table,
):
    width, rows, cells = features.shape
    devices = lax.axis_size("gx")
    planes = rows * devices
    assert rows == 1 and cells == ROWS * LANES and width == TILES * SUB and devices % 2 == 0
    plane = features.reshape(width, cells)
    scale = block_scale.reshape(1, width)
    zone = zone_ids.reshape(ROWS, LANES)
    opened = face_open.reshape(3, ROWS, LANES)
    shares = devices // KY
    held = KZ // shares

    span = QUARTER * LANES
    chunks = cells // span
    table_z, table_y, turns = z_forward_table(), y_forward_table(), turn_forward_table()
    lines, values = pl.pallas_call(
        forward_kernel,
        in_specs=[pl.BlockSpec(memory_space=pl.ANY)] * 5,
        out_specs=[whole()] * 2,
        out_shape=[
            jax.ShapeDtypeStruct((KY * SUB // 2, LANES), F32),
            jax.ShapeDtypeStruct((width, cells), BF16),
        ],
        scratch_shapes=[
            pltpu.VMEM((chunks, width, span), BF16),
            pltpu.VMEM((1, width), F32),
            pltpu.VMEM(table_z.shape, BF16),
            pltpu.VMEM(table_y.shape, BF16),
            pltpu.VMEM(turns.shape, F32),
            pltpu.SemaphoreType.DMA((4 + chunks,)),
        ],
        compiler_params=params(),
        name="forward_yz",
    )(*map(near, (plane, scale, jnp.asarray(table_z), jnp.asarray(table_y), jnp.asarray(turns))))

    part = SUB // 2
    share = held * 2 * TILES
    blocks = lines.reshape(KY, part, 2, shares, share)
    blocks = blocks.transpose(0, 3, 1, 2, 4).reshape(devices, part, 2 * share)
    blocks = lax.all_to_all(blocks, "gx", 0, 0, tiled=True)
    lines = blocks.reshape(planes * part, 2 * share)

    modes = spec_weight.shape[3]
    hidden = mlp_in.shape[0]
    back, *wide = pl.pallas_call(
        mix_kernel,
        in_specs=[whole()] * 8,
        out_specs=[whole()] * 4,
        out_shape=[
            jax.ShapeDtypeStruct((planes * part, 2 * share), F32),
            jax.ShapeDtypeStruct((SUB * width, SUB * width), BF16),
            jax.ShapeDtypeStruct((SUB * hidden, SUB * width), BF16),
            jax.ShapeDtypeStruct((4 * SUB, SUB * hidden), BF16),
        ],
        scratch_shapes=[
            pltpu.VMEM((SUB, 2 * TILES, modes), F32),
            pltpu.VMEM((2, modes // LANES, 2 * width, LANES), F32),
        ],
        compiler_params=params(),
        name="mix_modes",
    )(
        lines,
        spec_weight,
        jnp.asarray(halves(x_forward_table(planes), 0)),
        jnp.asarray(halves(x_back_table(planes), 1)),
        bypass_weight,
        mlp_in.T,
        mlp_out,
        decode_weight,
    )

    blocks = back.reshape(devices, part, 2 * share)
    blocks = lax.all_to_all(blocks, "gx", 0, 0, tiled=True)
    blocks = blocks.reshape(KY, shares, part, 2, share).transpose(0, 2, 3, 1, 4)
    lines = blocks.reshape(KY * part, 2 * HALF)

    tables = np.concatenate([y_back_table(), z_back_table(planes * NY * NZ)], axis=0)
    tables = jnp.asarray(tables)

    def network(first, count):
        side = jax.ShapeDtypeStruct((3, count, LANES), F32)
        smem = pl.BlockSpec(memory_space=pltpu.SMEM)
        return pl.pallas_call(
            functools.partial(point_kernel, first=first),
            in_specs=[whole()] * 7 + [smem] + [whole()] * 2,
            out_specs=[whole()] * 3,
            out_shape=[side, side, jax.ShapeDtypeStruct((count, LANES), F32)],
            scratch_shapes=[pltpu.VMEM((count * SUB, TILES * LANES), F32)],
            compiler_params=params(),
            cost_estimate=pl.CostEstimate(
                flops=count * LANES * 400000, bytes_accessed=count * LANES * 200, transcendentals=0
            ),
            name="point_network",
        )(
            lines,
            values,
            *wide,
            zone,
            opened,
            perm_table,
            tables,
            jnp.asarray(turn_back_table()),
        )

    far = [(i, i + 1) for i in range(1, devices - 1, 2)]
    far = far + [(b, a) for a, b in far]
    near_by = [(i, i + 1) for i in range(0, devices, 2)]
    near_by = near_by + [(b, a) for a, b in near_by]
    *first, first_filled = network(0, ROWS - QUARTER)
    first_other = [lax.ppermute(first[1], "gx", far), lax.ppermute(first[0], "gx", near_by)]
    *last, last_filled = network(ROWS - QUARTER, QUARTER)
    last_other = [lax.ppermute(last[1], "gx", far), lax.ppermute(last[0], "gx", near_by)]
    fields, partial = pl.pallas_call(
        inner_kernel,
        in_specs=[whole()] * 6 + [pl.BlockSpec(memory_space=pltpu.SMEM)],
        out_specs=[whole()] * 2,
        out_shape=[
            jax.ShapeDtypeStruct((2, ROWS, LANES), F32),
            jax.ShapeDtypeStruct((ROWS, LANES), F32),
        ],
        compiler_params=params(),
        name="faces_in_plane",
    )(first[0], last[0], first_filled, last_filled, zone, opened, perm_table)
    residual = pl.pallas_call(
        outer_kernel,
        in_specs=[whole()] * 9,
        out_specs=whole(),
        out_shape=jax.ShapeDtypeStruct((ROWS, LANES), F32),
        compiler_params=params(),
        name="faces_between_planes",
    )(partial, *first, *first_other, *last, *last_other)
    return (fields.reshape(2, 1, cells), residual.reshape(1, cells))


def solution(mesh):
    in_specs = (
        P(None, ("groups", "gx"), None),
        P(None, ("groups", "gx")),
        P(None, None, None, "gx"),
        P(),
        P(),
        P(),
        P(),
        P(("groups", "gx"), None),
        P(None, ("groups", "gx"), None),
        P(),
    )
    out_specs = (P(None, ("groups", "gx"), None), P(("groups", "gx"), None))
    return jax.shard_map(body, mesh=mesh, in_specs=in_specs, out_specs=out_specs, check_vma=False)
```

```python
import functools
import math

import jax
import jax.numpy as jnp
import ml_dtypes
import numpy as np
from jax import lax
from jax.experimental import pallas as pl
from jax.experimental.pallas import tpu as pltpu
from jax.sharding import PartitionSpec as P

NY = 512
NZ = 64
KX = 32
KY = 32
KZ = 8
ZONES = 8
LANES = 128
SUB = 8
PAIRS = LANES // NZ
ROWS = NY // PAIRS
TILES = 4
TWO = 2
HALF = KZ * 2 * TILES
QUARTER = ROWS // 4
FOLD = KY // 2
CLASSES = (
    list(range(1, FOLD + 1, 2)),
    list(range(0, FOLD + 1, 4)),
    list(range(2, FOLD + 1, 4)),
)
EVENS, ODDS = list(range(2, FOLD + 1, 2)), list(range(1, FOLD + 1, 2))
GELU_A = math.sqrt(2.0 / math.pi)
GELU_B = GELU_A * 0.044715
F32 = jnp.float32
BF16 = jnp.bfloat16


def signed(count):
    steps = np.arange(count)
    return np.where(steps < count // 2, steps, steps - count)


def angles(freqs, positions, length):
    return 2.0 * np.pi * ((freqs[:, None] * positions[None, :]) % length) / length


def halves(table, axis):
    high = np.asarray(table, np.float64).astype(ml_dtypes.bfloat16)
    low = (table - high.astype(np.float64)).astype(ml_dtypes.bfloat16)
    return np.concatenate([high, low], axis=axis)


def spread(small):
    return np.kron(small, np.eye(SUB))


def z_forward_table():
    angle = angles(np.arange(KZ), np.arange(NZ), NZ)
    table = np.zeros((TWO, PAIRS, NZ, 2, KZ, PAIRS, 2, TWO))
    for t in range(TWO):
        for p in range(PAIRS):
            table[t, p, :, 0, :, p, 0, t] = np.cos(angle).T
            table[t, p, :, 0, :, p, 1, t] = -np.sin(angle).T
            table[t, p, :, 1, :, p, 0, t] = -np.sin(angle).T
            table[t, p, :, 1, :, p, 1, t] = -np.cos(angle).T
    return halves(table.reshape(TWO * LANES, LANES), 1)


def y_forward_table():
    angle = angles(np.arange(FOLD + 1), np.arange(QUARTER) * PAIRS, NY)
    parts = []
    for group in CLASSES:
        parts += [np.cos(angle[group]), np.sin(angle[[k for k in group if k]])]
    return halves(spread(np.concatenate(parts, axis=0)), 1)


def turn_forward_table():
    parity = angles(np.arange(FOLD + 1), np.arange(PAIRS), NY)
    parity = np.tile(np.repeat(parity, 2 * TWO, axis=1), (1, 2 * KZ))
    return np.stack([np.cos(parity), np.sin(parity)]).astype(np.float32)


def turn_back_table():
    parity = np.repeat(angles(signed(KY), np.array([1]), NY), LANES, axis=1)
    return np.stack([np.cos(parity), np.sin(parity)]).astype(np.float32)


def x_forward_table(planes):
    angle = angles(signed(KX), np.arange(planes), planes)

    def one(small):
        wide = np.zeros((2, planes, SUB // 2, SUB, KX))
        for s in range(SUB):
            wide[s // (SUB // 2), :, s % (SUB // 2), s, :] = small.T
        return wide.reshape(planes * SUB, SUB * KX)

    return np.concatenate([one(np.cos(angle)), one(np.sin(angle))], axis=0)


def x_back_table(planes):
    table = x_forward_table(planes).reshape(2, planes * SUB, SUB * KX)
    return np.concatenate([table[0], table[1]], axis=1)


def y_back_table():
    sides = []
    for freqs in (EVENS, ODDS):
        angle = angles(np.array(freqs), np.arange(QUARTER) * PAIRS, NY)
        sides.append(halves(spread(np.concatenate([np.cos(angle).T, np.sin(angle).T], axis=1)), 1))
    return np.concatenate(sides, axis=1)


def z_back_table(total):
    angle = angles(np.arange(KZ), np.arange(NZ), NZ)
    weight = np.where(np.arange(KZ) == 0, 1.0, 2.0)[:, None] / total
    table = np.zeros((PAIRS, KZ, TILES // TWO, 2, TWO, TWO, PAIRS, NZ))
    for t in range(TWO):
        for p in range(PAIRS):
            table[p, :, :, 0, t, t, p, :] = (weight * np.cos(angle))[:, None]
            table[p, :, :, 1, t, t, p, :] = (-weight * np.sin(angle))[:, None]
    high, low = np.split(halves(table, 0), 2)
    blocks = [high, low.copy(), low.copy(), np.zeros_like(low)]
    blocks[1][:, :, 1] = 0
    blocks[2][:, :, 0] = 0
    blocks = [block.reshape(LANES, TWO * LANES) for block in blocks]
    return np.concatenate([np.concatenate(blocks[k : k + 2], axis=1) for k in (0, 2)], axis=0)


def dot(a, b, dims=((1,), (0,)), precision=None):
    return lax.dot_general(a, b, (dims, ((), ())), precision=precision, preferred_element_type=F32)


def split(x):
    high = x.astype(BF16)
    return high, (x - high.astype(F32)).astype(BF16)


def column(row):
    n = row.shape[1]
    square = lax.broadcasted_iota(jnp.int32, (n, n), 0) == lax.broadcasted_iota(jnp.int32, (n, n), 1)
    return jnp.sum(jnp.where(square, row, 0.0), axis=1, keepdims=True)


def tall(table, first, count):
    return jnp.concatenate(
        [jnp.broadcast_to(table[k : k + 1], (SUB, LANES)) for k in range(first, first + count)],
        axis=0,
    )


def twice(x):
    return jnp.concatenate([x, x], axis=1)


def quarters(real, imag, turns):
    return ((real, imag), (-imag, real), (-real, -imag), (imag, -real))[turns % 4]


def forward_kernel(
    features, scale, table_z, table_y, turns, lines, values, held, factor, own_z, own_y, own_turns, done
):
    span = QUARTER * LANES
    chunks = features.shape[1] // span
    loads = [(scale, factor), (table_z, own_z), (table_y, own_y), (turns, own_turns)]
    loads += [(features.at[:, span * m : span * (m + 1)], held.at[m]) for m in range(chunks)]
    loads = [pltpu.make_async_copy(*pair, done.at[k]) for k, pair in enumerate(loads)]
    for load in loads:
        load.start()

    n = (FOLD + 1) * SUB
    def along_z(m):
        scaled = held[m].astype(F32) * gain
        values[:, span * m : span * (m + 1)] = scaled.astype(BF16)

        def tile(t, j):
            return scaled[SUB * t : SUB * (t + 1), LANES * j : LANES * (j + 1)]

        cells = jnp.concatenate(
            [
                jnp.concatenate([tile(t, j), tile(t + 1, j)], axis=1)
                for t in range(0, TILES, TWO)
                for j in range(QUARTER)
            ],
            axis=0,
        ).astype(BF16)
        part = dot(cells, own_z[...])
        part = part[:, :LANES] + part[:, LANES:]
        return jnp.concatenate([part[: SUB * QUARTER], part[SUB * QUARTER :]], axis=1)

    def along_y(place, group, x):
        table = own_y[SUB * place : SUB * (place + 2 * len(group) - (0 in group))]
        inner = table.shape[1] // 2
        high, low = split(x)
        sums = dot(
            jnp.concatenate([table[:, :inner], table], axis=1),
            jnp.concatenate([low, high, high], axis=0),
        )
        tiles = [sums[SUB * k : SUB * (k + 1)] for k in range(sums.shape[0] // SUB)]
        cosines, sines = tiles[: len(group)], tiles[len(group) :]
        return cosines, ([jnp.zeros_like(tiles[0])] if 0 in group else []) + sines

    for load in loads:
        load.wait()
    gain = column(factor[...])
    q = [along_z(m) for m in range(chunks)]
    sums, differences = [q[0] + q[2], q[1] + q[3]], [q[0] - q[2], q[1] - q[3]]
    even, odd = [None] * (FOLD + 1), [None] * (FOLD + 1)
    place = 0
    for group in CLASSES:
        if group[0] % 2:
            cosines, sines = along_y(place, group, jnp.concatenate(differences, axis=1))
            half = cosines[0].shape[1] // 2
            for k, c, s in zip(group, cosines, sines):
                sign = 1.0 if k % 4 == 1 else -1.0
                even[k] = c[:, :half] - sign * s[:, half:]
                odd[k] = s[:, :half] + sign * c[:, half:]
        else:
            x = sums[0] + sums[1] if group[0] % 4 == 0 else sums[0] - sums[1]
            for k, c, s in zip(group, *along_y(place, group, x)):
                even[k], odd[k] = c, s
        place += 2 * len(group) - (0 in group)

    first, second = jnp.concatenate(even, axis=0), jnp.concatenate(odd, axis=0)
    cosine = twice(tall(own_turns[0], 0, FOLD + 1))
    sine = twice(tall(own_turns[1], 0, FOLD + 1))
    even = cosine * first - sine * second
    odd = sine * first + cosine * second
    lane = lax.broadcasted_iota(jnp.int32, (n, LANES), 1)
    own = (lane & (2 * TWO)) == 0

    def packed(sign):
        sides = []
        for k in range(2):
            at = slice(LANES * k, LANES * (k + 1))
            line = even[:, at] + sign * pltpu.roll(odd[:, at], HALF, 1)
            shift = LANES - 2 * TWO if k == 0 else 2 * TWO
            sides.append(line + pltpu.roll(line, shift, 1))
        line = jnp.where(own, sides[0], sides[1])
        raised = pltpu.roll(pltpu.roll(line, HALF, 1), n - SUB // 2, 0)
        return jnp.where(lane < HALF, line, raised)

    up, down = packed(1.0), packed(-1.0)
    for k in range(FOLD):
        lines[SUB // 2 * k : SUB // 2 * (k + 1)] = up[SUB * k : SUB * k + SUB // 2]
    for k in range(FOLD, 0, -1):
        at = (KY - k) * SUB // 2
        lines[at : at + SUB // 2] = down[SUB * k : SUB * k + SUB // 2]


def swap_blocks(pieces):
    lane = lax.broadcasted_iota(jnp.int32, pieces[0].shape, 1) // KX
    out = []
    for e in range(4):
        got = None
        for b in range(4):
            moved = pieces[b] if b == e else pltpu.roll(pieces[b], (KX * (b - e)) % LANES, 1)
            got = moved if got is None else jnp.where(lane == b, moved, got)
        out.append(got)
    return out


def diagonal(block):
    width = block.shape[1]
    wide = (1, SUB * width)
    if width % LANES:
        row = lax.broadcasted_iota(jnp.int32, (width, SUB * width), 0)
        lane = lax.broadcasted_iota(jnp.int32, (width, SUB * width), 1)
        spread_out = (lax.rem(lane, width) == row).astype(F32).astype(BF16)
        block = dot(block, spread_out)
    else:
        block = jnp.concatenate([block.astype(F32)] * SUB, axis=1)
    lane = lax.broadcasted_iota(jnp.int32, wide, 1)
    return jnp.concatenate(
        [
            jnp.where((lane >= width * g) & (lane < width * (g + 1)), block, 0.0).astype(BF16)
            for g in range(SUB)
        ],
        axis=0,
    )


def turned_by_i(x, axis):
    size = x.shape[axis]
    place = lax.broadcasted_iota(jnp.int32, x.shape, axis)
    after = pltpu.roll(x, size - TWO, axis)
    before = pltpu.roll(x, TWO, axis)
    return jnp.where((place & TWO) == 0, -after, before)


def mix_kernel(
    lines,
    weight,
    table_x,
    table_back,
    bypass,
    mlp_in_t,
    mlp_out,
    decode,
    back,
    wide_bypass,
    wide_in,
    wide_out,
    modes,
    mixed,
):
    wide_bypass[...] = diagonal(bypass[...])
    wide_in[...] = diagonal((0.5 * mlp_in_t[...].astype(F32)).T.astype(BF16))
    heads = split(0.5 * dot(decode[...], mlp_out[...]))
    rows = [diagonal(part[k : k + 1]).astype(F32) for part in heads for k in range(2)]
    wide_out[...] = jnp.concatenate(rows, axis=0).astype(BF16)

    half = lines.shape[1] // 2
    count = half // (2 * TILES)
    groups = count // 4
    flipped = lines[...].T
    straight = jnp.concatenate([flipped[:half], flipped[half:]], axis=1)
    pair = jnp.concatenate([straight, -turned_by_i(straight, 0)], axis=1)
    high, low = split(pair)
    table = table_x[...]
    inner = table.shape[0] // 2
    spectrum = dot(
        jnp.concatenate([low, high, high], axis=1),
        jnp.concatenate([table[:inner], table], axis=0),
    )
    for c in range(SUB // 4):
        for a in range(groups):
            got = swap_blocks(
                [
                    spectrum[SUB * (4 * a + b) : SUB * (4 * a + b + 1), LANES * c : LANES * (c + 1)]
                    for b in range(4)
                ]
            )
            for e in range(4):
                modes[4 * c + e, :, LANES * a : LANES * (a + 1)] = got[e]
    width = weight.shape[1]
    real = jnp.zeros((width, count * KX), F32)
    imag = jnp.zeros((width, count * KX), F32)
    for i in range(width):
        t, v = i // SUB, i % SUB
        at = t // TWO * 2 * TWO + t % TWO
        in_real = modes[v, at : at + 1, :]
        in_imag = modes[v, at + TWO : at + TWO + 1, :]
        w_real = weight[0, i].astype(F32)
        w_imag = weight[1, i].astype(F32)
        real += in_real * w_real - in_imag * w_imag
        imag += in_real * w_imag + in_imag * w_real
    for a in range(groups):
        for t in range(TILES):
            here = slice(SUB * t, SUB * (t + 1)), slice(LANES * a, LANES * (a + 1))
            at = (t // TWO * 2 * TWO + t % TWO) * SUB
            mixed[0, a, at : at + SUB] = real[here]
            mixed[1, a, at : at + SUB] = -imag[here]
            at += TWO * SUB
            mixed[0, a, at : at + SUB] = imag[here]
            mixed[1, a, at : at + SUB] = real[here]
    rows = []
    for k in range(2):
        seen = [
            [mixed[k, a, pl.ds(v, 2 * TILES, stride=SUB), :] for v in range(SUB)]
            for a in range(groups)
        ]
        parts = [[None] * (SUB // 4) for _ in range(count)]
        for c in range(SUB // 4):
            for a in range(groups):
                got = swap_blocks(seen[a][4 * c : 4 * c + 4])
                for b in range(4):
                    parts[4 * a + b][c] = got[b]
        rows.append(jnp.concatenate([jnp.concatenate(p, axis=1) for p in parts], axis=0))
    high, low = split(jnp.concatenate(rows, axis=1))
    table = table_back[...]
    inner = table.shape[1] // 2
    got = dot(
        jnp.concatenate([table[:, :inner], table], axis=1),
        jnp.concatenate([low, high, high], axis=1),
        ((1,), (1,)),
    )
    count = got.shape[0] // 2
    back[...] = jnp.concatenate([got[:count], got[count:]], axis=1)


def gelu_twice(x):
    return x + x * jnp.tanh(x * (GELU_A + GELU_B * (x * x)))


def point_kernel(
    lines,
    values,
    wide_bypass,
    wide_in,
    wide_out,
    zone,
    opened,
    perm_table,
    tables,
    turns,
    near_side,
    far_side,
    filled,
    smooth,
    first,
):
    rows = near_side.shape[1]
    sent = lines[...]
    rolled = pltpu.roll(sent, HALF, 1)
    top = lax.broadcasted_iota(jnp.int32, sent.shape, 0) % SUB < SUB // 2
    of_even = jnp.where(top, sent, pltpu.roll(rolled, SUB // 2, 0))
    of_odd = jnp.where(top, pltpu.roll(sent, sent.shape[0] - SUB // 2, 0), rolled)
    held = jnp.concatenate(
        [x[SUB * k : SUB * (k + 1)] for k in range(KY // 2) for x in (of_even, of_odd)], axis=0
    )
    low_half = lax.broadcasted_iota(jnp.int32, held.shape, 1) < HALF
    held = jnp.where(low_half, held, pltpu.roll(held, HALF, 1))
    other = turned_by_i(held, 1)
    cosine, sine = tall(turns[0], 0, KY), tall(turns[1], 0, KY)
    straight = jnp.where(low_half, held, cosine * held + sine * other)
    turned = jnp.where(low_half, other, cosine * other - sine * held)

    def at(x, k):
        return x[SUB * k : SUB * (k + 1)]

    even = [at(straight, k) + at(straight, KY - k) for k in range(1, FOLD)]
    odd = [at(turned, k) - at(turned, KY - k) for k in range(1, FOLD)]
    even.append(at(straight, FOLD))
    odd.append(-at(turned, FOLD))
    level = jnp.concatenate([at(straight, 0)] * QUARTER, axis=0)
    count = QUARTER * SUB
    quarter = first // QUARTER

    def along_y(freqs, place, turns_of):
        sides = [quarters(even[k - 1], -odd[k - 1], turns_of * k) for k in freqs]
        sides = [real for real, _ in sides] + [-imag for _, imag in sides]
        sides = jnp.concatenate(split(jnp.concatenate(sides, axis=0)), axis=1)
        both = dot(tables[:count, place : place + 2 * LANES], jnp.concatenate([sides] * 2, axis=0))
        return both[:, :LANES] + both[:, LANES:]

    wanted = sorted({(quarter + m) % 2 for m in range(rows // QUARTER)})
    even_sums = {m: along_y(EVENS, 0, m) + level for m in wanted}
    odd_sums = {m: along_y(ODDS, 2 * LANES, m) for m in wanted}
    high_table = tables[count : count + LANES, : 2 * LANES]
    low_tables = tables[count : count + LANES, 2 * LANES :], tables[count + LANES :, : 2 * LANES]
    lane = lax.broadcasted_iota(jnp.int32, (count, LANES), 1)
    second_pair = (lane & (2 * TWO)) != 0
    for m in range(rows // QUARTER):
        side = (quarter + m) % 2
        minus = (quarter + m) // 2 % 2
        gained = even_sums[side] - odd_sums[side] if minus else even_sums[side] + odd_sums[side]
        high = gained.astype(BF16)
        rounded = high.astype(F32)
        rest = gained - rounded
        for k, shift in enumerate((2 * TWO, LANES - 2 * TWO)):
            moved = pltpu.roll(rest, shift, 1)
            own = jnp.where(second_pair, *((rounded, moved) if k else (moved, rounded)))
            smooth[count * m : count * (m + 1), 2 * LANES * k : 2 * LANES * (k + 1)] = dot(
                jnp.concatenate([own.astype(BF16), high], axis=1),
                jnp.concatenate([high_table, low_tables[k]], axis=0),
            )

    groups = rows // SUB

    def grouped(tile):
        return jnp.concatenate(
            [
                jnp.concatenate([tile(SUB * a + g) for a in range(groups)], axis=1)
                for g in range(SUB)
            ],
            axis=0,
        )

    own = grouped(lambda j: values[:, LANES * (first + j) : LANES * (first + j + 1)])
    spectral = grouped(
        lambda j: jnp.concatenate(
            [
                smooth[SUB * j : SUB * (j + 1), LANES * t : LANES * (t + 1)]
                for t in range(TILES)
            ],
            axis=0,
        )
    )
    lifted = gelu_twice(spectral + dot(wide_bypass[...], own)).astype(BF16)
    inner = dot(wide_in[...], lifted).astype(BF16)
    hidden = inner + inner * jnp.tanh(inner * (BF16(GELU_A) + BF16(GELU_B) * (inner * inner)))
    decoded = dot(wide_out[...], hidden)
    decoded = decoded[: 2 * SUB] + decoded[2 * SUB :]
    even_plane = lax.axis_index("gx") % 2 == 0
    for a in range(rows // SUB):
        pressure = decoded[:SUB, LANES * a : LANES * (a + 1)]
        saturation = jax.nn.sigmoid(decoded[SUB:, LANES * a : LANES * (a + 1)])
        square = saturation * saturation
        rest = 1.0 - saturation
        at = slice(SUB * a, SUB * (a + 1))
        here = slice(first + SUB * a, first + SUB * (a + 1))
        filled[at] = saturation
        mobility = square / (square + 0.5 * rest * rest)
        perm = lookup(zone[here], perm_table)
        gated = perm * opened[0, here].astype(F32)
        near_side[0, at] = pressure
        near_side[1, at] = mobility
        near_side[2, at] = jnp.where(even_plane, gated, perm)
        far_side[0, at] = pressure
        far_side[1, at] = mobility
        far_side[2, at] = jnp.where(even_plane, perm, gated)


def lookup(zones, perm_table):
    perm = jnp.zeros(zones.shape, F32)
    for k in range(ZONES):
        perm = jnp.where(zones == k, perm_table[k], perm)
    return perm


def joined(first, second):
    both = first + second
    return jnp.where(both > 0.0, first * second / jnp.where(both > 0.0, both, 1.0), 0.0)


def ahead_y(field):
    rolled = pltpu.roll(field, NZ, 1)
    lane = lax.broadcasted_iota(jnp.int32, field.shape, 1)
    row = lax.broadcasted_iota(jnp.int32, field.shape, 0)
    below = pltpu.roll(rolled, field.shape[0] - 1, 0)
    below = jnp.where(row == field.shape[0] - 1, 0.0, below)
    return jnp.where(lane < LANES - NZ, rolled, below)


def behind_y(field):
    rolled = pltpu.roll(field, NZ, 1)
    lane = lax.broadcasted_iota(jnp.int32, field.shape, 1)
    row = lax.broadcasted_iota(jnp.int32, field.shape, 0)
    above = pltpu.roll(rolled, 1, 0)
    above = jnp.where(row == 0, 0.0, above)
    return jnp.where(lane >= NZ, rolled, above)


def ahead_z(field):
    lane = lax.broadcasted_iota(jnp.int32, field.shape, 1)
    return jnp.where(lane % NZ == NZ - 1, 0.0, pltpu.roll(field, LANES - 1, 1))


def behind_z(field):
    lane = lax.broadcasted_iota(jnp.int32, field.shape, 1)
    return jnp.where(lane % NZ == 0, 0.0, pltpu.roll(field, 1, 1))


def inner_kernel(
    first, last, first_filled, last_filled, zone, opened, perm_table, fields, partial
):
    pressure, mobility = [jnp.concatenate([first[k], last[k]], axis=0) for k in range(2)]
    fields[0] = pressure
    fields[1] = jnp.concatenate([first_filled[...], last_filled[...]], axis=0)
    perm = lookup(zone[...], perm_table)
    residual = jnp.zeros(pressure.shape, F32)
    for axis, ahead, behind in ((1, ahead_y, behind_y), (2, ahead_z, behind_z)):
        link = opened[axis].astype(F32) * joined(perm, ahead(perm))
        flux = link * (mobility + ahead(mobility)) * (pressure - ahead(pressure))
        residual = residual + (flux - behind(flux))
    partial[...] = residual


def outer_kernel(partial, *refs):
    residual = refs[-1]

    def flow(mine, other):
        link = joined(mine[2], other[2])
        return link * (mine[1] + other[1]) * (mine[0] - other[0])

    cut = refs[0].shape[1]
    for at, sides in ((slice(0, cut), refs[:4]), (slice(cut, ROWS), refs[4:8])):
        residual[at] = partial[at] + flow(sides[0], sides[3]) + flow(sides[1], sides[2])


def near(x):
    return pltpu.with_memory_space_constraint(x, pltpu.HBM)


def whole():
    return pl.BlockSpec(memory_space=pltpu.VMEM)


def params():
    return pltpu.CompilerParams(vmem_limit_bytes=40 * 1024 * 1024)


def body(
    features,
    block_scale,
    spec_weight,
    bypass_weight,
    mlp_in,
    mlp_out,
    decode_weight,
    zone_ids,
    face_open,
    perm_table,
):
    width, rows, cells = features.shape
    devices = lax.axis_size("gx")
    planes = rows * devices
    assert rows == 1 and cells == ROWS * LANES and width == TILES * SUB and devices % 2 == 0
    plane = features.reshape(width, cells)
    scale = block_scale.reshape(1, width)
    zone = zone_ids.reshape(ROWS, LANES)
    opened = face_open.reshape(3, ROWS, LANES)
    shares = devices // KY
    held = KZ // shares

    span = QUARTER * LANES
    chunks = cells // span
    table_z, table_y, turns = z_forward_table(), y_forward_table(), turn_forward_table()
    lines, values = pl.pallas_call(
        forward_kernel,
        in_specs=[pl.BlockSpec(memory_space=pl.ANY)] * 5,
        out_specs=[whole()] * 2,
        out_shape=[
            jax.ShapeDtypeStruct((KY * SUB // 2, LANES), F32),
            jax.ShapeDtypeStruct((width, cells), BF16),
        ],
        scratch_shapes=[
            pltpu.VMEM((chunks, width, span), BF16),
            pltpu.VMEM((1, width), F32),
            pltpu.VMEM(table_z.shape, BF16),
            pltpu.VMEM(table_y.shape, BF16),
            pltpu.VMEM(turns.shape, F32),
            pltpu.SemaphoreType.DMA((4 + chunks,)),
        ],
        compiler_params=params(),
        name="forward_yz",
    )(*map(near, (plane, scale, jnp.asarray(table_z), jnp.asarray(table_y), jnp.asarray(turns))))

    part = SUB // 2
    share = held * 2 * TILES
    blocks = lines.reshape(KY, part, 2, shares, share)
    blocks = blocks.transpose(0, 3, 1, 2, 4).reshape(devices, part, 2 * share)
    blocks = lax.all_to_all(blocks, "gx", 0, 0, tiled=True)
    lines = blocks.reshape(planes * part, 2 * share)

    modes = spec_weight.shape[3]
    hidden = mlp_in.shape[0]
    back, *wide = pl.pallas_call(
        mix_kernel,
        in_specs=[whole()] * 8,
        out_specs=[whole()] * 4,
        out_shape=[
            jax.ShapeDtypeStruct((planes * part, 2 * share), F32),
            jax.ShapeDtypeStruct((SUB * width, SUB * width), BF16),
            jax.ShapeDtypeStruct((SUB * hidden, SUB * width), BF16),
            jax.ShapeDtypeStruct((4 * SUB, SUB * hidden), BF16),
        ],
        scratch_shapes=[
            pltpu.VMEM((SUB, 2 * TILES, modes), F32),
            pltpu.VMEM((2, modes // LANES, 2 * width, LANES), F32),
        ],
        compiler_params=params(),
        name="mix_modes",
    )(
        lines,
        spec_weight,
        jnp.asarray(halves(x_forward_table(planes), 0)),
        jnp.asarray(halves(x_back_table(planes), 1)),
        bypass_weight,
        mlp_in.T,
        mlp_out,
        decode_weight,
    )

    blocks = back.reshape(devices, part, 2 * share)
    blocks = lax.all_to_all(blocks, "gx", 0, 0, tiled=True)
    blocks = blocks.reshape(KY, shares, part, 2, share).transpose(0, 2, 3, 1, 4)
    lines = blocks.reshape(KY * part, 2 * HALF)

    tables = np.concatenate([y_back_table(), z_back_table(planes * NY * NZ)], axis=0)
    tables = jnp.asarray(tables)

    def network(first, count):
        side = jax.ShapeDtypeStruct((3, count, LANES), F32)
        smem = pl.BlockSpec(memory_space=pltpu.SMEM)
        return pl.pallas_call(
            functools.partial(point_kernel, first=first),
            in_specs=[whole()] * 7 + [smem] + [whole()] * 2,
            out_specs=[whole()] * 3,
            out_shape=[side, side, jax.ShapeDtypeStruct((count, LANES), F32)],
            scratch_shapes=[pltpu.VMEM((count * SUB, TILES * LANES), F32)],
            compiler_params=params(),
            cost_estimate=pl.CostEstimate(
                flops=count * LANES * 400000, bytes_accessed=count * LANES * 200, transcendentals=0
            ),
            name="point_network",
        )(
            lines,
            values,
            *wide,
            zone,
            opened,
            perm_table,
            tables,
            jnp.asarray(turn_back_table()),
        )

    far = [(i, i + 1) for i in range(1, devices - 1, 2)]
    far = far + [(b, a) for a, b in far]
    near_by = [(i, i + 1) for i in range(0, devices, 2)]
    near_by = near_by + [(b, a) for a, b in near_by]
    *first, first_filled = network(0, ROWS - QUARTER)
    first_other = [lax.ppermute(first[1], "gx", far), lax.ppermute(first[0], "gx", near_by)]
    *last, last_filled = network(ROWS - QUARTER, QUARTER)
    last_other = [lax.ppermute(last[1], "gx", far), lax.ppermute(last[0], "gx", near_by)]
    fields, partial = pl.pallas_call(
        inner_kernel,
        in_specs=[whole()] * 6 + [pl.BlockSpec(memory_space=pltpu.SMEM)],
        out_specs=[whole()] * 2,
        out_shape=[
            jax.ShapeDtypeStruct((2, ROWS, LANES), F32),
            jax.ShapeDtypeStruct((ROWS, LANES), F32),
        ],
        compiler_params=params(),
        name="faces_in_plane",
    )(first[0], last[0], first_filled, last_filled, zone, opened, perm_table)
    residual = pl.pallas_call(
        outer_kernel,
        in_specs=[whole()] * 9,
        out_specs=whole(),
        out_shape=jax.ShapeDtypeStruct((ROWS, LANES), F32),
        compiler_params=params(),
        name="faces_between_planes",
    )(partial, *first, *first_other, *last, *last_other)
    return (fields.reshape(2, 1, cells), residual.reshape(1, cells))


def solution(mesh):
    in_specs = (
        P(None, ("groups", "gx"), None),
        P(None, ("groups", "gx")),
        P(None, None, None, "gx"),
        P(),
        P(),
        P(),
        P(),
        P(("groups", "gx"), None),
        P(None, ("groups", "gx"), None),
        P(),
    )
    out_specs = (P(None, ("groups", "gx"), None), P(("groups", "gx"), None))
    return jax.shard_map(body, mesh=mesh, in_specs=in_specs, out_specs=out_specs, check_vma=False)
```

```python
import functools
import math

import jax
import jax.numpy as jnp
import ml_dtypes
import numpy as np
from jax import lax
from jax.experimental import pallas as pl
from jax.experimental.pallas import tpu as pltpu
from jax.sharding import PartitionSpec as P

NY = 512
NZ = 64
KX = 32
KY = 32
KZ = 8
ZONES = 8
LANES = 128
SUB = 8
PAIRS = LANES // NZ
ROWS = NY // PAIRS
TILES = 4
TWO = 2
HALF = KZ * 2 * TILES
QUARTER = ROWS // 4
FOLD = KY // 2
CLASSES = (
    list(range(1, FOLD + 1, 2)),
    list(range(0, FOLD + 1, 4)),
    list(range(2, FOLD + 1, 4)),
)
EVENS, ODDS = list(range(2, FOLD + 1, 2)), list(range(1, FOLD + 1, 2))
GELU_A = math.sqrt(2.0 / math.pi)
GELU_B = GELU_A * 0.044715
F32 = jnp.float32
BF16 = jnp.bfloat16


def signed(count):
    steps = np.arange(count)
    return np.where(steps < count // 2, steps, steps - count)


def angles(freqs, positions, length):
    return 2.0 * np.pi * ((freqs[:, None] * positions[None, :]) % length) / length


def halves(table, axis):
    high = np.asarray(table, np.float64).astype(ml_dtypes.bfloat16)
    low = (table - high.astype(np.float64)).astype(ml_dtypes.bfloat16)
    return np.concatenate([high, low], axis=axis)


def spread(small):
    return np.kron(small, np.eye(SUB))


def z_forward_table():
    angle = angles(np.arange(KZ), np.arange(NZ), NZ)
    table = np.zeros((TWO, PAIRS, NZ, 2, KZ, PAIRS, 2, TWO))
    for t in range(TWO):
        for p in range(PAIRS):
            table[t, p, :, 0, :, p, 0, t] = np.cos(angle).T
            table[t, p, :, 0, :, p, 1, t] = -np.sin(angle).T
            table[t, p, :, 1, :, p, 0, t] = -np.sin(angle).T
            table[t, p, :, 1, :, p, 1, t] = -np.cos(angle).T
    return halves(table.reshape(TWO * LANES, LANES), 1)


def y_forward_table():
    angle = angles(np.arange(FOLD + 1), np.arange(QUARTER) * PAIRS, NY)
    parts = []
    for group in CLASSES:
        parts += [np.cos(angle[group]), np.sin(angle[[k for k in group if k]])]
    return halves(spread(np.concatenate(parts, axis=0)), 1)


def turn_forward_table():
    parity = angles(np.arange(FOLD + 1), np.arange(PAIRS), NY)
    parity = np.tile(np.repeat(parity, 2 * TWO, axis=1), (1, 2 * KZ))
    return np.stack([np.cos(parity), np.sin(parity)]).astype(np.float32)


def turn_back_table():
    parity = np.repeat(angles(signed(KY), np.array([1]), NY), LANES, axis=1)
    return np.stack([np.cos(parity), np.sin(parity)]).astype(np.float32)


def x_forward_table(planes):
    angle = angles(signed(KX), np.arange(planes), planes)

    def one(small):
        wide = np.zeros((2, planes, SUB // 2, SUB, KX))
        for s in range(SUB):
            wide[s // (SUB // 2), :, s % (SUB // 2), s, :] = small.T
        return wide.reshape(planes * SUB, SUB * KX)

    return np.concatenate([one(np.cos(angle)), one(np.sin(angle))], axis=0)


def x_back_table(planes):
    table = x_forward_table(planes).reshape(2, planes * SUB, SUB * KX)
    return np.concatenate([table[0], table[1]], axis=1)


def y_back_table():
    sides = []
    for freqs in (EVENS, ODDS):
        angle = angles(np.array(freqs), np.arange(QUARTER) * PAIRS, NY)
        sides.append(halves(spread(np.concatenate([np.cos(angle).T, np.sin(angle).T], axis=1)), 1))
    return np.concatenate(sides, axis=1)


def z_back_table(total):
    angle = angles(np.arange(KZ), np.arange(NZ), NZ)
    weight = np.where(np.arange(KZ) == 0, 1.0, 2.0)[:, None] / total
    table = np.zeros((PAIRS, KZ, TILES // TWO, 2, TWO, TWO, PAIRS, NZ))
    for t in range(TWO):
        for p in range(PAIRS):
            table[p, :, :, 0, t, t, p, :] = (weight * np.cos(angle))[:, None]
            table[p, :, :, 1, t, t, p, :] = (-weight * np.sin(angle))[:, None]
    high, low = np.split(halves(table, 0), 2)
    blocks = [high, low.copy(), low.copy(), np.zeros_like(low)]
    blocks[1][:, :, 1] = 0
    blocks[2][:, :, 0] = 0
    blocks = [block.reshape(LANES, TWO * LANES) for block in blocks]
    return np.concatenate([np.concatenate(blocks[k : k + 2], axis=1) for k in (0, 2)], axis=0)


def dot(a, b, dims=((1,), (0,)), precision=None):
    return lax.dot_general(a, b, (dims, ((), ())), precision=precision, preferred_element_type=F32)


def split(x):
    high = x.astype(BF16)
    return high, (x - high.astype(F32)).astype(BF16)


def column(row):
    n = row.shape[1]
    square = lax.broadcasted_iota(jnp.int32, (n, n), 0) == lax.broadcasted_iota(jnp.int32, (n, n), 1)
    return jnp.sum(jnp.where(square, row, 0.0), axis=1, keepdims=True)


def tall(table, first, count):
    return jnp.concatenate(
        [jnp.broadcast_to(table[k : k + 1], (SUB, LANES)) for k in range(first, first + count)],
        axis=0,
    )


def twice(x):
    return jnp.concatenate([x, x], axis=1)


def quarters(real, imag, turns):
    return ((real, imag), (-imag, real), (-real, -imag), (imag, -real))[turns % 4]


def forward_kernel(
    features, scale, table_z, table_y, turns, lines, values, held, factor, own_z, own_y, own_turns, done
):
    span = QUARTER * LANES
    chunks = features.shape[1] // span
    loads = [(scale, factor), (table_z, own_z), (table_y, own_y), (turns, own_turns)]
    loads += [(features.at[:, span * m : span * (m + 1)], held.at[m]) for m in range(chunks)]
    loads = [pltpu.make_async_copy(*pair, done.at[k]) for k, pair in enumerate(loads)]
    for load in loads:
        load.start()

    n = (FOLD + 1) * SUB
    def along_z(m):
        scaled = held[m].astype(F32) * gain
        values[:, span * m : span * (m + 1)] = scaled.astype(BF16)

        def tile(t, j):
            return scaled[SUB * t : SUB * (t + 1), LANES * j : LANES * (j + 1)]

        cells = jnp.concatenate(
            [
                jnp.concatenate([tile(t, j), tile(t + 1, j)], axis=1)
                for t in range(0, TILES, TWO)
                for j in range(QUARTER)
            ],
            axis=0,
        ).astype(BF16)
        part = dot(cells, own_z[...])
        part = part[:, :LANES] + part[:, LANES:]
        return jnp.concatenate([part[: SUB * QUARTER], part[SUB * QUARTER :]], axis=1)

    def along_y(place, group, x):
        table = own_y[SUB * place : SUB * (place + 2 * len(group) - (0 in group))]
        inner = table.shape[1] // 2
        high, low = split(x)
        sums = dot(
            jnp.concatenate([table[:, :inner], table], axis=1),
            jnp.concatenate([low, high, high], axis=0),
        )
        tiles = [sums[SUB * k : SUB * (k + 1)] for k in range(sums.shape[0] // SUB)]
        cosines, sines = tiles[: len(group)], tiles[len(group) :]
        return cosines, ([jnp.zeros_like(tiles[0])] if 0 in group else []) + sines

    for load in loads:
        load.wait()
    gain = column(factor[...])
    q = [along_z(m) for m in range(chunks)]
    sums, differences = [q[0] + q[2], q[1] + q[3]], [q[0] - q[2], q[1] - q[3]]
    even, odd = [None] * (FOLD + 1), [None] * (FOLD + 1)
    place = 0
    for group in CLASSES:
        if group[0] % 2:
            cosines, sines = along_y(place, group, jnp.concatenate(differences, axis=1))
            half = cosines[0].shape[1] // 2
            for k, c, s in zip(group, cosines, sines):
                sign = 1.0 if k % 4 == 1 else -1.0
                even[k] = c[:, :half] - sign * s[:, half:]
                odd[k] = s[:, :half] + sign * c[:, half:]
        else:
            x = sums[0] + sums[1] if group[0] % 4 == 0 else sums[0] - sums[1]
            for k, c, s in zip(group, *along_y(place, group, x)):
                even[k], odd[k] = c, s
        place += 2 * len(group) - (0 in group)

    first, second = jnp.concatenate(even, axis=0), jnp.concatenate(odd, axis=0)
    cosine = twice(tall(own_turns[0], 0, FOLD + 1))
    sine = twice(tall(own_turns[1], 0, FOLD + 1))
    even = cosine * first - sine * second
    odd = sine * first + cosine * second
    lane = lax.broadcasted_iota(jnp.int32, (n, LANES), 1)
    own = (lane & (2 * TWO)) == 0

    def packed(sign):
        sides = []
        for k in range(2):
            at = slice(LANES * k, LANES * (k + 1))
            line = even[:, at] + sign * pltpu.roll(odd[:, at], HALF, 1)
            shift = LANES - 2 * TWO if k == 0 else 2 * TWO
            sides.append(line + pltpu.roll(line, shift, 1))
        line = jnp.where(own, sides[0], sides[1])
        raised = pltpu.roll(pltpu.roll(line, HALF, 1), n - SUB // 2, 0)
        return jnp.where(lane < HALF, line, raised)

    up, down = packed(1.0), packed(-1.0)
    for k in range(FOLD):
        lines[SUB // 2 * k : SUB // 2 * (k + 1)] = up[SUB * k : SUB * k + SUB // 2]
    for k in range(FOLD, 0, -1):
        at = (KY - k) * SUB // 2
        lines[at : at + SUB // 2] = down[SUB * k : SUB * k + SUB // 2]


def swap_blocks(pieces):
    lane = lax.broadcasted_iota(jnp.int32, pieces[0].shape, 1) // KX
    out = []
    for e in range(4):
        got = None
        for b in range(4):
            moved = pieces[b] if b == e else pltpu.roll(pieces[b], (KX * (b - e)) % LANES, 1)
            got = moved if got is None else jnp.where(lane == b, moved, got)
        out.append(got)
    return out


def diagonal(block):
    width = block.shape[1]
    wide = (1, SUB * width)
    if width % LANES:
        row = lax.broadcasted_iota(jnp.int32, (width, SUB * width), 0)
        lane = lax.broadcasted_iota(jnp.int32, (width, SUB * width), 1)
        spread_out = (lax.rem(lane, width) == row).astype(F32).astype(BF16)
        block = dot(block, spread_out)
    else:
        block = jnp.concatenate([block.astype(F32)] * SUB, axis=1)
    lane = lax.broadcasted_iota(jnp.int32, wide, 1)
    return jnp.concatenate(
        [
            jnp.where((lane >= width * g) & (lane < width * (g + 1)), block, 0.0).astype(BF16)
            for g in range(SUB)
        ],
        axis=0,
    )


def turned_by_i(x, axis):
    size = x.shape[axis]
    place = lax.broadcasted_iota(jnp.int32, x.shape, axis)
    after = pltpu.roll(x, size - TWO, axis)
    before = pltpu.roll(x, TWO, axis)
    return jnp.where((place & TWO) == 0, -after, before)


def mix_kernel(
    lines,
    weight,
    table_x,
    table_back,
    bypass,
    mlp_in_t,
    mlp_out,
    decode,
    back,
    wide_bypass,
    wide_in,
    wide_out,
    modes,
    mixed,
):
    wide_bypass[...] = diagonal(bypass[...])
    wide_in[...] = diagonal((0.5 * mlp_in_t[...].astype(F32)).T.astype(BF16))
    heads = split(0.5 * dot(decode[...], mlp_out[...]))
    rows = [diagonal(part[k : k + 1]).astype(F32) for part in heads for k in range(2)]
    wide_out[...] = jnp.concatenate(rows, axis=0).astype(BF16)

    half = lines.shape[1] // 2
    count = half // (2 * TILES)
    groups = count // 4
    flipped = lines[...].T
    straight = jnp.concatenate([flipped[:half], flipped[half:]], axis=1)
    pair = jnp.concatenate([straight, -turned_by_i(straight, 0)], axis=1)
    high, low = split(pair)
    table = table_x[...]
    inner = table.shape[0] // 2
    spectrum = dot(
        jnp.concatenate([low, high, high], axis=1),
        jnp.concatenate([table[:inner], table], axis=0),
    )
    for c in range(SUB // 4):
        for a in range(groups):
            got = swap_blocks(
                [
                    spectrum[SUB * (4 * a + b) : SUB * (4 * a + b + 1), LANES * c : LANES * (c + 1)]
                    for b in range(4)
                ]
            )
            for e in range(4):
                modes[4 * c + e, :, LANES * a : LANES * (a + 1)] = got[e]
    width = weight.shape[1]
    real = jnp.zeros((width, count * KX), F32)
    imag = jnp.zeros((width, count * KX), F32)
    for i in range(width):
        t, v = i // SUB, i % SUB
        at = t // TWO * 2 * TWO + t % TWO
        in_real = modes[v, at : at + 1, :]
        in_imag = modes[v, at + TWO : at + TWO + 1, :]
        w_real = weight[0, i].astype(F32)
        w_imag = weight[1, i].astype(F32)
        real += in_real * w_real - in_imag * w_imag
        imag += in_real * w_imag + in_imag * w_real
    for a in range(groups):
        for t in range(TILES):
            here = slice(SUB * t, SUB * (t + 1)), slice(LANES * a, LANES * (a + 1))
            at = (t // TWO * 2 * TWO + t % TWO) * SUB
            mixed[0, a, at : at + SUB] = real[here]
            mixed[1, a, at : at + SUB] = -imag[here]
            at += TWO * SUB
            mixed[0, a, at : at + SUB] = imag[here]
            mixed[1, a, at : at + SUB] = real[here]
    rows = []
    for k in range(2):
        seen = [
            [mixed[k, a, pl.ds(v, 2 * TILES, stride=SUB), :] for v in range(SUB)]
            for a in range(groups)
        ]
        parts = [[None] * (SUB // 4) for _ in range(count)]
        for c in range(SUB // 4):
            for a in range(groups):
                got = swap_blocks(seen[a][4 * c : 4 * c + 4])
                for b in range(4):
                    parts[4 * a + b][c] = got[b]
        rows.append(jnp.concatenate([jnp.concatenate(p, axis=1) for p in parts], axis=0))
    high, low = split(jnp.concatenate(rows, axis=1))
    table = table_back[...]
    inner = table.shape[1] // 2
    got = dot(
        jnp.concatenate([table[:, :inner], table], axis=1),
        jnp.concatenate([low, high, high], axis=1),
        ((1,), (1,)),
    )
    count = got.shape[0] // 2
    back[...] = jnp.concatenate([got[:count], got[count:]], axis=1)


def gelu_twice(x):
    return x + x * jnp.tanh(x * (GELU_A + GELU_B * (x * x)))


def point_kernel(
    lines,
    values,
    wide_bypass,
    wide_in,
    wide_out,
    zone,
    opened,
    perm_table,
    tables,
    turns,
    near_side,
    far_side,
    filled,
    smooth,
    first,
):
    rows = near_side.shape[1]
    sent = lines[...]
    rolled = pltpu.roll(sent, HALF, 1)
    top = lax.broadcasted_iota(jnp.int32, sent.shape, 0) % SUB < SUB // 2
    of_even = jnp.where(top, sent, pltpu.roll(rolled, SUB // 2, 0))
    of_odd = jnp.where(top, pltpu.roll(sent, sent.shape[0] - SUB // 2, 0), rolled)
    held = jnp.concatenate(
        [x[SUB * k : SUB * (k + 1)] for k in range(KY // 2) for x in (of_even, of_odd)], axis=0
    )
    low_half = lax.broadcasted_iota(jnp.int32, held.shape, 1) < HALF
    held = jnp.where(low_half, held, pltpu.roll(held, HALF, 1))
    other = turned_by_i(held, 1)
    cosine, sine = tall(turns[0], 0, KY), tall(turns[1], 0, KY)
    straight = jnp.where(low_half, held, cosine * held + sine * other)
    turned = jnp.where(low_half, other, cosine * other - sine * held)

    def at(x, k):
        return x[SUB * k : SUB * (k + 1)]

    even = [at(straight, k) + at(straight, KY - k) for k in range(1, FOLD)]
    odd = [at(turned, k) - at(turned, KY - k) for k in range(1, FOLD)]
    even.append(at(straight, FOLD))
    odd.append(-at(turned, FOLD))
    level = jnp.concatenate([at(straight, 0)] * QUARTER, axis=0)
    count = QUARTER * SUB
    quarter = first // QUARTER

    def along_y(freqs, place, turns_of):
        sides = [quarters(even[k - 1], -odd[k - 1], turns_of * k) for k in freqs]
        sides = [real for real, _ in sides] + [-imag for _, imag in sides]
        sides = jnp.concatenate(split(jnp.concatenate(sides, axis=0)), axis=1)
        both = dot(tables[:count, place : place + 2 * LANES], jnp.concatenate([sides] * 2, axis=0))
        return both[:, :LANES] + both[:, LANES:]

    wanted = sorted({(quarter + m) % 2 for m in range(rows // QUARTER)})
    even_sums = {m: along_y(EVENS, 0, m) + level for m in wanted}
    odd_sums = {m: along_y(ODDS, 2 * LANES, m) for m in wanted}
    high_table = tables[count : count + LANES, : 2 * LANES]
    low_tables = tables[count : count + LANES, 2 * LANES :], tables[count + LANES :, : 2 * LANES]
    lane = lax.broadcasted_iota(jnp.int32, (count, LANES), 1)
    second_pair = (lane & (2 * TWO)) != 0
    for m in range(rows // QUARTER):
        side = (quarter + m) % 2
        minus = (quarter + m) // 2 % 2
        gained = even_sums[side] - odd_sums[side] if minus else even_sums[side] + odd_sums[side]
        high = gained.astype(BF16)
        rounded = high.astype(F32)
        rest = gained - rounded
        for k, shift in enumerate((2 * TWO, LANES - 2 * TWO)):
            moved = pltpu.roll(rest, shift, 1)
            own = jnp.where(second_pair, *((rounded, moved) if k else (moved, rounded)))
            smooth[count * m : count * (m + 1), 2 * LANES * k : 2 * LANES * (k + 1)] = dot(
                jnp.concatenate([own.astype(BF16), high], axis=1),
                jnp.concatenate([high_table, low_tables[k]], axis=0),
            )

    groups = rows // SUB

    def grouped(tile):
        return jnp.concatenate(
            [
                jnp.concatenate([tile(SUB * a + g) for a in range(groups)], axis=1)
                for g in range(SUB)
            ],
            axis=0,
        )

    own = grouped(lambda j: values[:, LANES * (first + j) : LANES * (first + j + 1)])
    spectral = grouped(
        lambda j: jnp.concatenate(
            [
                smooth[SUB * j : SUB * (j + 1), LANES * t : LANES * (t + 1)]
                for t in range(TILES)
            ],
            axis=0,
        )
    )
    lifted = gelu_twice(spectral + dot(wide_bypass[...], own)).astype(BF16)
    inner = dot(wide_in[...], lifted).astype(BF16)
    hidden = inner + inner * jnp.tanh(inner * (BF16(GELU_A) + BF16(GELU_B) * (inner * inner)))
    decoded = dot(wide_out[...], hidden)
    decoded = decoded[: 2 * SUB] + decoded[2 * SUB :]
    even_plane = lax.axis_index("gx") % 2 == 0
    for a in range(rows // SUB):
        pressure = decoded[:SUB, LANES * a : LANES * (a + 1)]
        saturation = jax.nn.sigmoid(decoded[SUB:, LANES * a : LANES * (a + 1)])
        square = saturation * saturation
        rest = 1.0 - saturation
        at = slice(SUB * a, SUB * (a + 1))
        here = slice(first + SUB * a, first + SUB * (a + 1))
        filled[at] = saturation
        mobility = square / (square + 0.5 * rest * rest)
        perm = lookup(zone[here], perm_table)
        gated = perm * opened[0, here].astype(F32)
        near_side[0, at] = pressure
        near_side[1, at] = mobility
        near_side[2, at] = jnp.where(even_plane, gated, perm)
        far_side[0, at] = pressure
        far_side[1, at] = mobility
        far_side[2, at] = jnp.where(even_plane, perm, gated)


def lookup(zones, perm_table):
    perm = jnp.zeros(zones.shape, F32)
    for k in range(ZONES):
        perm = jnp.where(zones == k, perm_table[k], perm)
    return perm


def joined(first, second):
    both = first + second
    return jnp.where(both > 0.0, first * second / jnp.where(both > 0.0, both, 1.0), 0.0)


def ahead_y(field):
    rolled = pltpu.roll(field, NZ, 1)
    lane = lax.broadcasted_iota(jnp.int32, field.shape, 1)
    row = lax.broadcasted_iota(jnp.int32, field.shape, 0)
    below = pltpu.roll(rolled, field.shape[0] - 1, 0)
    below = jnp.where(row == field.shape[0] - 1, 0.0, below)
    return jnp.where(lane < LANES - NZ, rolled, below)


def behind_y(field):
    rolled = pltpu.roll(field, NZ, 1)
    lane = lax.broadcasted_iota(jnp.int32, field.shape, 1)
    row = lax.broadcasted_iota(jnp.int32, field.shape, 0)
    above = pltpu.roll(rolled, 1, 0)
    above = jnp.where(row == 0, 0.0, above)
    return jnp.where(lane >= NZ, rolled, above)


def ahead_z(field):
    lane = lax.broadcasted_iota(jnp.int32, field.shape, 1)
    return jnp.where(lane % NZ == NZ - 1, 0.0, pltpu.roll(field, LANES - 1, 1))


def behind_z(field):
    lane = lax.broadcasted_iota(jnp.int32, field.shape, 1)
    return jnp.where(lane % NZ == 0, 0.0, pltpu.roll(field, 1, 1))


def inner_kernel(
    first, last, first_filled, last_filled, zone, opened, perm_table, fields, partial
):
    pressure, mobility = [jnp.concatenate([first[k], last[k]], axis=0) for k in range(2)]
    fields[0] = pressure
    fields[1] = jnp.concatenate([first_filled[...], last_filled[...]], axis=0)
    perm = lookup(zone[...], perm_table)
    residual = jnp.zeros(pressure.shape, F32)
    for axis, ahead, behind in ((1, ahead_y, behind_y), (2, ahead_z, behind_z)):
        link = opened[axis].astype(F32) * joined(perm, ahead(perm))
        flux = link * (mobility + ahead(mobility)) * (pressure - ahead(pressure))
        residual = residual + (flux - behind(flux))
    partial[...] = residual


def outer_kernel(partial, *refs):
    residual = refs[-1]

    def flow(mine, other):
        link = joined(mine[2], other[2])
        return link * (mine[1] + other[1]) * (mine[0] - other[0])

    cut = refs[0].shape[1]
    for at, sides in ((slice(0, cut), refs[:4]), (slice(cut, ROWS), refs[4:8])):
        residual[at] = partial[at] + flow(sides[0], sides[2]) + flow(sides[1], sides[3])


def near(x):
    return pltpu.with_memory_space_constraint(x, pltpu.HBM)


def whole():
    return pl.BlockSpec(memory_space=pltpu.VMEM)


def params():
    return pltpu.CompilerParams(vmem_limit_bytes=40 * 1024 * 1024)


def body(
    features,
    block_scale,
    spec_weight,
    bypass_weight,
    mlp_in,
    mlp_out,
    decode_weight,
    zone_ids,
    face_open,
    perm_table,
):
    width, rows, cells = features.shape
    devices = lax.axis_size("gx")
    planes = rows * devices
    assert rows == 1 and cells == ROWS * LANES and width == TILES * SUB and devices % 2 == 0
    plane = features.reshape(width, cells)
    scale = block_scale.reshape(1, width)
    zone = zone_ids.reshape(ROWS, LANES)
    opened = face_open.reshape(3, ROWS, LANES)
    shares = devices // KY
    held = KZ // shares

    span = QUARTER * LANES
    chunks = cells // span
    table_z, table_y, turns = z_forward_table(), y_forward_table(), turn_forward_table()
    lines, values = pl.pallas_call(
        forward_kernel,
        in_specs=[pl.BlockSpec(memory_space=pl.ANY)] * 5,
        out_specs=[whole()] * 2,
        out_shape=[
            jax.ShapeDtypeStruct((KY * SUB // 2, LANES), F32),
            jax.ShapeDtypeStruct((width, cells), BF16),
        ],
        scratch_shapes=[
            pltpu.VMEM((chunks, width, span), BF16),
            pltpu.VMEM((1, width), F32),
            pltpu.VMEM(table_z.shape, BF16),
            pltpu.VMEM(table_y.shape, BF16),
            pltpu.VMEM(turns.shape, F32),
            pltpu.SemaphoreType.DMA((4 + chunks,)),
        ],
        compiler_params=params(),
        name="forward_yz",
    )(*map(near, (plane, scale, jnp.asarray(table_z), jnp.asarray(table_y), jnp.asarray(turns))))

    part = SUB // 2
    share = held * 2 * TILES
    blocks = lines.reshape(KY, part, 2, shares, share)
    blocks = blocks.transpose(0, 3, 1, 2, 4).reshape(devices, part, 2 * share)
    blocks = lax.all_to_all(blocks, "gx", 0, 0, tiled=True)
    lines = blocks.reshape(planes * part, 2 * share)

    modes = spec_weight.shape[3]
    hidden = mlp_in.shape[0]
    back, *wide = pl.pallas_call(
        mix_kernel,
        in_specs=[whole()] * 8,
        out_specs=[whole()] * 4,
        out_shape=[
            jax.ShapeDtypeStruct((planes * part, 2 * share), F32),
            jax.ShapeDtypeStruct((SUB * width, SUB * width), BF16),
            jax.ShapeDtypeStruct((SUB * hidden, SUB * width), BF16),
            jax.ShapeDtypeStruct((4 * SUB, SUB * hidden), BF16),
        ],
        scratch_shapes=[
            pltpu.VMEM((SUB, 2 * TILES, modes), F32),
            pltpu.VMEM((2, modes // LANES, 2 * width, LANES), F32),
        ],
        compiler_params=params(),
        name="mix_modes",
    )(
        lines,
        spec_weight,
        jnp.asarray(halves(x_forward_table(planes), 0)),
        jnp.asarray(halves(x_back_table(planes), 1)),
        bypass_weight,
        mlp_in.T,
        mlp_out,
        decode_weight,
    )

    blocks = back.reshape(devices, part, 2 * share)
    blocks = lax.all_to_all(blocks, "gx", 0, 0, tiled=True)
    blocks = blocks.reshape(KY, shares, part, 2, share).transpose(0, 2, 3, 1, 4)
    lines = blocks.reshape(KY * part, 2 * HALF)

    tables = np.concatenate([y_back_table(), z_back_table(planes * NY * NZ)], axis=0)
    tables = jnp.asarray(tables)

    def network(first, count):
        side = jax.ShapeDtypeStruct((3, count, LANES), F32)
        smem = pl.BlockSpec(memory_space=pltpu.SMEM)
        return pl.pallas_call(
            functools.partial(point_kernel, first=first),
            in_specs=[whole()] * 7 + [smem] + [whole()] * 2,
            out_specs=[whole()] * 3,
            out_shape=[side, side, jax.ShapeDtypeStruct((count, LANES), F32)],
            scratch_shapes=[pltpu.VMEM((count * SUB, TILES * LANES), F32)],
            compiler_params=params(),
            cost_estimate=pl.CostEstimate(
                flops=count * LANES * 400000, bytes_accessed=count * LANES * 200, transcendentals=0
            ),
            name="point_network",
        )(
            lines,
            values,
            *wide,
            zone,
            opened,
            perm_table,
            tables,
            jnp.asarray(turn_back_table()),
        )

    far = [(i, i + 1) for i in range(1, devices - 1, 2)]
    far = far + [(b, a) for a, b in far]
    near_by = [(i, i + 1) for i in range(0, devices, 2)]
    near_by = near_by + [(b, a) for a, b in near_by]
    *first, first_filled = network(0, ROWS - QUARTER)
    first_other = [lax.ppermute(first[0], "gx", near_by), lax.ppermute(first[1], "gx", far)]
    *last, last_filled = network(ROWS - QUARTER, QUARTER)
    last_other = [lax.ppermute(last[1], "gx", far), lax.ppermute(last[0], "gx", near_by)]
    fields, partial = pl.pallas_call(
        inner_kernel,
        in_specs=[whole()] * 6 + [pl.BlockSpec(memory_space=pltpu.SMEM)],
        out_specs=[whole()] * 2,
        out_shape=[
            jax.ShapeDtypeStruct((2, ROWS, LANES), F32),
            jax.ShapeDtypeStruct((ROWS, LANES), F32),
        ],
        compiler_params=params(),
        name="faces_in_plane",
    )(first[0], last[0], first_filled, last_filled, zone, opened, perm_table)
    residual = pl.pallas_call(
        outer_kernel,
        in_specs=[whole()] * 9,
        out_specs=whole(),
        out_shape=jax.ShapeDtypeStruct((ROWS, LANES), F32),
        compiler_params=params(),
        name="faces_between_planes",
    )(partial, *first, *first_other, *last, *last_other[::-1])
    return (fields.reshape(2, 1, cells), residual.reshape(1, cells))


def solution(mesh):
    in_specs = (
        P(None, ("groups", "gx"), None),
        P(None, ("groups", "gx")),
        P(None, None, None, "gx"),
        P(),
        P(),
        P(),
        P(),
        P(("groups", "gx"), None),
        P(None, ("groups", "gx"), None),
        P(),
    )
    out_specs = (P(None, ("groups", "gx"), None), P(("groups", "gx"), None))
    return jax.shard_map(body, mesh=mesh, in_specs=in_specs, out_specs=out_specs, check_vma=False)
```
